128 devices in a mesh: wide: 16 (over x_lo, y, core), narrow: 8 (over x_hi, z).
Axes of the slice: x: 4 (x_hi: 2, x_lo: 2; x = x_hi * 2 + x_lo), y: 4, z: 4, core: 2. Of those that a mesh axis runs over, the one named last changes fastest.
Arguments:
- tokens: bfloat16 [2, 4096, 2048], P(None, 'wide'), may hold values from -6 to 6
- cotangent: bfloat16 [2, 4096, 2048], P(None, 'wide'), may hold values from -6 to 6
- lengths: int32 [2], replicated, may hold values from 256 to 4096, as said below
- query_weight: bfloat16 [2048, 2048], P(None, 'narrow'), may hold values from -0.125 to 0.125
- keyval_weight: bfloat16 [2, 2048, 512], P(None, None, 'narrow'), may hold values from -0.125 to 0.125
- output_weight: bfloat16 [2048, 2048], P('narrow'), may hold values from -0.75 to 0.75
- gateup_weight: bfloat16 [2, 2048, 8192], P(None, None, 'narrow'), may hold values from -1 to 1
- down_weight: bfloat16 [8192, 2048], P('narrow'), may hold values from -0.0625 to 0.0625
- norm_gains: bfloat16 [2, 2048], replicated, may hold values from 0.25 to 3
- query_first: float32 [2048, 2048], P('wide', 'narrow'), may hold values from -9.1552734e-05 to 9.1552734e-05
- keyval_first: float32 [2, 2048, 512], P(None, 'wide', 'narrow'), may hold values from -9.1552734e-05 to 9.1552734e-05
- output_first: float32 [2048, 2048], P('narrow', 'wide'), may hold values from -9.1552734e-05 to 9.1552734e-05
- gateup_first: float32 [2, 2048, 8192], P(None, 'wide', 'narrow'), may hold values from -9.1552734e-05 to 9.1552734e-05
- down_first: float32 [8192, 2048], P('narrow', 'wide'), may hold values from -9.1552734e-05 to 9.1552734e-05
- gains_first: float32 [2, 2048], P(None, 'wide'), may hold values from -9.1552734e-05 to 9.1552734e-05
- query_second: float32 [2048, 2048], P('wide', 'narrow'), may hold values from 4.2748038e-10 to 6.905452e-09
- keyval_second: float32 [2, 2048, 512], P(None, 'wide', 'narrow'), may hold values from 4.2748038e-10 to 6.905452e-09
- output_second: float32 [2048, 2048], P('narrow', 'wide'), may hold values from 5.3435048e-11 to 8.631815e-10
- gateup_second: float32 [2, 2048, 8192], P(None, 'wide', 'narrow'), may hold values from 4.2748038e-10 to 6.905452e-09
- down_second: float32 [8192, 2048], P('narrow', 'wide'), may hold values from 4.2748038e-10 to 6.905452e-09
- gains_second: float32 [2, 2048], P(None, 'wide'), may hold values from 4.2748038e-10 to 6.905452e-09
Outputs:
- layer_out: bfloat16 [2, 4096, 2048], P(None, 'wide')
- input_grad: bfloat16 [2, 4096, 2048], P(None, 'wide')
- query_grad: float32 [2048, 2048], P('wide', 'narrow')
- keyval_grad: float32 [2, 2048, 512], P(None, 'wide', 'narrow')
- output_grad: float32 [2048, 2048], P('narrow', 'wide')
- gateup_grad: float32 [2, 2048, 8192], P(None, 'wide', 'narrow')
- down_grad: float32 [8192, 2048], P('narrow', 'wide')
- gains_grad: float32 [2, 2048], P(None, 'wide')
- grad_norm: float32 [], replicated
- query_momentum: float32 [2048, 2048], P('wide', 'narrow')
- keyval_momentum: float32 [2, 2048, 512], P(None, 'wide', 'narrow')
- output_momentum: float32 [2048, 2048], P('narrow', 'wide')
- gateup_momentum: float32 [2, 2048, 8192], P(None, 'wide', 'narrow')
- down_momentum: float32 [8192, 2048], P('narrow', 'wide')
- gains_momentum: float32 [2, 2048], P(None, 'wide')
- query_variance: float32 [2048, 2048], P('wide', 'narrow')
- keyval_variance: float32 [2, 2048, 512], P(None, 'wide', 'narrow')
- output_variance: float32 [2048, 2048], P('narrow', 'wide')
- gateup_variance: float32 [2, 2048, 8192], P(None, 'wide', 'narrow')
- down_variance: float32 [8192, 2048], P('narrow', 'wide')
- gains_variance: float32 [2, 2048], P(None, 'wide')
- query_updated: float32 [2048, 2048], P('wide', 'narrow')
- keyval_updated: float32 [2, 2048, 512], P(None, 'wide', 'narrow')
- output_updated: float32 [2048, 2048], P('narrow', 'wide')
- gateup_updated: float32 [2, 2048, 8192], P(None, 'wide', 'narrow')
- down_updated: float32 [8192, 2048], P('narrow', 'wide')
- gains_updated: float32 [2, 2048], P(None, 'wide')
The draws below stay inside these ranges and needn't reach their ends.
Inputs may be any that keep to these rules, and one draw needn't show every extreme that they name: `lengths`: in every draw one bucket, which one drawn from the seed, holds a sequence of all 4096 positions.
All inputs are finite; a program needn't handle non-finite values.
Results may differ from the reference program's by a relative error of at most 0.04.
Values may be sent and summed in bfloat16 or wider, within the bound.
A program may use at most 192 MiB of HBM per device.

```python
import math
import jax
import jax.numpy as jnp
from jax import lax

D = 2048
HEADS = 32
KV = 8
HD = 64
FF = 8192
BTOK = 256
BUCKETS = 2
STEP = 10
BLEN = 4096
PARAMS = 60821504


def draw_lengths(key, part):
    key = jax.random.fold_in(key, 11)
    key_draw, key_pick = jax.random.split(key)
    drawn_lengths = jax.random.randint(key_draw, (BUCKETS,), BTOK, BLEN + 1)
    chosen = jax.random.randint(key_pick, (), 0, BUCKETS)
    return jnp.where(jnp.arange(BUCKETS) == chosen, BLEN, drawn_lengths).astype(jnp.int32)


def draw_norm_gains(key, part):
    key = jax.random.fold_in(key, 12)
    fraction = jnp.arange(D, dtype=jnp.float32) / D
    rising = 0.6 + 1.2 * fraction
    jitter = jnp.exp(jax.random.uniform(key, (2, D), jnp.float32, -0.35, 0.35))
    return (rising[None, :] * jitter).astype(jnp.bfloat16)


def draw_gateup_weight(key, part):
    key = jax.random.fold_in(key, 13)
    normal_draw = jax.random.normal(key, (2, D, FF), jnp.float32) * D ** (-0.5)
    normal_draw = jnp.clip(normal_draw, -0.5, 0.5)
    column = 0.6 + 1.2 * jnp.arange(FF, dtype=jnp.float32) / FF
    factor = jnp.stack([jnp.ones((FF,), jnp.float32), column])
    return (normal_draw * factor[:, None, :]).astype(jnp.bfloat16)


def block_levels(key, dims, cuts, low, high):
    factor_of, own = 1.0, jax.random.fold_in(key, 6)
    for dim, shards_of in cuts:
        draws = jnp.exp(jax.random.uniform(jax.random.fold_in(own, dim), (shards_of,), jnp.float32, low / len(cuts), high / len(cuts)))
        factor_of = factor_of * jnp.repeat(draws, dims[dim] // shards_of).reshape([-1 if axis == dim else 1 for axis in range(len(dims))])
    return factor_of


def centred(stream_key, shape, scale, most, pieces=(), held_as=jnp.bfloat16):
    drawn = jax.random.normal(stream_key, shape, jnp.float32) * scale
    if len(pieces) > 0:
        drawn = block_levels(stream_key, shape, pieces, -0.22, 0.18) * drawn
    return jnp.clip(drawn, min=-most, max=most).astype(held_as)


def setup_inputs(seed: int = 0) -> dict:
    arg_keys = jax.random.split(jax.random.key(seed), 22)
    return {
        "tokens": centred(arg_keys[0], (BUCKETS, BLEN, D), 1.0, 6.0, ((1, 16),)),
        "cotangent": centred(arg_keys[1], (BUCKETS, BLEN, D), 1.0, 6.0, ((1, 16),)),
        "lengths": draw_lengths(jax.random.fold_in(arg_keys[21], 71), 0),
        "query_weight": centred(arg_keys[3], (D, HEADS * HD), D ** -0.5, 0.125, ((1, 8),)),
        "keyval_weight": centred(arg_keys[4], (2, D, KV * HD), D ** -0.5, 0.125, ((2, 8),)),
        "output_weight": centred(arg_keys[5], (HEADS * HD, D), (HEADS * HD // 32) ** -0.5, 0.75, ((0, 8),)),
        "gateup_weight": draw_gateup_weight(jax.random.fold_in(arg_keys[21], 71), 0),
        "down_weight": centred(arg_keys[7], (FF, D), FF ** -0.5, 0.0625, ((0, 8),)),
        "norm_gains": draw_norm_gains(jax.random.fold_in(arg_keys[21], 71), 0),
        "query_first": centred(arg_keys[9], (D, HEADS * HD), (0.11 * PARAMS ** -0.5), 9.1552734375e-05, ((0, 16), (1, 8)), jnp.float32),
        "keyval_first": centred(arg_keys[10], (2, D, KV * HD), (0.11 * PARAMS ** -0.5), 9.1552734375e-05, ((1, 16), (2, 8)), jnp.float32),
        "output_first": centred(arg_keys[11], (HEADS * HD, D), (0.11 * PARAMS ** -0.5), 9.1552734375e-05, ((0, 8), (1, 16)), jnp.float32),
        "gateup_first": centred(arg_keys[12], (2, D, FF), (0.11 * PARAMS ** -0.5), 9.1552734375e-05, ((1, 16), (2, 8)), jnp.float32),
        "down_first": centred(arg_keys[13], (FF, D), (0.11 * PARAMS ** -0.5), 9.1552734375e-05, ((0, 8), (1, 16)), jnp.float32),
        "gains_first": centred(arg_keys[14], (2, D), (0.11 * PARAMS ** -0.5), 9.1552734375e-05, ((1, 16),), jnp.float32),
        "query_second": jnp.clip(jnp.exp(math.log(6.905452210048679e-09) - 2.7821582 * jax.random.uniform(arg_keys[15], (D, HEADS * HD), jnp.float32) ** block_levels(arg_keys[15], (D, HEADS * HD), ((0, 16), (1, 8)), -0.2, 0.2)), 4.2748038442397274e-10, 6.905452210048679e-09),
        "keyval_second": jnp.clip(jnp.exp(math.log(6.905452210048679e-09) - 2.7821582 * jax.random.uniform(arg_keys[16], (2, D, KV * HD), jnp.float32) ** block_levels(arg_keys[16], (2, D, KV * HD), ((1, 16), (2, 8)), -0.2, 0.2)), 4.2748038442397274e-10, 6.905452210048679e-09),
        "output_second": jnp.clip(jnp.exp(math.log(8.631815262560849e-10) - 2.7821582 * jax.random.uniform(arg_keys[17], (HEADS * HD, D), jnp.float32) ** block_levels(arg_keys[17], (HEADS * HD, D), ((0, 8), (1, 16)), -0.2, 0.2)), 5.343504805299659e-11, 8.631815262560849e-10),
        "gateup_second": jnp.clip(jnp.exp(math.log(6.905452210048679e-09) - 2.7821582 * jax.random.uniform(arg_keys[18], (2, D, FF), jnp.float32) ** block_levels(arg_keys[18], (2, D, FF), ((1, 16), (2, 8)), -0.2, 0.2)), 4.2748038442397274e-10, 6.905452210048679e-09),
        "down_second": jnp.clip(jnp.exp(math.log(6.905452210048679e-09) - 2.7821582 * jax.random.uniform(arg_keys[19], (FF, D), jnp.float32) ** block_levels(arg_keys[19], (FF, D), ((0, 8), (1, 16)), -0.2, 0.2)), 4.2748038442397274e-10, 6.905452210048679e-09),
        "gains_second": jnp.clip(jnp.exp(math.log(6.905452210048679e-09) - 2.7821582 * jax.random.uniform(arg_keys[20], (2, D), jnp.float32) ** block_levels(arg_keys[20], (2, D), ((1, 16),), -0.2, 0.2)), 4.2748038442397274e-10, 6.905452210048679e-09),
    }


highest = lax.Precision.HIGHEST
norm_eps = 1e-05
rope_theta = 500000.0
rope_factor = 32.0
rope_low = 1.0
rope_high = 4.0
rope_context = 8192.0
clip_limit = 1.0
beta_first = 0.9
beta_second = 0.95
adam_eps = 1e-08
learn_rate = 0.09
gain_rate = 1.2
decay_rate = 0.1
masked_score = -1e+30

@jax.custom_vjp
def low(v):
    return lax.optimization_barrier(v.astype(jnp.bfloat16)).astype(jnp.float32)

@jax.custom_vjp
def low_back(v):
    return v

def low_keep(v):
    return (low(v), None)

def low_pass(kept, grad):
    return (grad,)

def back_keep(v):
    return (v, None)

def back_low(kept, grad):
    return (low(grad),)
low.defvjp(low_keep, low_pass)
low_back.defvjp(back_keep, back_low)

def rope_tables(positions, head_width):
    half_width = head_width // 2
    exponent = jnp.arange(half_width, dtype=jnp.float32) * (2.0 / head_width)
    base_freq = jnp.power(jnp.float32(rope_theta), -exponent)
    wavelen = 2.0 * math.pi / base_freq
    smooth = (rope_context / wavelen - rope_low) / (rope_high - rope_low)
    blended = (1.0 - smooth) * base_freq / rope_factor + smooth * base_freq
    scaled = jnp.where(wavelen < rope_context / rope_high, base_freq, jnp.where(wavelen > rope_context / rope_low, base_freq / rope_factor, blended))
    angles = positions.astype(jnp.float32)[:, None] * scaled[None, :]
    return (jnp.cos(angles), jnp.sin(angles))

def rotate(values, cosine, sine_table):
    half_width = values.shape[-1] // 2
    front_half = values[..., :half_width]
    back_half = values[..., half_width:]
    cosine = cosine[:, None, :]
    sine_table = sine_table[:, None, :]
    return jnp.concatenate([front_half * cosine - back_half * sine_table, back_half * cosine + front_half * sine_table], axis=-1)

def rms_scale(values):
    return values * lax.rsqrt(lax.optimization_barrier(jnp.mean(values * values, axis=-1, keepdims=True)) + norm_eps)

def head_attention(inputs):
    query_rows, key_rows, value_rows, length = inputs
    bucket_len = key_rows.shape[0]
    score_scale = query_rows.shape[-1] ** (-0.5)
    scores = low_back(jnp.einsum('lgh,mh->glm', query_rows, key_rows, precision=highest) * score_scale)
    slot_ids = jnp.arange(bucket_len)
    allowed = (slot_ids[None, :] <= slot_ids[:, None]) & (slot_ids[None, :] < length)
    scores = jnp.where(allowed[None], scores, masked_score)
    row_top = lax.optimization_barrier(jnp.max(scores, axis=-1, keepdims=True))
    weights = jnp.exp(scores - row_top)
    probabilities = weights / lax.optimization_barrier(jnp.sum(weights, axis=-1, keepdims=True))
    return jnp.einsum('glm,mh->lgh', low(probabilities), value_rows, precision=highest)

def forward_pass(inputs, params, lengths, cosine, sine_table):
    query_weight, keyval_weight, output_weight, gateup_weight, down_weight, norm_gains = params
    bucket_count, bucket_len, model_width = inputs.shape
    head_count = query_weight.shape[1] // HD
    group_count = keyval_weight.shape[2] // HD
    per_group = head_count // group_count
    normed_one = low(rms_scale(inputs) * norm_gains[0])
    query_pre = low_back(jnp.einsum('bld,de->ble', normed_one, query_weight, precision=highest))
    keyval_pre = low_back(jnp.einsum('bld,cde->cble', normed_one, keyval_weight, precision=highest))
    queries = low(rotate(query_pre.reshape(bucket_count, bucket_len, head_count, HD), cosine, sine_table))
    keys_rot = low(rotate(keyval_pre[0].reshape(bucket_count, bucket_len, group_count, HD), cosine, sine_table))
    values_low = low(keyval_pre[1].reshape(bucket_count, bucket_len, group_count, HD))
    query_sets = queries.reshape(bucket_count, bucket_len, group_count, per_group, HD).transpose(0, 2, 1, 3, 4)
    query_sets = query_sets.reshape(bucket_count * group_count, bucket_len, per_group, HD)
    key_sets = keys_rot.transpose(0, 2, 1, 3).reshape(bucket_count * group_count, bucket_len, HD)
    value_sets = values_low.transpose(0, 2, 1, 3).reshape(bucket_count * group_count, bucket_len, HD)
    length_sets = jnp.repeat(lengths, group_count)
    attended = lax.map(jax.checkpoint(head_attention), (query_sets, key_sets, value_sets, length_sets))
    attended = attended.reshape(bucket_count, group_count, bucket_len, per_group, HD).transpose(0, 2, 1, 3, 4)
    attended = attended.reshape(bucket_count, bucket_len, head_count * HD)
    attended_low = low(low_back(attended))
    hidden = inputs + low_back(jnp.einsum('ble,ed->bld', attended_low, output_weight, precision=highest))
    normed_two = low(rms_scale(hidden) * norm_gains[1])
    gate_up = low_back(jnp.einsum('bld,cdf->cblf', normed_two, gateup_weight, precision=highest))
    mixed = low(gate_up[0] * jax.nn.sigmoid(gate_up[0]) * gate_up[1])
    return hidden + low_back(jnp.einsum('blf,fd->bld', mixed, down_weight, precision=highest))

def adam_update(weight, gradient, old_first, old_second, step_rate, decay_factor):
    momentum = beta_first * old_first + (1.0 - beta_first) * gradient
    variance = beta_second * old_second + (1.0 - beta_second) * gradient * gradient
    corrected = momentum / (1.0 - beta_first ** STEP)
    second_hat = variance / (1.0 - beta_second ** STEP)
    updated = weight * (1.0 - step_rate * decay_factor) - step_rate * corrected / (jnp.sqrt(second_hat) + adam_eps)
    return (updated, momentum, variance)

def reference(tokens, cotangent, lengths, query_weight, keyval_weight, output_weight, gateup_weight, down_weight, norm_gains, query_first, keyval_first, output_first, gateup_first, down_first, gains_first, query_second, keyval_second, output_second, gateup_second, down_second, gains_second):
    olds = tuple((weight.astype(jnp.float32) for weight in (query_weight, keyval_weight, output_weight, gateup_weight, down_weight, norm_gains)))
    inputs = tokens.astype(jnp.float32)
    bucket_len = inputs.shape[1]
    slot_ids = jnp.arange(bucket_len)
    cosine, sine_table = rope_tables(slot_ids, HD)
    live_mask = (slot_ids[None, :] < lengths[:, None]).astype(jnp.float32)

    def forward(inputs, *params):
        return forward_pass(inputs, params, lengths, cosine, sine_table)
    output, pullback = jax.vjp(forward, inputs, *olds)
    grads = pullback(cotangent.astype(jnp.float32) * live_mask[:, :, None])
    weight_grads = grads[1:]
    squares = jnp.zeros((), jnp.float32)
    for gradient in weight_grads:
        squares = squares + jnp.sum(gradient * gradient)
    grad_norm = jnp.sqrt(squares)
    factor = jnp.minimum(1.0, clip_limit / (grad_norm + 1e-06))
    clipped = tuple((gradient * factor for gradient in weight_grads))
    firsts = (query_first, keyval_first, output_first, gateup_first, down_first, gains_first)
    seconds = (query_second, keyval_second, output_second, gateup_second, down_second, gains_second)
    results = []
    for number in range(6):
        step_rate = gain_rate if number == 5 else learn_rate
        decay_factor = 0.0 if number == 5 else decay_rate
        results.append(adam_update(olds[number], clipped[number], firsts[number], seconds[number], step_rate, decay_factor))
    return (output.astype(jnp.bfloat16), grads[0].astype(jnp.bfloat16), clipped[0], clipped[1], clipped[2], clipped[3], clipped[4], clipped[5], grad_norm, results[0][1], results[1][1], results[2][1], results[3][1], results[4][1], results[5][1], results[0][2], results[1][2], results[2][2], results[3][2], results[4][2], results[5][2], results[0][0], results[1][0], results[2][0], results[3][0], results[4][0], results[5][0])
```

```python
import functools
import math

import jax
import jax.numpy as jnp
from jax import lax
from jax.experimental import pallas as pl
from jax.experimental.pallas import tpu as pltpu
from jax.sharding import PartitionSpec as P

HD = 64
STEP = 10


norm_eps = 1e-05
rope_theta = 500000.0
rope_factor = 32.0
rope_low = 1.0
rope_high = 4.0
rope_context = 8192.0
clip_limit = 1.0
beta_first = 0.9
beta_second = 0.95
adam_eps = 1e-08
learn_rate = 0.09
gain_rate = 1.2
decay_rate = 0.1
masked_score = -1e30


bf16 = jnp.bfloat16
f32 = jnp.float32
MESH = pl.DeviceIdType.MESH
MB = 1024 * 1024


def dot_nn(a, b):
    return jnp.dot(a, b, preferred_element_type=f32)


def dot_nt(a, b):
    return lax.dot_general(a, b, (((1,), (1,)), ((), ())), preferred_element_type=f32)


def dot_tn(a, b):
    return lax.dot_general(a, b, (((0,), (0,)), ((), ())), preferred_element_type=f32)


def greet(targets):
    barrier = pltpu.get_barrier_semaphore()
    for target in targets:
        pl.semaphore_signal(barrier, inc=1, device_id=target, device_id_type=MESH)
    pl.semaphore_wait(barrier, len(targets))


def tile(j, size):
    return pl.ds(pl.multiple_of(j * size, size), size)


def middle_kernel(
    peers,
    chunks,
    ob_ref,
    wo_hbm,
    tok_ref,
    dy_ref,
    dyb_hbm,
    gains_ref,
    wgu_hbm,
    wd_hbm,
    hidden_ref,
    ffsum_ref,
    dob_ref,
    dh_ref,
    gain_ref,
    gout_hbm,
    ggu_hbm,
    gdown_hbm,
    wo,
    wgu,
    wd,
    dyb,
    da,
    n2,
    dgu,
    mixed,
    dhb,
    send,
    recv,
    send2,
    recv2,
    send3,
    recv3,
    gout,
    ggu,
    gdown,
    in_sem,
    out_sem,
    s_sem,
    r_sem,
    s_sem2,
    r_sem2,
    s_sem3,
    r_sem3,
):
    me = lax.axis_index("narrow")
    wide_me = lax.axis_index("wide")
    rows = tok_ref.shape[0]
    width = tok_ref.shape[1]
    units = wd.shape[0]
    span = 256
    peer = [(wide_me, lax.rem(me + step, peers)) for step in range(1, peers)]
    loads = [
        pltpu.make_async_copy(wo_hbm, wo, in_sem.at[0]),
        pltpu.make_async_copy(wd_hbm, wd, in_sem.at[1]),
        pltpu.make_async_copy(dyb_hbm, dyb, in_sem.at[2]),
        pltpu.make_async_copy(wgu_hbm, wgu, in_sem.at[3]),
    ]
    for load in loads:
        load.start()
    greet(peer)

    def send_block(slot, src, dst, ssem, rsem):
        copy = pltpu.make_async_remote_copy(
            src_ref=src, dst_ref=dst, send_sem=ssem, recv_sem=rsem,
            device_id=peer[slot], device_id_type=MESH,
        )
        copy.start()
        return copy

    loads[0].wait()
    flight = []
    for slot in range(peers - 1):
        theirs = pl.ds(pl.multiple_of(peer[slot][1] * rows, rows), rows)
        send[slot] = dot_nn(ob_ref[theirs, :], wo[...]).astype(bf16)
        flight.append(send_block(slot, send.at[slot], recv.at[slot], s_sem.at[0, slot], r_sem.at[0, slot]))
    mine = pl.ds(pl.multiple_of(me * rows, rows), rows)
    hidden = tok_ref[...].astype(f32) + dot_nn(ob_ref[mine, :], wo[...])
    loads[1].wait()
    loads[2].wait()

    def grad_middle(j, carry):
        da[:, tile(j, span)] = dot_nt(dyb[...], wd[tile(j, span), :])
        return carry

    lax.fori_loop(0, units // span, grad_middle, 0)
    for copy in flight:
        copy.wait_recv()
    for slot in range(peers - 1):
        hidden = hidden + recv[slot].astype(f32)
    hidden_ref[...] = hidden
    inverse = lax.rsqrt(jnp.mean(hidden * hidden, axis=-1, keepdims=True) + norm_eps)
    gain2 = gains_ref[1:2, :].astype(f32)
    n2[mine, :] = (hidden * inverse * gain2).astype(bf16)
    for copy in flight:
        copy.wait_send()
    flight = [
        send_block(slot, n2.at[mine, :], n2.at[mine, :], s_sem.at[1, slot], r_sem.at[1, slot])
        for slot in range(peers - 1)
    ]
    loads[3].wait()
    for copy in flight:
        copy.wait()

    def gate_up(j, carry):
        gate = dot_nn(n2[...], wgu[0, :, tile(j, span)])
        up = dot_nn(n2[...], wgu[1, :, tile(j, span)])
        sigmoid = jax.nn.sigmoid(gate)
        activated = gate * sigmoid
        mixed[:, tile(j, span)] = (activated * up).astype(bf16)
        grad = da[:, tile(j, span)]
        dgu[0, :, tile(j, span)] = (
            grad * up * sigmoid * (1.0 + gate * (1.0 - sigmoid))
        ).astype(bf16)
        dgu[1, :, tile(j, span)] = (grad * activated).astype(bf16)
        return carry

    lax.fori_loop(0, units // span, gate_up, 0)

    chunk = width // chunks

    def scatter(out, into, ssem, rsem, product):
        def per_chunk(c, carry):
            columns = tile(c, chunk)
            out[:, columns] = product(c).astype(bf16)
            for slot in range(peers - 1):
                theirs = pl.ds(pl.multiple_of(peer[slot][1] * rows, rows), rows)
                send_block(
                    slot, out.at[theirs, columns], into.at[slot, :, columns],
                    ssem.at[slot, c], rsem.at[slot, c],
                )
            return carry

        lax.fori_loop(0, chunks, per_chunk, 0)

    def scatter_wait(out, into, ssem, rsem):
        def per_chunk(c, carry):
            columns = tile(c, chunk)
            for slot in range(peers - 1):
                theirs = pl.ds(pl.multiple_of(peer[slot][1] * rows, rows), rows)
                pltpu.make_async_remote_copy(
                    src_ref=out.at[theirs, columns], dst_ref=into.at[slot, :, columns],
                    send_sem=ssem.at[slot, c], recv_sem=rsem.at[slot, c],
                    device_id=peer[slot], device_id_type=MESH,
                ).wait()
            return carry

        lax.fori_loop(0, chunks, per_chunk, 0)

    scatter(
        send2, recv2, s_sem2, r_sem2,
        lambda c: dot_nt(dgu[0], wgu[0, tile(c, chunk), :]) + dot_nt(dgu[1], wgu[1, tile(c, chunk), :]),
    )
    scatter(send3, recv3, s_sem3, r_sem3, lambda c: dot_nn(mixed[...], wd[:, tile(c, chunk)]))

    def grad_gateup(j, carry):
        which = lax.div(j, width // span)
        part = lax.rem(j, width // span)
        ggu[which, tile(part, span), :] = dot_tn(n2[:, tile(part, span)], dgu[which]).astype(bf16)
        return carry

    lax.fori_loop(0, 2 * (width // span), grad_gateup, 0)
    store_gu = pltpu.make_async_copy(ggu, ggu_hbm, out_sem.at[0])
    store_gu.start()

    scatter_wait(send2, recv2, s_sem2, r_sem2)
    total = send2[mine, :].astype(f32)
    for slot in range(peers - 1):
        total = total + recv2[slot].astype(f32)
    z2 = hidden_ref[...] * inverse
    gain_ref[...] = jnp.broadcast_to(jnp.sum(total * z2, axis=0, keepdims=True), gain_ref.shape)
    weighted = total * gain2
    dh = dy_ref[...].astype(f32) + inverse * (
        weighted - z2 * jnp.mean(weighted * z2, axis=-1, keepdims=True)
    )
    dh_ref[...] = dh
    dhb[mine, :] = dh.astype(bf16)
    flight = [
        send_block(slot, dhb.at[mine, :], dhb.at[mine, :], s_sem.at[2, slot], r_sem.at[2, slot])
        for slot in range(peers - 1)
    ]

    def grad_down(j, carry):
        gdown[tile(j, span), :] = dot_tn(mixed[:, tile(j, span)], dyb[...]).astype(bf16)
        return carry

    lax.fori_loop(0, units // span, grad_down, 0)
    store_down = pltpu.make_async_copy(gdown, gdown_hbm, out_sem.at[1])
    store_down.start()
    for copy in flight:
        copy.wait()
    dob_ref[...] = dot_nt(dhb[...], wo[...]).astype(bf16)

    def grad_out(j, carry):
        gout[:, tile(j, span)] = dot_tn(ob_ref[...], dhb[:, tile(j, span)]).astype(bf16)
        return carry

    lax.fori_loop(0, width // span, grad_out, 0)
    store_out = pltpu.make_async_copy(gout, gout_hbm, out_sem.at[2])
    store_out.start()
    scatter_wait(send3, recv3, s_sem3, r_sem3)
    total = send3[mine, :].astype(f32)
    for slot in range(peers - 1):
        total = total + recv3[slot].astype(f32)
    ffsum_ref[...] = (hidden_ref[...] + total).astype(bf16)
    store_gu.wait()
    store_down.wait()
    store_out.wait()


def middle(peers, ob, wo, tok_rows, dy_rows, dyb, gains, wgu, wd):
    tokens, width = dyb.shape
    rows = tok_rows.shape[0]
    units = wd.shape[0]
    heads = wo.shape[0]
    chunks = 4
    anywhere = pl.BlockSpec(memory_space=pl.ANY)
    here = pl.BlockSpec(memory_space=pltpu.VMEM)
    shape = jax.ShapeDtypeStruct
    dma = pltpu.SemaphoreType.DMA
    return pl.pallas_call(
        functools.partial(middle_kernel, peers, chunks),
        out_shape=(
            shape((rows, width), f32),
            shape((rows, width), bf16),
            shape((tokens, heads), bf16),
            shape((rows, width), f32),
            shape((8, width), f32),
            shape((heads, width), bf16),
            shape((2, width, units), bf16),
            shape((units, width), bf16),
        ),
        in_specs=[here, anywhere, here, here, anywhere, here, anywhere, anywhere],
        out_specs=(here, here, here, here, here, anywhere, anywhere, anywhere),
        scratch_shapes=[
            pltpu.VMEM(wo.shape, bf16),
            pltpu.VMEM(wgu.shape, bf16),
            pltpu.VMEM(wd.shape, bf16),
            pltpu.VMEM((tokens, width), bf16),
            pltpu.VMEM((tokens, units), f32),
            pltpu.VMEM((tokens, width), bf16),
            pltpu.VMEM((2, tokens, units), bf16),
            pltpu.VMEM((tokens, units), bf16),
            pltpu.VMEM((tokens, width), bf16),
            pltpu.VMEM((peers - 1, rows, width), bf16),
            pltpu.VMEM((peers - 1, rows, width), bf16),
            pltpu.VMEM((tokens, width), bf16),
            pltpu.VMEM((peers - 1, rows, width), bf16),
            pltpu.VMEM((tokens, width), bf16),
            pltpu.VMEM((peers - 1, rows, width), bf16),
            pltpu.VMEM((heads, width), bf16),
            pltpu.VMEM((2, width, units), bf16),
            pltpu.VMEM((units, width), bf16),
            dma((4,)),
            dma((3,)),
            dma((3, peers - 1)),
            dma((3, peers - 1)),
            dma((peers - 1, chunks)),
            dma((peers - 1, chunks)),
            dma((peers - 1, chunks)),
            dma((peers - 1, chunks)),
        ],
        compiler_params=pltpu.CompilerParams(
            collective_id=1, has_side_effects=True, vmem_limit_bytes=63 * MB
        ),
        name="middle",
    )(ob, wo, tok_rows, dy_rows, dyb, gains, wgu, wd)


def swap_halves(u):
    half = HD // 2
    width = u.shape[-1]
    lane = lax.broadcasted_iota(jnp.int32, u.shape, u.ndim - 1)
    ahead = pltpu.roll(u, width - half, u.ndim - 1)
    behind = pltpu.roll(u, half, u.ndim - 1)
    return jnp.where(lax.rem(lane, HD) < half, ahead, behind)


def front_kernel(
    others, tok_ref, gains_ref, wq_ref, wkv_ref, cos_ref, sin_ref,
    n1_ref, q_ref, kv_ref, s_sem, r_sem, f_s_sem, f_r_sem,
):
    narrow_me = lax.axis_index("narrow")
    me = lax.axis_index("wide")
    chips = others + 1
    chip, core = lax.div(me, 2), lax.rem(me, 2)
    chip_of = [lax.rem(chip + step, chips) for step in range(1, chips)]
    peer = [(2 * there + core, narrow_me) for there in chip_of]
    mate = (2 * chip + 1 - core, narrow_me)
    greet(peer + [mate])
    tokens, width = tok_ref.shape
    span = 64

    def normed(j, carry):
        rows = tile(j, span)
        values = tok_ref[rows, :].astype(f32)
        inverse = lax.rsqrt(jnp.mean(values * values, axis=-1, keepdims=True) + norm_eps)
        n1_ref[rows, :] = (values * inverse * gains_ref[0:1, :].astype(f32)).astype(bf16)
        return carry

    lax.fori_loop(0, tokens // span, normed, 0)
    lane = lax.broadcasted_iota(jnp.int32, (tokens, 2 * HD), 1)
    cosine, sine = cos_ref[...], sin_ref[...]
    kv = dot_nn(n1_ref[...], wkv_ref[...])
    turned = kv * cosine + swap_halves(kv) * sine
    kv_ref[me] = jnp.where(lane < HD, turned, kv).astype(bf16)

    def send(src, there, ssem, rsem):
        copy = pltpu.make_async_remote_copy(
            src_ref=src, dst_ref=src, send_sem=ssem, recv_sem=rsem,
            device_id=there, device_id_type=MESH,
        )
        copy.start()
        return copy

    flight = [
        send(kv_ref.at[me], peer[step], s_sem.at[step], r_sem.at[step]) for step in range(others)
    ]
    to_mate = [send(kv_ref.at[me], mate, f_s_sem.at[others], f_r_sem.at[others])]
    for pair in range(wq_ref.shape[1] // (2 * HD)):
        columns = pl.ds(pair * 2 * HD, 2 * HD)
        query = dot_nn(n1_ref[...], wq_ref[:, columns])
        q_ref[:, columns] = ((query * cosine + swap_halves(query) * sine) * HD**-0.5).astype(bf16)
    for step in range(others):
        arrived = lax.rem(chip + chips - 1 - step, chips)
        flight[step].wait_recv()
        block = kv_ref.at[2 * arrived + core]
        to_mate.append(send(block, mate, f_s_sem.at[step], f_r_sem.at[step]))
    for copy in flight:
        copy.wait_send()
    for copy in to_mate:
        copy.wait()


def front(wide_count, tokens, gains, wq, wkv, cosine, sine):
    count, width = tokens.shape
    others = wide_count // 2 - 1
    here = pl.BlockSpec(memory_space=pltpu.VMEM)
    shape = jax.ShapeDtypeStruct
    dma = pltpu.SemaphoreType.DMA
    return pl.pallas_call(
        functools.partial(front_kernel, others),
        out_shape=(
            shape((count, width), bf16),
            shape((count, wq.shape[1]), bf16),
            shape((wide_count, count, 2 * HD), bf16),
        ),
        in_specs=[here] * 6,
        out_specs=(here, here, here),
        scratch_shapes=[dma((others,)), dma((others,)), dma((others + 1,)), dma((others + 1,))],
        compiler_params=pltpu.CompilerParams(
            collective_id=2, has_side_effects=True, vmem_limit_bytes=48 * MB
        ),
        name="front",
    )(tokens, gains, wq, wkv, cosine, sine)


def wide_rows(block):
    return block.reshape(block.shape[0] * block.shape[1], block.shape[2])


def head_lanes(ref, rows, head, high):
    pair = ref[rows, pl.ds((head // 2) * 2 * HD, 2 * HD)].astype(f32)
    lane = lax.broadcasted_iota(jnp.int32, pair.shape, 1)
    if (head % 2 == 1) != high:
        pair = pltpu.roll(pair, HD, 1)
    return jnp.where((lane >= HD) == high, pair, 0.0)


def attend_kernel(blocks, len_ref, q_ref, kv_ref, ob_ref, o_ref, log_ref, head_q):
    me = lax.axis_index("wide")
    rows_each = kv_ref.shape[1] // 2
    heads = q_ref.shape[1] // HD
    key_span = blocks * rows_each
    first = me * rows_each
    for bucket in range(2):
        rows = pl.ds(bucket * rows_each, rows_each)
        for head in range(heads):
            head_q[head] = head_lanes(q_ref, rows, head, False).astype(bf16)
        length = len_ref[bucket]
        whole = lax.div(jnp.minimum(first, length), key_span)
        last = lax.div(jnp.minimum(first + rows_each, length) + key_span - 1, key_span)

        def step(masked, index, carry):
            block = wide_rows(kv_ref[pl.ds(index * blocks, blocks), rows, :])
            lane = lax.broadcasted_iota(jnp.int32, block.shape, 1)
            ones_v = jnp.where(lane < HD, jnp.ones_like(block), block)
            if masked:
                key = index * key_span + lax.broadcasted_iota(jnp.int32, (rows_each, key_span), 1)
                place = first + lax.broadcasted_iota(jnp.int32, (rows_each, key_span), 0)
                allowed = (key <= place) & (key < length)
            result = []
            for head in range(heads):
                best, total = carry[head]
                scores = dot_nt(head_q[head], block)
                if masked:
                    scores = jnp.where(allowed, scores, masked_score)
                new_best = jnp.maximum(best, jnp.max(scores, axis=-1, keepdims=True))
                weights = jnp.exp(scores - new_best).astype(bf16)
                total = total * jnp.exp(best - new_best) + dot_nn(weights, ones_v)
                result.append((new_best, total))
            return tuple(result)

        carry = tuple(
            (jnp.full((rows_each, 1), masked_score, f32), jnp.zeros((rows_each, 2 * HD), f32))
            for _ in range(heads)
        )
        carry = lax.fori_loop(0, whole, functools.partial(step, False), carry)
        carry = lax.fori_loop(whole, last, functools.partial(step, True), carry)
        lane = lax.broadcasted_iota(jnp.int32, (rows_each, 2 * HD), 1)
        outs = []
        for head in range(heads):
            best, total = carry[head]
            sums = jnp.where(lane < HD, total, pltpu.roll(total, HD, 1))
            log_row = jnp.transpose(best + jnp.log(sums))
            log_ref[pl.ds(bucket * heads + head, 1), :] = log_row[0:1, :]
            outs.append(total / sums)
        for pair in range(heads // 2):
            value = jnp.where(lane < HD, pltpu.roll(outs[2 * pair], HD, 1), outs[2 * pair + 1])
            columns = pl.ds(pair * 2 * HD, 2 * HD)
            o_ref[rows, columns] = value
            ob_ref[rows, columns] = value.astype(bf16)


def attend(lengths, queries, pairs):
    shape = jax.ShapeDtypeStruct
    here = pl.BlockSpec(memory_space=pltpu.VMEM)
    rows_each = queries.shape[0] // 2
    heads = queries.shape[1] // HD
    return pl.pallas_call(
        functools.partial(attend_kernel, 2),
        out_shape=(
            shape(queries.shape, bf16), shape(queries.shape, f32), shape((2 * heads, rows_each), f32),
        ),
        in_specs=[pl.BlockSpec(memory_space=pltpu.SMEM), here, here],
        out_specs=(here, here, here),
        scratch_shapes=[pltpu.VMEM((heads, rows_each, 2 * HD), bf16)],
        compiler_params=pltpu.CompilerParams(vmem_limit_bytes=48 * MB),
        name="attend",
    )(lengths, queries, pairs)


def attend_back_kernel(
    blocks, len_ref, q_ref, kv_ref, o_ref, log_ref, dob_ref, cos_ref, sin_ref,
    dq_ref, dkv_ref, head_q, head_do, delta, grad,
):
    me = lax.axis_index("wide")
    rows_each = kv_ref.shape[1] // 2
    heads = q_ref.shape[1] // HD
    key_span = blocks * rows_each
    first = me * rows_each

    def clear(index, carry):
        dkv_ref[index] = jnp.zeros(dkv_ref.shape[1:], bf16)
        return carry

    lax.fori_loop(0, dkv_ref.shape[0], clear, 0)
    for bucket in range(2):
        rows = pl.ds(bucket * rows_each, rows_each)
        for head in range(heads):
            head_q[head] = head_lanes(q_ref, rows, head, False).astype(bf16)
            upper = head_lanes(dob_ref, rows, head, True)
            head_do[head] = upper.astype(bf16)
            product = upper * head_lanes(o_ref, rows, head, True)
            delta[pl.ds(head, 1), :] = jnp.sum(jnp.transpose(product), axis=0, keepdims=True)
            grad[head] = jnp.zeros((rows_each, 2 * HD), f32)
        length = len_ref[bucket]
        whole = lax.div(jnp.minimum(first, length), key_span)
        last = lax.div(jnp.minimum(first + rows_each, length) + key_span - 1, key_span)
        last = jnp.where(first < length, last, 0)
        whole = jnp.minimum(whole, last)

        def step(masked, index, carry):
            block = wide_rows(kv_ref[pl.ds(index * blocks, blocks), rows, :])
            if masked:
                key = index * key_span + lax.broadcasted_iota(jnp.int32, (key_span, rows_each), 0)
                place = first + lax.broadcasted_iota(jnp.int32, (key_span, rows_each), 1)
                allowed = (key <= place) & (key < length)
            total = jnp.zeros((key_span, 2 * HD), f32)
            for head in range(heads):
                scores = dot_nt(block, head_q[head])
                if masked:
                    scores = jnp.where(allowed, scores, masked_score)
                chances = jnp.exp(scores - log_ref[pl.ds(bucket * heads + head, 1), :])
                slope = dot_nt(block, head_do[head]) - delta[pl.ds(head, 1), :]
                slope = (chances * slope).astype(bf16)
                total = total + dot_nn(slope, head_q[head]) + dot_nn(chances.astype(bf16), head_do[head])
                grad[head] = grad[head] + dot_tn(slope, block)
            dkv_ref[pl.ds(index * blocks, blocks), rows, :] = total.astype(bf16).reshape(
                blocks, rows_each, 2 * HD
            )
            return carry

        lax.fori_loop(0, whole, functools.partial(step, False), 0)
        lax.fori_loop(whole, last, functools.partial(step, True), 0)
        lane = lax.broadcasted_iota(jnp.int32, (rows_each, 2 * HD), 1)
        for pair in range(heads // 2):
            value = jnp.where(lane < HD, grad[2 * pair], pltpu.roll(grad[2 * pair + 1], HD, 1))
            value = value * HD**-0.5
            turned = value * cos_ref[rows, :] - swap_halves(value) * sin_ref[rows, :]
            dq_ref[rows, pl.ds(pair * 2 * HD, 2 * HD)] = turned.astype(bf16)


def attend_back(lengths, queries, pairs, out, logs, grad_out, cosine, sine):
    shape = jax.ShapeDtypeStruct
    here = pl.BlockSpec(memory_space=pltpu.VMEM)
    rows_each = queries.shape[0] // 2
    heads = queries.shape[1] // HD
    return pl.pallas_call(
        functools.partial(attend_back_kernel, 2),
        out_shape=(shape(queries.shape, bf16), shape(pairs.shape, bf16)),
        in_specs=[pl.BlockSpec(memory_space=pltpu.SMEM)] + [here] * 7,
        out_specs=(here, here),
        scratch_shapes=[
            pltpu.VMEM((heads, rows_each, 2 * HD), bf16),
            pltpu.VMEM((heads, rows_each, 2 * HD), bf16),
            pltpu.VMEM((heads, rows_each), f32),
            pltpu.VMEM((heads, rows_each, 2 * HD), f32),
        ],
        compiler_params=pltpu.CompilerParams(vmem_limit_bytes=48 * MB),
        name="attend_back",
    )(lengths, queries, pairs, out, logs, grad_out, cosine, sine)


class Item:
    def __init__(self, source, loaded, mate_in, own, chip_in, sems):
        self.source, self.loaded = source, loaded
        self.mate_in, self.own, self.chip_in = mate_in, own, chip_in
        self.s1, self.r1, self.s2, self.r2, self.ld = sems


def wide_place():
    me = lax.axis_index("wide")
    return lax.div(me, 2), lax.rem(me, 2)


def item_chip(k, chips):
    chip, _ = wide_place()
    return lax.rem(chip + 1 + k, chips)


def to_mate(item, k, chips):
    chip, core = wide_place()
    there = item_chip(k, chips)
    return pltpu.make_async_remote_copy(
        src_ref=item.source(2 * there + 1 - core), dst_ref=item.mate_in.at[k],
        send_sem=item.s1.at[k], recv_sem=item.r1.at[k],
        device_id=(2 * chip + 1 - core, lax.axis_index("narrow")), device_id_type=MESH,
    )


def own_load(item, k, chips):
    _, core = wide_place()
    there = item_chip(k, chips)
    return pltpu.make_async_copy(item.source(2 * there + core), item.own.at[k], item.ld.at[k])


def to_chip(item, k, chips):
    _, core = wide_place()
    there = item_chip(k, chips)
    return pltpu.make_async_remote_copy(
        src_ref=item.own.at[k], dst_ref=item.chip_in.at[k],
        send_sem=item.s2.at[k], recv_sem=item.r2.at[k],
        device_id=(2 * there + core, lax.axis_index("narrow")), device_id_type=MESH,
    )


def stage_one(item, chips):
    def per_block(k, carry):
        to_mate(item, k, chips).start()
        own_load(item, k, chips).start()
        return carry

    lax.fori_loop(0, chips, per_block, 0)


def add_mate(item, k, chips):
    to_mate(item, k, chips).wait_recv()
    own_load(item, k, chips).wait()
    item.own[k] = (item.own[k].astype(f32) + item.mate_in[k].astype(f32)).astype(bf16)


def stage_two(item, chips):
    def per_block(k, carry):
        add_mate(item, k, chips)
        to_chip(item, k, chips).start()
        return carry

    lax.fori_loop(0, chips - 1, per_block, 0)
    add_mate(item, chips - 1, chips)


def arrive(item, chips):
    def per_block(k, carry):
        to_chip(item, k, chips).wait_recv()
        return carry

    lax.fori_loop(0, chips - 1, per_block, 0)


def drain(item, chips):
    def per_block(k, carry):
        to_mate(item, k, chips).wait_send()
        return carry

    def per_chip(k, carry):
        to_chip(item, k, chips).wait_send()
        return carry

    lax.fori_loop(0, chips, per_block, 0)
    lax.fori_loop(0, chips - 1, per_chip, 0)


def block_total(item, rows, chips):
    total = item.own[chips - 1, rows, :].astype(f32)
    for k in range(chips - 1):
        total = total + item.chip_in[k, rows, :].astype(f32)
    return total


def finish(item, out_ref, chips):
    height, breadth = out_ref.shape
    span = max(8, min(height, 32768 // breadth))

    def per_tile(j, squares):
        rows = tile(j, span)
        total = block_total(item, rows, chips)
        out_ref[rows, :] = total
        return squares + jnp.sum(total * total, axis=0, keepdims=True)

    squares = lax.fori_loop(0, height // span, per_tile, jnp.zeros((1, breadth), f32))
    return jnp.sum(squares, axis=1, keepdims=True)


def last_kernel(
    peers, chips, chunks,
    dkv_ref, dq_ref, n1_ref, tok_ref, gains_ref, wq_ref, wkv_ref, dh_ref, rows_ref, gain2_ref,
    cos_ref, sin_ref, gout_hbm, ggu_hbm, gdown_hbm,
    layer_ref, grad_ref, q_ref, kv_ref, out_ref, gu_ref, down_ref, gains_out_ref, norm_ref,
    dkv, gq, gkv, send, recv, gain_part, gain_mate, gain_in, gain_near, norm_own, norm_mate, norm_in,
    *rest,
):
    buffers, rest = rest[: 3 * 7], rest[3 * 7 :]
    sems, rest = rest[: 5 * 7], rest[5 * 7 :]
    s_n, r_n, s_rs, r_rs, s_small, r_small, s_small2, r_small2 = rest
    sources = (
        (lambda w: dkv_ref.at[w], True),
        (lambda w: ggu_hbm.at[0, tile(w, 128), :], True),
        (lambda w: ggu_hbm.at[1, tile(w, 128), :], True),
        (lambda w: gdown_hbm.at[:, tile(w, 128)], True),
        (lambda w: gout_hbm.at[:, tile(w, 128)], True),
        (lambda w: gq.at[tile(w, 128), :], True),
        (lambda w: gkv.at[tile(w, 128), :], True),
    )
    items = [
        Item(source, loaded, *buffers[3 * i : 3 * i + 3], sems[5 * i : 5 * i + 5])
        for i, (source, loaded) in enumerate(sources)
    ]
    pair, gate, up, down, out, query, keyval = items
    me = lax.axis_index("narrow")
    wide_me = lax.axis_index("wide")
    chip, core = wide_place()
    peer = [(wide_me, lax.rem(me + step, peers)) for step in range(1, peers)]
    mate = (2 * chip + 1 - core, me)
    across = [(2 * lax.rem(chip + step, chips) + core, me) for step in range(1, chips)]
    rows = tok_ref.shape[0]
    width = tok_ref.shape[1]
    mine = pl.ds(pl.multiple_of(me * rows, rows), rows)
    span = 256

    def remote(src, dst, ssem, rsem, there):
        return pltpu.make_async_remote_copy(
            src_ref=src, dst_ref=dst, send_sem=ssem, recv_sem=rsem,
            device_id=there, device_id_type=MESH,
        )

    def spread(ref, phase):
        copies = [
            remote(ref.at[mine, :], ref.at[mine, :], s_n.at[phase, i], r_n.at[phase, i], peer[i])
            for i in range(peers - 1)
        ]
        for copy in copies:
            copy.start()
        return copies

    greet(peer + across + [mate])
    stage_one(pair, chips)
    layer_ref[mine, :] = rows_ref[...]
    layer_copies = spread(layer_ref, 0)

    def grad_query(j, carry):
        gq[tile(j, span), :] = dot_tn(n1_ref[:, tile(j, span)], dq_ref[...]).astype(bf16)
        return carry

    stage_two(pair, chips)
    for item in (gate, up, down, out):
        stage_one(item, chips)
    lax.fori_loop(0, width // span, grad_query, 0)
    stage_one(query, chips)
    arrive(pair, chips)
    total = block_total(pair, pl.ds(0, dkv.shape[0]), chips)
    lane = lax.broadcasted_iota(jnp.int32, total.shape, 1)
    turned = total * cos_ref[...] - swap_halves(total) * sin_ref[...]
    dkv[...] = jnp.where(lane < HD, turned, total).astype(bf16)

    chunk = width // chunks

    def rs_copy(slot, c):
        theirs = pl.ds(pl.multiple_of(peer[slot][1] * rows, rows), rows)
        return remote(
            send.at[theirs, tile(c, chunk)], recv.at[slot, :, tile(c, chunk)],
            s_rs.at[slot, c], r_rs.at[slot, c], peer[slot],
        )

    def scatter(c, carry):
        columns = tile(c, chunk)
        send[:, columns] = (
            dot_nt(dq_ref[...], wq_ref[columns, :]) + dot_nt(dkv[...], wkv_ref[columns, :])
        ).astype(bf16)
        for slot in range(peers - 1):
            rs_copy(slot, c).start()
        return carry

    lax.fori_loop(0, chunks, scatter, 0)

    def grad_keyval(j, carry):
        gkv[tile(j, span), :] = dot_tn(n1_ref[:, tile(j, span)], dkv[...]).astype(bf16)
        return carry

    lax.fori_loop(0, width // span, grad_keyval, 0)
    stage_one(keyval, chips)
    for item in (gate, up):
        stage_two(item, chips)

    def scatter_wait(c, carry):
        for slot in range(peers - 1):
            rs_copy(slot, c).wait()
        return carry

    lax.fori_loop(0, chunks, scatter_wait, 0)
    total = send[mine, :].astype(f32)
    for slot in range(peers - 1):
        total = total + recv[slot].astype(f32)
    values = tok_ref[...].astype(f32)
    inverse = lax.rsqrt(jnp.mean(values * values, axis=-1, keepdims=True) + norm_eps)
    z1 = values * inverse
    gain_part[...] = jnp.where(
        lax.broadcasted_iota(jnp.int32, gain_part.shape, 0) == 0,
        jnp.sum(total * z1, axis=0, keepdims=True), gain2_ref[...],
    )
    gain_copy = remote(gain_part, gain_mate, s_small.at[0], r_small.at[0], mate)
    gain_copy.start()
    weighted = total * gains_ref[0:1, :].astype(f32)
    grad_ref[mine, :] = (
        dh_ref[...] + inverse * (weighted - z1 * jnp.mean(weighted * z1, axis=-1, keepdims=True))
    ).astype(bf16)
    grad_copies = spread(grad_ref, 1)

    for item in (down, out, query, keyval):
        stage_two(item, chips)
    gain_copy.wait()
    gain_mate[...] = gain_mate[...] + gain_part[...]
    gain_copies = []
    for step in range(chips - 1):
        there = across[step][0]
        copy = remote(
            gain_mate.at[:, tile(there, 128)], gain_in.at[step],
            s_small.at[step + 1], r_small.at[step + 1], across[step],
        )
        copy.start()
        gain_copies.append(copy)
    squares = jnp.zeros((1, 1), f32)
    for item, share in (
        (gate, gu_ref.at[0]), (up, gu_ref.at[1]), (down, down_ref), (out, out_ref),
        (query, q_ref), (keyval, kv_ref),
    ):
        arrive(item, chips)
        squares = squares + finish(item, share, chips)
    for copy in gain_copies:
        copy.wait()
    total = gain_mate[:, tile(wide_me, 128)]
    for step in range(chips - 1):
        total = total + gain_in[step]
    row = lax.broadcasted_iota(jnp.int32, total.shape, 0)
    gain_near[peers - 1] = jnp.where(row < 2, total, jnp.broadcast_to(squares, total.shape))
    near_copies = [
        remote(gain_near.at[peers - 1], gain_near.at[i], s_n.at[2, i], r_n.at[2, i], peer[i])
        for i in range(peers - 1)
    ]
    for copy in near_copies:
        copy.start()
    for copy in near_copies:
        copy.wait()
    total = gain_near[0]
    for i in range(1, peers):
        total = total + gain_near[i]
    gains_out_ref[...] = total
    kept = jnp.where(row < 2, total, 0.0)
    gain_squares = jnp.sum(jnp.sum(kept * kept, axis=1, keepdims=True), axis=0, keepdims=True)
    norm_own[...] = total[2:3, :] + jnp.broadcast_to(gain_squares, norm_own.shape)
    copy = remote(norm_own, norm_mate, s_small2.at[0], r_small2.at[0], mate)
    copy.start()
    copy.wait()
    norm_mate[...] = norm_mate[...] + norm_own[...]
    copies = [
        remote(norm_mate, norm_in.at[step], s_small2.at[step + 1], r_small2.at[step + 1], across[step])
        for step in range(chips - 1)
    ]
    for copy in copies:
        copy.start()
    for copy in copies:
        copy.wait()
    total = norm_mate[...]
    for step in range(chips - 1):
        total = total + norm_in[step]
    norm_ref[...] = jnp.sqrt(total)
    for copy in layer_copies + grad_copies:
        copy.wait()
    for item in items:
        drain(item, chips)


def last(
    peers, chips, dkv, dq, n1, tok_rows, gains, wq, wkv, dh, layer_rows, gain2, cosine, sine,
    gout, ggu, gdown,
):
    count, width = n1.shape
    rows = tok_rows.shape[0]
    wide_count = 2 * chips
    share = width // wide_count
    units = gdown.shape[0]
    heads = gout.shape[0]
    chunks = 4
    here = pl.BlockSpec(memory_space=pltpu.VMEM)
    anywhere = pl.BlockSpec(memory_space=pl.ANY)
    shape = jax.ShapeDtypeStruct
    dma = pltpu.SemaphoreType.DMA
    blocks = (
        (count, 2 * HD), (share, units), (share, units), (units, share), (heads, share),
        (share, heads), (share, 2 * HD),
    )
    buffers, sems = [], []
    for block in blocks:
        buffers += [
            pltpu.VMEM((chips, *block), bf16), pltpu.VMEM((chips, *block), bf16),
            pltpu.VMEM((chips - 1, *block), bf16),
        ]
        sems += [dma((chips,)), dma((chips,)), dma((chips - 1,)), dma((chips - 1,)), dma((chips,))]
    return pl.pallas_call(
        functools.partial(last_kernel, peers, chips, chunks),
        out_shape=(
            shape((count, width), bf16),
            shape((count, width), bf16),
            shape((share, heads), f32),
            shape((share, 2 * HD), f32),
            shape((heads, share), f32),
            shape((2, share, units), f32),
            shape((units, share), f32),
            shape((8, share), f32),
            shape((8, share), f32),
        ),
        in_specs=[here] * 12 + [anywhere] * 3,
        out_specs=(here,) * 9,
        scratch_shapes=[
            pltpu.VMEM((count, 2 * HD), bf16),
            pltpu.VMEM((width, heads), bf16),
            pltpu.VMEM((width, 2 * HD), bf16),
            pltpu.VMEM((count, width), bf16),
            pltpu.VMEM((peers - 1, rows, width), bf16),
            pltpu.VMEM((8, width), f32),
            pltpu.VMEM((8, width), f32),
            pltpu.VMEM((chips - 1, 8, share), f32),
            pltpu.VMEM((peers, 8, share), f32),
            pltpu.VMEM((8, share), f32),
            pltpu.VMEM((8, share), f32),
            pltpu.VMEM((chips - 1, 8, share), f32),
            *buffers,
            *sems,
            dma((3, peers - 1)),
            dma((3, peers - 1)),
            dma((peers - 1, chunks)),
            dma((peers - 1, chunks)),
            dma((chips,)),
            dma((chips,)),
            dma((chips,)),
            dma((chips,)),
        ],
        compiler_params=pltpu.CompilerParams(
            collective_id=3, has_side_effects=True, vmem_limit_bytes=63 * MB
        ),
        name="last",
    )(
        dkv, dq, n1, tok_rows, gains, wq, wkv, dh, layer_rows, gain2, cosine, sine, gout, ggu, gdown
    )


def rope_tables(positions, head_width):
    half_width = head_width // 2
    exponent = jnp.arange(half_width, dtype=jnp.float32) * (2.0 / head_width)
    base_freq = jnp.power(jnp.float32(rope_theta), -exponent)
    wavelen = 2.0 * math.pi / base_freq
    smooth = (rope_context / wavelen - rope_low) / (rope_high - rope_low)
    blended = (1.0 - smooth) * base_freq / rope_factor + smooth * base_freq
    scaled = jnp.where(
        wavelen < rope_context / rope_high,
        base_freq,
        jnp.where(wavelen > rope_context / rope_low, base_freq / rope_factor, blended),
    )
    angles = positions.astype(jnp.float32)[:, None] * scaled[None, :]
    return (jnp.cos(angles), jnp.sin(angles))


def adam_update(weight, gradient, old_first, old_second, step_rate, decay_factor):
    momentum = beta_first * old_first + (1.0 - beta_first) * gradient
    variance = beta_second * old_second + (1.0 - beta_second) * gradient * gradient
    corrected = momentum / (1.0 - beta_first**STEP)
    second_hat = variance / (1.0 - beta_second**STEP)
    updated = weight * (1.0 - step_rate * decay_factor) - step_rate * corrected / (
        jnp.sqrt(second_hat) + adam_eps
    )
    return (updated, momentum, variance)


def shards(
    tokens,
    cotangent,
    lengths,
    query_weight,
    keyval_weight,
    output_weight,
    gateup_weight,
    down_weight,
    norm_gains,
    query_first,
    keyval_first,
    output_first,
    gateup_first,
    down_first,
    gains_first,
    query_second,
    keyval_second,
    output_second,
    gateup_second,
    down_second,
    gains_second,
):
    bucket_count, row_count, model_width = tokens.shape
    wide_count = lax.axis_size("wide")
    narrow_count = lax.axis_size("narrow")
    wide_rank = lax.axis_index("wide")
    narrow_rank = lax.axis_index("narrow")
    token_count = bucket_count * row_count
    share_rows = token_count // narrow_count
    positions = wide_rank * row_count + jnp.arange(row_count, dtype=jnp.int32)
    cosine, sine_table = rope_tables(positions, HD)
    cosine = jnp.tile(jnp.concatenate([cosine, cosine], axis=1), (bucket_count, 2))
    sine_table = jnp.tile(jnp.concatenate([-sine_table, sine_table], axis=1), (bucket_count, 2))
    inputs = tokens.reshape(token_count, model_width)
    live_mask = (positions[None, :] < lengths[:, None]).astype(jnp.bfloat16)
    grad_low = (cotangent * live_mask[:, :, None]).reshape(token_count, model_width)
    pair_weight = jnp.concatenate([keyval_weight[0], keyval_weight[1]], axis=1)

    def rows_of(values):
        return lax.dynamic_slice_in_dim(values, narrow_rank * share_rows, share_rows, 0)

    normed_one, queries, pairs = front(
        wide_count, inputs, norm_gains, query_weight, pair_weight, cosine, sine_table
    )
    attended_low, attended, logs = attend(lengths, queries, pairs)
    (
        hidden, result_rows, grad_heads, grad_hidden, gain_two, output_grad, gateup_grad, down_grad,
    ) = middle(
        narrow_count, attended_low, output_weight, rows_of(inputs),
        rows_of(grad_low), grad_low, norm_gains, gateup_weight, down_weight,
    )
    grad_query, grad_pairs = attend_back(
        lengths, queries, pairs, attended, logs, grad_heads, cosine, sine_table
    )
    (
        layer_out, input_grad, query_sum, pair_sum, output_sum, gateup_sum, down_sum, gains_sum, norm,
    ) = last(
        narrow_count, wide_count // 2, grad_pairs, grad_query, normed_one, rows_of(inputs),
        norm_gains, query_weight, pair_weight, grad_hidden, result_rows, gain_two, cosine,
        sine_table, output_grad, gateup_grad, down_grad,
    )
    layer_out = layer_out.reshape(bucket_count, row_count, model_width)
    input_grad = input_grad.reshape(bucket_count, row_count, model_width)
    keyval_sum = jnp.stack([pair_sum[:, :HD], pair_sum[:, HD:]])
    gains_sum = gains_sum[:2]
    reduced = (query_sum, keyval_sum, output_sum, gateup_sum, down_sum, gains_sum)
    grad_norm = norm[0, 0]
    factor = jnp.minimum(1.0, clip_limit / (grad_norm + 1e-06))

    def owned(weight, along):
        piece_size = weight.shape[along] // wide_count
        return lax.dynamic_slice_in_dim(weight, wide_rank * piece_size, piece_size, along).astype(
            jnp.float32
        )

    olds = (
        owned(query_weight, 0),
        owned(keyval_weight, 1),
        owned(output_weight, 1),
        owned(gateup_weight, 1),
        owned(down_weight, 1),
        owned(norm_gains, 1),
    )
    firsts = (query_first, keyval_first, output_first, gateup_first, down_first, gains_first)
    seconds = (query_second, keyval_second, output_second, gateup_second, down_second, gains_second)
    clipped = tuple((matrix * factor for matrix in reduced))
    results = []
    for number in range(6):
        step_rate = gain_rate if number == 5 else learn_rate
        decay_factor = 0.0 if number == 5 else decay_rate
        results.append(
            adam_update(
                olds[number],
                clipped[number],
                firsts[number],
                seconds[number],
                step_rate,
                decay_factor,
            )
        )
    return (
        layer_out,
        input_grad,
        clipped[0],
        clipped[1],
        clipped[2],
        clipped[3],
        clipped[4],
        clipped[5],
        grad_norm,
        results[0][1],
        results[1][1],
        results[2][1],
        results[3][1],
        results[4][1],
        results[5][1],
        results[0][2],
        results[1][2],
        results[2][2],
        results[3][2],
        results[4][2],
        results[5][2],
        results[0][0],
        results[1][0],
        results[2][0],
        results[3][0],
        results[4][0],
        results[5][0],
    )


def solution(mesh):
    return jax.shard_map(
        shards,
        mesh=mesh,
        in_specs=(
            P(None, "wide", None),
            P(None, "wide", None),
            P(),
            P(None, "narrow"),
            P(None, None, "narrow"),
            P("narrow", None),
            P(None, None, "narrow"),
            P("narrow", None),
            P(),
            P("wide", "narrow"),
            P(None, "wide", "narrow"),
            P("narrow", "wide"),
            P(None, "wide", "narrow"),
            P("narrow", "wide"),
            P(None, "wide"),
            P("wide", "narrow"),
            P(None, "wide", "narrow"),
            P("narrow", "wide"),
            P(None, "wide", "narrow"),
            P("narrow", "wide"),
            P(None, "wide"),
        ),
        out_specs=(
            P(None, "wide", None),
            P(None, "wide", None),
            P("wide", "narrow"),
            P(None, "wide", "narrow"),
            P("narrow", "wide"),
            P(None, "wide", "narrow"),
            P("narrow", "wide"),
            P(None, "wide"),
            P(),
            P("wide", "narrow"),
            P(None, "wide", "narrow"),
            P("narrow", "wide"),
            P(None, "wide", "narrow"),
            P("narrow", "wide"),
            P(None, "wide"),
            P("wide", "narrow"),
            P(None, "wide", "narrow"),
            P("narrow", "wide"),
            P(None, "wide", "narrow"),
            P("narrow", "wide"),
            P(None, "wide"),
            P("wide", "narrow"),
            P(None, "wide", "narrow"),
            P("narrow", "wide"),
            P(None, "wide", "narrow"),
            P("narrow", "wide"),
            P(None, "wide"),
        ),
        check_vma=False,
    )
```

```python
import functools
import math

import jax
import jax.numpy as jnp
from jax import lax
from jax.experimental import pallas as pl
from jax.experimental.pallas import tpu as pltpu
from jax.sharding import PartitionSpec as P

HD = 64
STEP = 10


norm_eps = 1e-05
rope_theta = 500000.0
rope_factor = 32.0
rope_low = 1.0
rope_high = 4.0
rope_context = 8192.0
clip_limit = 1.0
beta_first = 0.9
beta_second = 0.95
adam_eps = 1e-08
learn_rate = 0.09
gain_rate = 1.2
decay_rate = 0.1
masked_score = -1e30


bf16 = jnp.bfloat16
f32 = jnp.float32
MESH = pl.DeviceIdType.MESH
MB = 1024 * 1024
SLOTS = 7


def dot_nn(a, b):
    return jnp.dot(a, b, preferred_element_type=f32)


def dot_nt(a, b):
    return lax.dot_general(a, b, (((1,), (1,)), ((), ())), preferred_element_type=f32)


def dot_tn(a, b):
    return lax.dot_general(a, b, (((0,), (0,)), ((), ())), preferred_element_type=f32)


def tile(j, size):
    return pl.ds(pl.multiple_of(j * size, size), size)


def greet(targets):
    barrier = pltpu.get_barrier_semaphore()
    for target in targets:
        pl.semaphore_signal(barrier, inc=1, device_id=target, device_id_type=MESH)
    pl.semaphore_wait(barrier, len(targets))


def remote(src, dst, ssem, rsem, there):
    return pltpu.make_async_remote_copy(
        src_ref=src, dst_ref=dst, send_sem=ssem, recv_sem=rsem,
        device_id=there, device_id_type=MESH,
    )


class Grid:
    def __init__(self, axis):
        wide_me, narrow_me = lax.axis_index("wide"), lax.axis_index("narrow")
        self.axis, self.wide_me, self.narrow_me = axis, wide_me, narrow_me
        place = narrow_me if axis == "narrow" else lax.div(wide_me, 2)
        self.core = lax.rem(wide_me, 2)
        self.pair, self.ring = lax.div(place, 4), lax.rem(place, 4)

    def block(self, other, step):
        pair = 1 - self.pair if other else self.pair
        return 4 * pair + lax.rem(self.ring + step + 4, 4)

    def device(self, other, step):
        index = self.block(other, step)
        if self.axis == "narrow":
            return (self.wide_me, index)
        return (2 * index + self.core, self.narrow_me)

    def neighbours(self):
        return [self.device(0, 1), self.device(0, -1), self.device(0, 2), self.device(1, 0)]


def mate_of():
    wide_me = lax.axis_index("wide")
    return (wide_me + 1 - 2 * lax.rem(wide_me, 2), lax.axis_index("narrow"))


def mirror_of():
    return (lax.axis_size("wide") - 1 - lax.axis_index("wide"), lax.axis_index("narrow"))


class TreeSum:
    first = (((1, 1), (0, 1)), ((1, -1), (0, -1)), ((1, 2), (1, 0)), ((0, 1), (0, 1)), ((0, -1), (0, -1)))
    second = (((1, 0), (1, 0)), ((0, 2), (0, 2)))

    def __init__(self, grid, part, into, ssem, rsem):
        self.grid, self.part, self.into, self.ssem, self.rsem = grid, part, into, ssem, rsem

    def copy(self, slot):
        block, there = (self.first + self.second)[slot]
        return remote(
            self.part(self.grid.block(*block)), self.into(slot), self.ssem.at[slot],
            self.rsem.at[slot], self.grid.device(*there),
        )

    def start(self):
        for slot in range(5):
            self.copy(slot).start()

    def relay(self, add):
        self.copy(0).wait_recv()
        self.copy(1).wait_recv()
        add(self.grid.block(1, 0), (0, 1))
        self.copy(5).start()
        self.copy(2).wait_recv()
        add(self.grid.block(0, 2), (2,))
        self.copy(6).start()

    def arrive(self):
        for slot in (3, 4, 5, 6):
            self.copy(slot).wait_recv()

    def drain(self):
        for slot in range(SLOTS):
            self.copy(slot).wait_send()


class TreeGather:
    plan = (
        ((0, 0), (1, 0)), ((0, 0), (0, 1)), ((0, 0), (0, -1)), ((0, 0), (0, 2)),
        ((1, 0), (0, 1)), ((1, 0), (0, -1)), ((0, 2), (1, 0)),
    )
    lands = ((1, 0), (0, -1), (0, 1), (0, 2), (1, -1), (1, 1), (1, 2))

    def __init__(self, grid, place, ssem, rsem):
        self.grid, self.place, self.ssem, self.rsem = grid, place, ssem, rsem

    def copy(self, slot):
        block, there = self.plan[slot]
        ref = self.place(self.grid.block(*block))
        return remote(ref, ref, self.ssem.at[slot], self.rsem.at[slot], self.grid.device(*there))

    def start(self):
        for slot in range(4):
            self.copy(slot).start()

    def relay(self):
        self.copy(0).wait_recv()
        self.copy(4).start()
        self.copy(5).start()
        self.copy(3).wait_recv()
        self.copy(6).start()

    def arrive(self):
        for slot in (1, 2, 4, 5, 6):
            self.copy(slot).wait_recv()

    def drain(self):
        for slot in range(SLOTS):
            self.copy(slot).wait_send()


class MateSum:
    def __init__(self, source, own, into, ssem, rsem, lsem=None):
        self.source, self.own, self.into = source, own, into
        self.ssem, self.rsem, self.lsem = ssem, rsem, lsem

    def out(self, k):
        core = lax.rem(lax.axis_index("wide"), 2)
        return remote(
            self.source(2 * k + 1 - core), self.into(k), self.ssem.at[k], self.rsem.at[k], mate_of()
        )

    def start(self):
        def per_block(k, carry):
            self.out(k).start()
            return carry

        lax.fori_loop(0, 8, per_block, 0)

    def add(self):
        core = lax.rem(lax.axis_index("wide"), 2)

        def per_block(k, carry):
            self.out(k).wait_recv()
            self.own(k)[...] = (
                self.source(2 * k + core)[...].astype(f32) + self.into(k)[...].astype(f32)
            ).astype(bf16)
            return carry

        lax.fori_loop(0, 8, per_block, 0)

    def drain(self):
        def per_block(k, carry):
            self.out(k).wait_send()
            return carry

        lax.fori_loop(0, 8, per_block, 0)


def swap_halves(u):
    half = HD // 2
    width = u.shape[-1]
    lane = lax.broadcasted_iota(jnp.int32, u.shape, u.ndim - 1)
    ahead = pltpu.roll(u, width - half, u.ndim - 1)
    behind = pltpu.roll(u, half, u.ndim - 1)
    return jnp.where(lax.rem(lane, HD) < half, ahead, behind)


def inverse_rms(values):
    return lax.rsqrt(jnp.mean(values * values, axis=-1, keepdims=True) + norm_eps)


def head_lanes(pair, odd, high):
    lane = lax.broadcasted_iota(jnp.int32, pair.shape, 1)
    if odd != high:
        pair = pltpu.roll(pair, HD, 1)
    return jnp.where((lane >= HD) == high, pair, 0.0)


def pair_lanes(even, odd):
    lane = lax.broadcasted_iota(jnp.int32, even.shape, 1)
    return jnp.where(lane < HD, even, pltpu.roll(odd, HD, 1))


def key_block(kv, j, bucket, length):
    rows = kv.shape[1] // 2
    block = kv[pl.ds(2 * j, 2), pl.ds(bucket * rows, rows), :].reshape(2 * rows, 2 * HD)
    lane = lax.broadcasted_iota(jnp.int32, block.shape, 1)
    key = 2 * rows * j + lax.broadcasted_iota(jnp.int32, block.shape, 0)
    bias = jnp.where(key < length, 0.0, masked_score)
    masked = jnp.where(lane < HD, block.astype(f32), jnp.where(lane == HD, bias, 0.0)).astype(bf16)
    return block, masked


def head_stack(values, heads, high):
    return jnp.concatenate(
        [
            head_lanes(values[:, (head // 2) * 2 * HD : (head // 2 + 1) * 2 * HD], head % 2 == 1, high)
            for head in range(heads)
        ],
        axis=0,
    )


def forward_kernel(
    len_ref, tok_ref, gains_ref, wq_ref, wkv_ref, cos_ref, sin_ref, wo_hbm, wgu_hbm, wd_hbm, cot_hbm,
    n1_hbm, kv_hbm, qs_ref, os_ref, log_ref, hidden_ref, mixed_ref, dh_ref, gain_ref, dob_ref, gout_ref,
    pgate_hbm, pup_hbm, pdown_hbm,
    wo, wgu, wd, dyb, n1, kv, q, qm, ob, om, da, n2, dgu, dhb, part1, part2, into1, into2,
    mate_gu, mate_d, gdn,
    in_sem, out_sem, st_sem, kv_s, kv_r, km_s, km_r, ex_s, ex_r, rs_s, rs_r, ag_s, ag_r, mt_s, mt_r,
):
    narrow, wide = Grid("narrow"), Grid("wide")
    me, wide_me = narrow.narrow_me, narrow.wide_me
    core = wide.core
    chip = lax.div(wide_me, 2)
    last_chip = lax.axis_size("wide") // 2 - 1
    mate, mirror = mate_of(), mirror_of()
    tokens, width = tok_ref.shape
    rows = tokens // 2
    half = rows // 2
    share = rows // lax.axis_size("narrow")
    units = wd.shape[0]
    heads = wo.shape[0] // HD
    span = 256
    loads = [
        pltpu.make_async_copy(src, dst, in_sem.at[i])
        for i, (src, dst) in enumerate(((wo_hbm, wo), (cot_hbm, dyb), (wd_hbm, wd), (wgu_hbm, wgu)))
    ]
    for load in loads:
        load.start()
    greet(narrow.neighbours() + wide.neighbours() + [mate, mirror])

    def normed(j, carry):
        at = tile(j, 64)
        values = tok_ref[at, :].astype(f32)
        n1[at, :] = (values * inverse_rms(values) * gains_ref[0:1, :].astype(f32)).astype(bf16)
        return carry

    lax.fori_loop(0, tokens // 64, normed, 0)
    cosine, sine = cos_ref[...], sin_ref[...]
    value = dot_nn(n1[...], wkv_ref[...])
    lane = lax.broadcasted_iota(jnp.int32, value.shape, 1)
    kv[wide_me] = jnp.where(lane < HD, value * cosine + swap_halves(value) * sine, value).astype(bf16)
    keys = TreeGather(wide, lambda b: kv.at[2 * b + core], kv_s, kv_r)
    keys.start()

    def to_mate(block, i):
        ref = kv.at[2 * block + core]
        return remote(ref, ref, km_s.at[i], km_r.at[i], mate)

    to_mate(chip, 7).start()
    for pair in range(heads // 2):
        columns = pl.ds(pair * 2 * HD, 2 * HD)
        value = dot_nn(n1[...], wq_ref[:, columns])
        q[:, columns] = ((value * cosine + swap_halves(value) * sine) * HD**-0.5).astype(bf16)

    def later(bucket):
        return pl.ds(bucket * rows + half, half)

    queries = [
        remote(q.at[later(b), :], qm.at[b], ex_s.at[0, b], ex_r.at[0, b], mirror) for b in range(2)
    ]
    for copy in queries:
        copy.start()
    store_n1 = pltpu.make_async_copy(n1, n1_hbm, out_sem.at[0])
    store_n1.start()
    keys.relay()
    relayed = [wide.block(1, 0), wide.block(0, 2)]
    for i in range(2):
        to_mate(relayed[i], i).start()
    keys.arrive()
    relayed += [wide.block(*where) for where in ((0, -1), (0, 1), (1, -1), (1, 1), (1, 2))]
    for i in range(2, 7):
        to_mate(relayed[i], i).start()
    for copy in queries:
        copy.wait_recv()
    for b in range(2):
        for g in range(2):
            held = (q[pl.ds(b * rows, half), :] if g == 0 else qm[b]).astype(f32)
            stack = head_stack(held, heads, False)
            lane = lax.broadcasted_iota(jnp.int32, stack.shape, 1)
            qs_ref[b, g] = jnp.where(lane == HD, 1.0, stack).astype(bf16)
    loads[1].wait()
    for b in range(2):
        place = wide_me * rows + lax.broadcasted_iota(jnp.int32, (rows, 1), 0)
        mine = pl.ds(b * rows, rows)
        live = (place < len_ref[b]).astype(f32)
        dyb[mine, :] = (dyb[mine, :].astype(f32) * live).astype(bf16)
    for i in range(7):
        to_mate(relayed[i], i).wait_recv()
    to_mate(chip, 7).wait_recv()
    store_kv = pltpu.make_async_copy(kv, kv_hbm, out_sem.at[1])
    store_kv.start()

    parts = 2
    stack_rows = heads * half
    part_rows = stack_rows // parts

    def attention(b, g):
        length = len_ref[b]
        final = chip if g == 0 else last_chip - chip
        first = wide_me * rows if g == 0 else (2 * last_chip + 1 - wide_me) * rows + half

        def step(masked, j, carry):
            block, scored = key_block(kv, j, b, length)
            lane = lax.broadcasted_iota(jnp.int32, block.shape, 1)
            summed = jnp.where(lane < HD, jnp.ones_like(block), block)
            if masked:
                shape = (part_rows, 2 * rows)
                key = 2 * rows * j + lax.broadcasted_iota(jnp.int32, shape, 1)
                place = first + lax.rem(lax.broadcasted_iota(jnp.int32, shape, 0), half)
                allowed = key <= place
            result = []
            for p in range(parts):
                best, total = carry[p]
                scores = dot_nt(qs_ref[b, g, pl.ds(p * part_rows, part_rows), :], scored)
                if masked:
                    scores = jnp.where(allowed, scores, masked_score)
                new_best = jnp.maximum(best, jnp.max(scores, axis=-1, keepdims=True))
                weights = jnp.exp(scores - new_best).astype(bf16)
                total = total * jnp.exp(best - new_best) + dot_nn(weights, summed)
                result.append((new_best, total))
            return tuple(result)

        carry = tuple(
            (jnp.full((part_rows, 1), masked_score, f32), jnp.zeros((part_rows, 2 * HD), f32))
            for _ in range(parts)
        )
        carry = lax.fori_loop(0, final, functools.partial(step, False), carry)
        carry = step(True, final, carry)
        for p in range(parts):
            best, total = carry[p]
            lane = lax.broadcasted_iota(jnp.int32, total.shape, 1)
            sums = jnp.where(lane < HD, total, pltpu.roll(total, HD, 1))
            out = total / sums
            at = pl.ds(p * part_rows, part_rows)
            os_ref[b, g, at, :] = out
            logs = jnp.transpose(best + jnp.log(sums))
            log_ref[pl.ds(2 * b + g, 1), at] = logs[0:1, :]
        for pair in range(heads // 2):
            even = os_ref[b, g, pl.ds(2 * pair * half, half), :]
            odd = os_ref[b, g, pl.ds((2 * pair + 1) * half, half), :]
            value = pair_lanes(pltpu.roll(even, HD, 1), pltpu.roll(odd, HD, 1)).astype(bf16)
            columns = pl.ds(pair * 2 * HD, 2 * HD)
            if g == 0:
                ob[pl.ds(b * rows, half), columns] = value
            else:
                om[b, :, columns] = value

    def back_to_mirror(b):
        return remote(om.at[b], ob.at[later(b), :], ex_s.at[1, b], ex_r.at[1, b], mirror)

    def mine_in(b):
        return pl.ds(pl.multiple_of(b * rows + me * share, share), share)

    def their_rows(b):
        return lambda block: pl.ds(pl.multiple_of(b * rows + block * share, share), share)

    def sum_of(b, part, into, number):
        where = their_rows(b)
        return TreeSum(
            narrow, lambda block: part.at[where(block), :], lambda slot: into.at[b, slot],
            rs_s.at[number, b], rs_r.at[number, b],
        )

    def adder(b, part, into):
        where = their_rows(b)

        def add(block, slots):
            total = part[where(block), :].astype(f32)
            for slot in slots:
                total = total + into[b, slot].astype(f32)
            part[where(block), :] = total.astype(bf16)

        return add

    def total_of(b, part, into):
        total = part[mine_in(b), :].astype(f32)
        for slot in (3, 4, 5, 6):
            total = total + into[b, slot].astype(f32)
        return total

    def gather_of(b, buffer, number):
        where = their_rows(b)
        return TreeGather(
            narrow, lambda block: buffer.at[where(block), :], ag_s.at[number, b], ag_r.at[number, b]
        )

    sums1 = [sum_of(b, part1, into1, 0) for b in range(2)]
    sums2 = [sum_of(b, part2, into2, 1) for b in range(2)]
    gather1 = [gather_of(b, n2, 0) for b in range(2)]
    gather2 = [gather_of(b, dhb, 1) for b in range(2)]

    def project(b):
        back_to_mirror(b).wait_recv()
        mine = pl.ds(b * rows, rows)
        part1[mine, :] = dot_nn(ob[mine, :], wo[...]).astype(bf16)
        sums1[b].start()

    attention(0, 1)
    back_to_mirror(0).start()
    attention(0, 0)
    attention(1, 1)
    back_to_mirror(1).start()
    loads[0].wait()
    project(0)
    attention(1, 0)
    project(1)
    sums1[0].relay(adder(0, part1, into1))
    loads[2].wait()

    def grad_middle(j, carry):
        da[:, tile(j, span)] = dot_nt(dyb[...], wd[tile(j, span), :])
        return carry

    lax.fori_loop(0, units // span, grad_middle, 0)
    sums1[1].relay(adder(1, part1, into1))
    gain2 = gains_ref[1:2, :].astype(f32)
    gain_ref[...] = jnp.zeros(gain_ref.shape, f32)

    def second_norm(b):
        sums1[b].arrive()
        hidden = tok_ref[mine_in(b), :].astype(f32) + total_of(b, part1, into1)
        hidden_ref[b] = hidden
        n2[mine_in(b), :] = (hidden * inverse_rms(hidden) * gain2).astype(bf16)
        gather1[b].start()

    second_norm(0)
    second_norm(1)
    loads[3].wait()
    gather1[0].relay()
    gather1[1].relay()

    def feed(b):
        gather1[b].arrive()
        mine = pl.ds(b * rows, rows)

        def gate_up(j, carry):
            columns = tile(j, span)
            gate = dot_nn(n2[mine, :], wgu[0, :, columns])
            up = dot_nn(n2[mine, :], wgu[1, :, columns])
            sigmoid = jax.nn.sigmoid(gate)
            activated = gate * sigmoid
            mixed_ref[mine, columns] = (activated * up).astype(bf16)
            grad = da[mine, columns]
            dgu[0, mine, columns] = (
                grad * up * sigmoid * (1.0 + gate * (1.0 - sigmoid))
            ).astype(bf16)
            dgu[1, mine, columns] = (grad * activated).astype(bf16)
            return carry

        lax.fori_loop(0, units // span, gate_up, 0)

        def grad_norm_two(c, carry):
            columns = tile(c, 512)
            part2[mine, columns] = (
                dot_nt(dgu[0, mine, :], wgu[0, columns, :]) + dot_nt(dgu[1, mine, :], wgu[1, columns, :])
            ).astype(bf16)
            return carry

        lax.fori_loop(0, width // 512, grad_norm_two, 0)
        sums2[b].start()

    feed(0)
    feed(1)
    sums2[0].relay(adder(0, part2, into2))

    def grad_gateup(which):
        def per_tile(j, carry):
            wgu[which, tile(j, span), :] = dot_tn(n2[:, tile(j, span)], dgu[which]).astype(bf16)
            return carry

        lax.fori_loop(0, width // span, per_tile, 0)

    grad_gateup(0)
    wide_share = width // 16
    mates = [
        MateSum(
            lambda w: wgu.at[0, tile(w, wide_share), :], lambda k: wgu.at[0, tile(2 * k + core, wide_share), :],
            lambda k: mate_gu.at[0, k], mt_s.at[0], mt_r.at[0],
        ),
        MateSum(
            lambda w: wgu.at[1, tile(w, wide_share), :], lambda k: wgu.at[1, tile(2 * k + core, wide_share), :],
            lambda k: mate_gu.at[1, k], mt_s.at[1], mt_r.at[1],
        ),
        MateSum(
            lambda w: gdn.at[w], lambda k: gdn.at[2 * k + core],
            lambda k: mate_d.at[k], mt_s.at[2], mt_r.at[2],
        ),
    ]
    mates[0].start()
    sums2[1].relay(adder(1, part2, into2))

    def second_norm_back(b):
        sums2[b].arrive()
        total = total_of(b, part2, into2)
        hidden = hidden_ref[b]
        inverse = inverse_rms(hidden)
        z2 = hidden * inverse
        gain_ref[pl.ds(b, 1), :] = jnp.sum(total * z2, axis=0, keepdims=True)
        weighted = total * gain2
        dh = dyb[mine_in(b), :].astype(f32) + inverse * (
            weighted - z2 * jnp.mean(weighted * z2, axis=-1, keepdims=True)
        )
        dh_ref[b] = dh
        dhb[mine_in(b), :] = dh.astype(bf16)
        gather2[b].start()

    second_norm_back(0)
    second_norm_back(1)
    grad_gateup(1)
    mates[1].start()
    gather2[0].relay()
    gather2[1].relay()

    def grad_down(j, carry):
        found = dot_tn(mixed_ref[:, tile(j, span)], dyb[...]).astype(bf16)
        for w in range(16):
            gdn[w, tile(j, span), :] = found[:, w * wide_share : (w + 1) * wide_share]
        return carry

    lax.fori_loop(0, units // span, grad_down, 0)
    mates[2].start()
    mates[0].add()
    for b in range(2):
        gather2[b].arrive()
        mine = pl.ds(b * rows, rows)
        dob_ref[mine, :] = dot_nt(dhb[mine, :], wo[...]).astype(bf16)

    def grad_out(j, carry):
        gout_ref[:, tile(j, span)] = dot_tn(ob[...], dhb[:, tile(j, span)]).astype(bf16)
        return carry

    lax.fori_loop(0, width // span, grad_out, 0)

    def kept(which, out_hbm, k):
        return pltpu.make_async_copy(mates[which].own(k), out_hbm.at[k], st_sem.at[which, k])

    outs = (pgate_hbm, pup_hbm, pdown_hbm)

    def keep(which):
        def per_block(k, carry):
            kept(which, outs[which], k).start()
            return carry

        lax.fori_loop(0, 8, per_block, 0)

    keep(0)
    for which in (1, 2):
        mates[which].add()
        keep(which)
    for b in range(2):
        sums1[b].drain()
        sums2[b].drain()
        gather1[b].drain()
        gather2[b].drain()
        queries[b].wait_send()
        back_to_mirror(b).wait_send()
    keys.drain()
    for i in range(7):
        to_mate(relayed[i], i).wait_send()
    to_mate(chip, 7).wait_send()
    for sums in mates:
        sums.drain()
    store_n1.wait()
    store_kv.wait()
    for which in range(3):
        def per_store(k, carry):
            kept(which, outs[which], k).wait()
            return carry

        lax.fori_loop(0, 8, per_store, 0)


def forward(lengths, tokens, gains, wq, wkv, cosine, sine, wo, wgu, wd, cotangent):
    count, width = tokens.shape
    rows = count // 2
    share = rows // 8
    units = wd.shape[0]
    lanes = wq.shape[1]
    heads = lanes // HD
    stack = heads * rows // 2
    wide_count = 16
    wide_share = width // wide_count
    here = pl.BlockSpec(memory_space=pltpu.VMEM)
    anywhere = pl.BlockSpec(memory_space=pl.ANY)
    shape = jax.ShapeDtypeStruct
    dma = pltpu.SemaphoreType.DMA
    vmem = pltpu.VMEM
    return pl.pallas_call(
        forward_kernel,
        out_shape=(
            shape((count, width), bf16),
            shape((wide_count, count, 2 * HD), bf16),
            shape((2, 2, stack, 2 * HD), bf16),
            shape((2, 2, stack, 2 * HD), f32),
            shape((8, stack), f32),
            shape((2, share, width), f32),
            shape((count, units), bf16),
            shape((2, share, width), f32),
            shape((8, width), f32),
            shape((count, lanes), bf16),
            shape((lanes, width), bf16),
            shape((8, wide_share, units), bf16),
            shape((8, wide_share, units), bf16),
            shape((8, units, wide_share), bf16),
        ),
        in_specs=[pl.BlockSpec(memory_space=pltpu.SMEM)] + [here] * 6 + [anywhere] * 4,
        out_specs=(anywhere, anywhere) + (here,) * 9 + (anywhere,) * 3,
        scratch_shapes=[
            vmem(wo.shape, bf16),
            vmem(wgu.shape, bf16),
            vmem(wd.shape, bf16),
            vmem((count, width), bf16),
            vmem((count, width), bf16),
            vmem((wide_count, count, 2 * HD), bf16),
            vmem((count, lanes), bf16),
            vmem((2, rows // 2, lanes), bf16),
            vmem((count, lanes), bf16),
            vmem((2, rows // 2, lanes), bf16),
            vmem((count, units), f32),
            vmem((count, width), bf16),
            vmem((2, count, units), bf16),
            vmem((count, width), bf16),
            vmem((count, width), bf16),
            vmem((count, width), bf16),
            vmem((2, SLOTS, share, width), bf16),
            vmem((2, SLOTS, share, width), bf16),
            vmem((2, 8, wide_share, units), bf16),
            vmem((8, units, wide_share), bf16),
            vmem((wide_count, units, wide_share), bf16),
            dma((4,)),
            dma((2,)),
            dma((3, 8)),
            dma((SLOTS,)),
            dma((SLOTS,)),
            dma((8,)),
            dma((8,)),
            dma((2, 2)),
            dma((2, 2)),
            dma((2, 2, SLOTS)),
            dma((2, 2, SLOTS)),
            dma((2, 2, SLOTS)),
            dma((2, 2, SLOTS)),
            dma((3, 8)),
            dma((3, 8)),
        ],
        compiler_params=pltpu.CompilerParams(
            collective_id=1, has_side_effects=True, vmem_limit_bytes=63 * MB
        ),
        name="forward",
    )(lengths, tokens, gains, wq, wkv, cosine, sine, wo, wgu, wd, cotangent)


def block_adder(part, into):
    def add(block, slots):
        total = part(block)[...].astype(f32)
        for slot in slots:
            total = total + into(slot)[...].astype(f32)
        part(block)[...] = total.astype(part(block).dtype)

    return add


class Item:
    def __init__(self, grid, part, into, ssem, rsem, mates=None):
        self.part, self.into, self.mates = part, into, mates
        self.own = grid.block(0, 0)
        self.tree = TreeSum(grid, lambda b: part.at[b], lambda slot: into.at[slot], ssem, rsem)
        self.add = block_adder(lambda b: part.at[b], lambda slot: into.at[slot])

    def relay(self):
        self.tree.relay(self.add)

    def finish(self, out_ref):
        self.tree.arrive()
        height, breadth = out_ref.shape
        span = max(8, min(height, 32768 // breadth))

        def per_tile(j, squares):
            rows = tile(j, span)
            total = self.part[self.own, rows, :].astype(f32)
            for slot in (3, 4, 5, 6):
                total = total + self.into[slot, rows, :].astype(f32)
            out_ref[rows, :] = total
            return squares + jnp.sum(total * total, axis=0, keepdims=True)

        squares = lax.fori_loop(0, height // span, per_tile, jnp.zeros((1, breadth), f32))
        return jnp.sum(squares, axis=1, keepdims=True)

    def drain(self):
        self.tree.drain()
        if self.mates is not None:
            self.mates.drain()


def backward_kernel(
    len_ref, tok_hbm, gains_ref, wq_ref, wkv_ref, cos_ref, sin_ref, cosq_ref, sinq_ref,
    qs_ref, os_ref, log_ref, hidden_ref, mixed_ref, dh_ref, gain2_ref, dob_ref, gout_ref,
    kv_hbm, n1_hbm, wd_hbm, pgate_hbm, pup_hbm, pdown_hbm,
    layer_ref, grad_ref, q_ref, pair_ref, out_ref, gu_ref, down_ref, gains_out_ref, norm_ref,
    kv, n1, wd, tok, pgate, pup, pdown, pout, pq, pkv, igate, iup, idown, iout, iq, ikv,
    mout, mq, mkv, gq, gkv, part3, part4, into3, into4, acc, dkv, dkm, dkin, dkv_low, dq, dqm, dm,
    dos, qclean, delta, dqacc, gpart, gmate, gin, near, norm_own, norm_mate, norm_all,
    ld_sem, rs_s, rs_r, ag_s, ag_r, dm_s, dm_r, dt_s, dt_r, im_s, im_r, it_s, it_r, ex_s, ex_r,
    g_s, g_r, h_s, h_r, w_s, w_r, sm_s, sm_r,
):
    narrow, wide = Grid("narrow"), Grid("wide")
    me, wide_me = narrow.narrow_me, narrow.wide_me
    core = wide.core
    chip = lax.div(wide_me, 2)
    last_chip = lax.axis_size("wide") // 2 - 1
    peers = lax.axis_size("narrow")
    mate, mirror = mate_of(), mirror_of()
    tokens, width = layer_ref.shape
    rows = tokens // 2
    half = rows // 2
    share = rows // peers
    heads = wq_ref.shape[1] // HD
    span = 256
    wide_share = width // 16

    def mine_in(b):
        return pl.ds(pl.multiple_of(b * rows + me * share, share), share)

    def later(b):
        return pl.ds(b * rows + half, half)

    pairs = (
        (kv_hbm, kv), (wd_hbm, wd), (pgate_hbm, pgate), (pdown_hbm, pdown), (pup_hbm, pup), (n1_hbm, n1),
        (tok_hbm.at[mine_in(0), :], tok.at[0]), (tok_hbm.at[mine_in(1), :], tok.at[1]),
    )
    loads = [pltpu.make_async_copy(src, dst, ld_sem.at[i]) for i, (src, dst) in enumerate(pairs)]
    for load in loads:
        load.start()
    greet(narrow.neighbours() + wide.neighbours() + [mate, mirror])

    grads_there = [
        remote(dob_ref.at[later(b), :], dm.at[b], ex_s.at[0, b], ex_r.at[0, b], mirror) for b in range(2)
    ]
    for copy in grads_there:
        copy.start()

    def mates_of(source, own, into, number):
        return MateSum(
            source, lambda k: own.at[k], lambda k: into.at[k], im_s.at[number], im_r.at[number]
        )

    gate = Item(wide, pgate, igate, it_s.at[0], it_r.at[0])
    up = Item(wide, pup, iup, it_s.at[1], it_r.at[1])
    down = Item(wide, pdown, idown, it_s.at[2], it_r.at[2])
    out = Item(
        wide, pout, iout, it_s.at[3], it_r.at[3],
        mates_of(lambda w: gout_ref.at[:, tile(w, wide_share)], pout, mout, 0),
    )
    query = Item(
        wide, pq, iq, it_s.at[4], it_r.at[4],
        mates_of(lambda w: gq.at[tile(w, wide_share), :], pq, mq, 1),
    )
    keyval = Item(
        wide, pkv, ikv, it_s.at[5], it_r.at[5],
        mates_of(lambda w: gkv.at[tile(w, wide_share), :], pkv, mkv, 2),
    )
    out.mates.start()

    def their_rows(b):
        return lambda block: pl.ds(pl.multiple_of(b * rows + block * share, share), share)

    def sum_of(b, part, into, number):
        where = their_rows(b)
        return TreeSum(
            narrow, lambda block: part.at[where(block), :], lambda slot: into.at[b, slot],
            rs_s.at[number, b], rs_r.at[number, b],
        )

    def adder(b, part, into):
        where = their_rows(b)
        return block_adder(lambda block: part.at[where(block), :], lambda slot: into.at[b, slot])

    def total_of(b, part, into):
        total = part[mine_in(b), :].astype(f32)
        for slot in (3, 4, 5, 6):
            total = total + into[b, slot].astype(f32)
        return total

    def gather_of(b, buffer, number):
        where = their_rows(b)
        return TreeGather(
            narrow, lambda block: buffer.at[where(block), :], ag_s.at[number, b], ag_r.at[number, b]
        )

    sums3 = [sum_of(b, part3, into3, 0) for b in range(2)]
    sums4 = [sum_of(b, part4, into4, 1) for b in range(2)]
    gather3 = [gather_of(b, layer_ref, 0) for b in range(2)]
    gather4 = [gather_of(b, grad_ref, 1) for b in range(2)]

    loads[1].wait()
    for b in range(2):
        mine = pl.ds(b * rows, rows)

        def feed(c, carry):
            part3[mine, tile(c, 512)] = dot_nn(mixed_ref[mine, :], wd[:, tile(c, 512)]).astype(bf16)
            return carry

        lax.fori_loop(0, width // 512, feed, 0)
        sums3[b].start()
    for i, item in ((2, gate), (3, down), (4, up)):
        loads[i].wait()
        item.tree.start()
    loads[0].wait()
    stack_rows = heads * half
    parts = 2
    part_rows = stack_rows // parts

    def attention(b, g):
        length = len_ref[b]
        final = chip if g == 0 else last_chip - chip
        first = wide_me * rows if g == 0 else (2 * last_chip + 1 - wide_me) * rows + half
        held = (dob_ref[pl.ds(b * rows, half), :] if g == 0 else dm[b]).astype(f32)
        stack = head_stack(held, heads, True)
        dos[...] = stack.astype(bf16)
        for p in range(parts):
            at = pl.ds(p * part_rows, part_rows)
            product = stack[p * part_rows : (p + 1) * part_rows] * os_ref[b, g, at, :]
            delta[:, at] = jnp.sum(jnp.transpose(product), axis=0, keepdims=True)
        lane = lax.broadcasted_iota(jnp.int32, qclean.shape, 1)
        qclean[...] = jnp.where(lane < HD, qs_ref[b, g].astype(f32), 0.0).astype(bf16)
        dqacc[...] = jnp.zeros(dqacc.shape, f32)

        def step(masked, j, carry):
            block, scored = key_block(kv, j, b, length)
            if masked:
                shape = (2 * rows, part_rows)
                key = 2 * rows * j + lax.broadcasted_iota(jnp.int32, shape, 0)
                place = first + lax.rem(lax.broadcasted_iota(jnp.int32, shape, 1), half)
                allowed = key <= place
            total = acc[j]
            for p in range(parts):
                at = pl.ds(p * part_rows, part_rows)
                scores = dot_nt(scored, qs_ref[b, g, at, :])
                if masked:
                    scores = jnp.where(allowed, scores, masked_score)
                chances = jnp.exp(scores - log_ref[pl.ds(2 * b + g, 1), at])
                slope = (chances * (dot_nt(block, dos[at, :]) - delta[:, at])).astype(bf16)
                total = total + dot_nn(slope, qclean[at, :]) + dot_nn(chances.astype(bf16), dos[at, :])
                dqacc[at, :] = dqacc[at, :] + dot_tn(slope, block)
            acc[j] = total
            return carry

        lax.fori_loop(0, final, functools.partial(step, False), 0)
        step(True, final, 0)
        for pair in range(heads // 2):
            even = dqacc[pl.ds(2 * pair * half, half), :]
            odd = dqacc[pl.ds((2 * pair + 1) * half, half), :]
            value = pair_lanes(even, odd) * HD**-0.5
            value = (value * cosq_ref[g] - swap_halves(value) * sinq_ref[g]).astype(bf16)
            columns = pl.ds(pair * 2 * HD, 2 * HD)
            if g == 0:
                dq[pl.ds(b * rows, half), columns] = value
            else:
                dqm[b, :, columns] = value

    def query_back(b):
        return remote(dqm.at[b], dq.at[later(b), :], ex_s.at[1, b], ex_r.at[1, b], mirror)

    def clear():
        def per_block(j, carry):
            acc[j] = jnp.zeros(acc.shape[1:], f32)
            return carry

        lax.fori_loop(0, acc.shape[0], per_block, 0)

    pair_mates = [
        MateSum(
            lambda w, b=b: dkv.at[b, w], lambda k, b=b: dkv.at[b, 2 * k + core],
            lambda k, b=b: dkm.at[b, k], dm_s.at[b], dm_r.at[b],
        )
        for b in range(2)
    ]
    pair_trees = [
        TreeSum(
            wide, lambda block, b=b: dkv.at[b, 2 * block + core], lambda slot, b=b: dkin.at[b, slot],
            dt_s.at[b], dt_r.at[b],
        )
        for b in range(2)
    ]

    def pair_relay(b):
        pair_trees[b].relay(
            block_adder(lambda block: dkv.at[b, 2 * block + core], lambda slot: dkin.at[b, slot])
        )

    def pair_send(b):
        def per_block(j, carry):
            dkv[b, pl.ds(2 * j, 2)] = acc[j].astype(bf16).reshape(2, rows, 2 * HD)
            return carry

        lax.fori_loop(0, acc.shape[0], per_block, 0)
        pair_mates[b].start()

    def pair_mid(b):
        pair_mates[b].add()
        pair_trees[b].start()

    def pair_total(b):
        pair_trees[b].arrive()
        total = dkv[b, wide_me].astype(f32)
        for slot in (3, 4, 5, 6):
            total = total + dkin[b, slot].astype(f32)
        mine = pl.ds(b * rows, rows)
        lane = lax.broadcasted_iota(jnp.int32, total.shape, 1)
        turned = total * cos_ref[...] - swap_halves(total) * sin_ref[...]
        dkv_low[mine, :] = jnp.where(lane < HD, turned, total).astype(bf16)

    def norm_one_back(b):
        mine = pl.ds(b * rows, rows)

        def per_chunk(c, carry):
            columns = tile(c, 512)
            part4[mine, columns] = (
                dot_nt(dq[mine, :], wq_ref[columns, :]) + dot_nt(dkv_low[mine, :], wkv_ref[columns, :])
            ).astype(bf16)
            return carry

        lax.fori_loop(0, width // 512, per_chunk, 0)
        sums4[b].start()

    def result_rows(b):
        sums3[b].arrive()
        layer_ref[mine_in(b), :] = (hidden_ref[b] + total_of(b, part3, into3)).astype(bf16)
        gather3[b].start()

    gains1 = gains_ref[0:1, :].astype(f32)

    def input_rows(b):
        sums4[b].arrive()
        total = total_of(b, part4, into4)
        values = tok[b].astype(f32)
        inverse = inverse_rms(values)
        z1 = values * inverse
        weighted = total * gains1
        grad_ref[mine_in(b), :] = (
            dh_ref[b] + inverse * (weighted - z1 * jnp.mean(weighted * z1, axis=-1, keepdims=True))
        ).astype(bf16)
        gather4[b].start()
        return jnp.sum(total * z1, axis=0, keepdims=True)

    clear()
    for copy in grads_there:
        copy.wait_recv()
    attention(0, 1)
    query_back(0).start()
    attention(0, 0)
    pair_send(0)
    sums3[0].relay(adder(0, part3, into3))
    sums3[1].relay(adder(1, part3, into3))
    clear()
    attention(1, 1)
    query_back(1).start()
    pair_mid(0)
    result_rows(0)
    result_rows(1)
    attention(1, 0)
    pair_send(1)
    pair_relay(0)
    for item in (gate, down):
        item.relay()
    gather3[0].relay()
    gather3[1].relay()
    out.mates.add()
    out.tree.start()
    pair_mid(1)
    pair_total(0)
    query_back(0).wait_recv()
    norm_one_back(0)
    query_back(1).wait_recv()
    loads[5].wait()

    def grad_query(j, carry):
        gq[tile(j, span), :] = dot_tn(n1[:, tile(j, span)], dq[...]).astype(bf16)
        return carry

    lax.fori_loop(0, width // span, grad_query, 0)
    query.mates.start()
    pair_relay(1)
    up.relay()
    sums4[0].relay(adder(0, part4, into4))
    pair_total(1)
    norm_one_back(1)

    def grad_keyval(j, carry):
        gkv[tile(j, span), :] = dot_tn(n1[:, tile(j, span)], dkv_low[...]).astype(bf16)
        return carry

    lax.fori_loop(0, width // span, grad_keyval, 0)
    keyval.mates.start()
    query.mates.add()
    query.tree.start()
    loads[6].wait()
    loads[7].wait()
    gain1 = input_rows(0)
    keyval.mates.add()
    keyval.tree.start()
    sums4[1].relay(adder(1, part4, into4))
    out.relay()
    gather4[0].relay()
    query.relay()
    keyval.relay()
    gain1 = gain1 + input_rows(1)

    row = lax.broadcasted_iota(jnp.int32, gpart.shape, 0)
    gain2 = gain2_ref[0:1, :] + gain2_ref[1:2, :]
    gpart[...] = jnp.where(row == 0, gain1, jnp.where(row == 1, gain2, 0.0))
    gain_mate = remote(gpart, gmate, sm_s.at[0], sm_r.at[0], mate)
    gain_mate.start()
    squares = gate.finish(gu_ref.at[0]) + down.finish(down_ref) + up.finish(gu_ref.at[1])
    gain_mate.wait()
    gpart[...] = gpart[...] + gmate[...]
    def gain_block(block):
        return gpart.at[:, tile(2 * block + core, wide_share)]

    gain_tree = TreeSum(wide, gain_block, lambda slot: gin.at[slot], g_s, g_r)
    gain_tree.start()
    gather4[1].relay()
    squares = squares + out.finish(out_ref) + query.finish(q_ref) + keyval.finish(pair_ref)
    gain_tree.relay(block_adder(gain_block, lambda slot: gin.at[slot]))
    gain_tree.arrive()
    total = gpart[:, tile(wide_me, wide_share)]
    for slot in (3, 4, 5, 6):
        total = total + gin[slot]
    row = lax.broadcasted_iota(jnp.int32, total.shape, 0)
    near[me] = jnp.where(row < 2, total, jnp.broadcast_to(squares, total.shape))
    near_gather = TreeGather(narrow, lambda block: near.at[block], h_s, h_r)
    near_gather.start()
    near_gather.relay()
    near_gather.arrive()
    total = near[0]
    for i in range(1, 8):
        total = total + near[i]
    gains_out_ref[...] = total
    kept = jnp.where(row < 2, total, 0.0)
    gain_squares = jnp.sum(jnp.sum(kept * kept, axis=1, keepdims=True), axis=0, keepdims=True)
    norm_own[...] = total[2:3, :] + jnp.broadcast_to(gain_squares, norm_own.shape)
    norm_copy = remote(norm_own, norm_mate, sm_s.at[1], sm_r.at[1], mate)
    norm_copy.start()
    norm_copy.wait()
    norm_all[chip] = norm_own[...] + norm_mate[...]
    norm_gather = TreeGather(wide, lambda block: norm_all.at[block], w_s, w_r)
    norm_gather.start()
    norm_gather.relay()
    norm_gather.arrive()
    total = norm_all[0]
    for i in range(1, 8):
        total = total + norm_all[i]
    norm_ref[...] = jnp.sqrt(total)
    for b in range(2):
        gather3[b].arrive()
        gather4[b].arrive()
        for each in (sums3[b], sums4[b], gather3[b], gather4[b], pair_mates[b], pair_trees[b]):
            each.drain()
        grads_there[b].wait_send()
        query_back(b).wait_send()
    for item in (gate, up, down, out, query, keyval, gain_tree, near_gather, norm_gather):
        item.drain()


def backward(
    lengths, tokens, gains, wq, wkv, cosine, sine, cosq, sinq, qs, outs, logs, hidden, mixed, dh, gain2,
    dob, gout, kv, n1, wd, pgate, pup, pdown,
):
    count, width = n1.shape
    rows = count // 2
    share = rows // 8
    units = wd.shape[0]
    lanes = wq.shape[1]
    stack = qs.shape[2]
    wide_count = 16
    wide_share = width // wide_count
    here = pl.BlockSpec(memory_space=pltpu.VMEM)
    anywhere = pl.BlockSpec(memory_space=pl.ANY)
    shape = jax.ShapeDtypeStruct
    dma = pltpu.SemaphoreType.DMA
    vmem = pltpu.VMEM
    blocks = (
        (wide_share, units), (wide_share, units), (units, wide_share), (lanes, wide_share),
        (wide_share, lanes), (wide_share, 2 * HD),
    )
    return pl.pallas_call(
        backward_kernel,
        out_shape=(
            shape((count, width), bf16),
            shape((count, width), bf16),
            shape((wide_share, lanes), f32),
            shape((wide_share, 2 * HD), f32),
            shape((lanes, wide_share), f32),
            shape((2, wide_share, units), f32),
            shape((units, wide_share), f32),
            shape((8, wide_share), f32),
            shape((8, wide_share), f32),
        ),
        in_specs=[pl.BlockSpec(memory_space=pltpu.SMEM), anywhere] + [here] * 16 + [anywhere] * 6,
        out_specs=(here,) * 9,
        scratch_shapes=[
            vmem(kv.shape, bf16),
            vmem((count, width), bf16),
            vmem(wd.shape, bf16),
            vmem((2, share, width), bf16),
            *[vmem((8, *block), bf16) for block in blocks],
            *[vmem((SLOTS, *block), bf16) for block in blocks],
            *[vmem((8, *block), bf16) for block in blocks[3:]],
            vmem((width, lanes), bf16),
            vmem((width, 2 * HD), bf16),
            vmem((count, width), bf16),
            vmem((count, width), bf16),
            vmem((2, SLOTS, share, width), bf16),
            vmem((2, SLOTS, share, width), bf16),
            vmem((8, 2 * rows, 2 * HD), f32),
            vmem((2, wide_count, rows, 2 * HD), bf16),
            vmem((2, 8, rows, 2 * HD), bf16),
            vmem((2, SLOTS, rows, 2 * HD), bf16),
            vmem((count, 2 * HD), bf16),
            vmem((count, lanes), bf16),
            vmem((2, rows // 2, lanes), bf16),
            vmem((2, rows // 2, lanes), bf16),
            vmem((stack, 2 * HD), bf16),
            vmem((stack, 2 * HD), bf16),
            vmem((1, stack), f32),
            vmem((stack, 2 * HD), f32),
            vmem((8, width), f32),
            vmem((8, width), f32),
            vmem((SLOTS, 8, wide_share), f32),
            vmem((8, 8, wide_share), f32),
            vmem((8, wide_share), f32),
            vmem((8, wide_share), f32),
            vmem((8, 8, wide_share), f32),
            dma((8,)),
            dma((2, 2, SLOTS)),
            dma((2, 2, SLOTS)),
            dma((2, 2, SLOTS)),
            dma((2, 2, SLOTS)),
            dma((2, 8)),
            dma((2, 8)),
            dma((2, SLOTS)),
            dma((2, SLOTS)),
            dma((3, 8)),
            dma((3, 8)),
            dma((6, SLOTS)),
            dma((6, SLOTS)),
            dma((2, 2)),
            dma((2, 2)),
            dma((SLOTS,)),
            dma((SLOTS,)),
            dma((SLOTS,)),
            dma((SLOTS,)),
            dma((SLOTS,)),
            dma((SLOTS,)),
            dma((2,)),
            dma((2,)),
        ],
        compiler_params=pltpu.CompilerParams(
            collective_id=2, has_side_effects=True, vmem_limit_bytes=63 * MB
        ),
        name="backward",
    )(
        lengths, tokens, gains, wq, wkv, cosine, sine, cosq, sinq, qs, outs, logs, hidden, mixed, dh,
        gain2, dob, gout, kv, n1, wd, pgate, pup, pdown,
    )


def rope_tables(positions, head_width):
    half_width = head_width // 2
    exponent = jnp.arange(half_width, dtype=jnp.float32) * (2.0 / head_width)
    base_freq = jnp.power(jnp.float32(rope_theta), -exponent)
    wavelen = 2.0 * math.pi / base_freq
    smooth = (rope_context / wavelen - rope_low) / (rope_high - rope_low)
    blended = (1.0 - smooth) * base_freq / rope_factor + smooth * base_freq
    scaled = jnp.where(
        wavelen < rope_context / rope_high,
        base_freq,
        jnp.where(wavelen > rope_context / rope_low, base_freq / rope_factor, blended),
    )
    angles = positions.astype(jnp.float32)[:, None] * scaled[None, :]
    return (jnp.cos(angles), jnp.sin(angles))


def adam_update(weight, gradient, old_first, old_second, step_rate, decay_factor):
    momentum = beta_first * old_first + (1.0 - beta_first) * gradient
    variance = beta_second * old_second + (1.0 - beta_second) * gradient * gradient
    corrected = momentum / (1.0 - beta_first**STEP)
    second_hat = variance / (1.0 - beta_second**STEP)
    updated = weight * (1.0 - step_rate * decay_factor) - step_rate * corrected / (
        jnp.sqrt(second_hat) + adam_eps
    )
    return (updated, momentum, variance)


def shards(
    tokens,
    cotangent,
    lengths,
    query_weight,
    keyval_weight,
    output_weight,
    gateup_weight,
    down_weight,
    norm_gains,
    query_first,
    keyval_first,
    output_first,
    gateup_first,
    down_first,
    gains_first,
    query_second,
    keyval_second,
    output_second,
    gateup_second,
    down_second,
    gains_second,
):
    bucket_count, row_count, model_width = tokens.shape
    wide_count = lax.axis_size("wide")
    wide_rank = lax.axis_index("wide")
    token_count = bucket_count * row_count
    half = row_count // 2

    def lane_tables(rank, first, count):
        positions = rank * row_count + first + jnp.arange(count, dtype=jnp.int32)
        cosine, sine = rope_tables(positions, HD)
        return (
            jnp.concatenate([cosine] * 4, axis=1),
            jnp.concatenate([-sine, sine, -sine, sine], axis=1),
        )

    cosine, sine = lane_tables(wide_rank, 0, row_count)
    mirror_cosine, mirror_sine = lane_tables(wide_count - 1 - wide_rank, half, half)
    inputs = tokens.reshape(token_count, model_width)
    pair_weight = jnp.concatenate([keyval_weight[0], keyval_weight[1]], axis=1)
    (
        normed_one, pairs, query_stack, out_stack, logs, hidden, mixed, grad_hidden, gain_two, grad_heads,
        output_grad, gate_part, up_part, down_part,
    ) = forward(
        lengths, inputs, norm_gains, query_weight, pair_weight, jnp.concatenate([cosine, cosine]),
        jnp.concatenate([sine, sine]), output_weight, gateup_weight, down_weight,
        cotangent.reshape(token_count, model_width),
    )
    (
        layer_out, input_grad, query_sum, pair_sum, output_sum, gateup_sum, down_sum, gains_sum, norm,
    ) = backward(
        lengths, inputs, norm_gains, query_weight, pair_weight, cosine, sine,
        jnp.stack([cosine[:half], mirror_cosine]), jnp.stack([sine[:half], mirror_sine]),
        query_stack, out_stack, logs, hidden, mixed, grad_hidden, gain_two, grad_heads, output_grad,
        pairs, normed_one, down_weight, gate_part, up_part, down_part,
    )
    layer_out = layer_out.reshape(bucket_count, row_count, model_width)
    input_grad = input_grad.reshape(bucket_count, row_count, model_width)
    keyval_sum = jnp.stack([pair_sum[:, :HD], pair_sum[:, HD:]])
    gains_sum = gains_sum[:2]
    reduced = (query_sum, keyval_sum, output_sum, gateup_sum, down_sum, gains_sum)
    grad_norm = norm[0, 0]
    factor = jnp.minimum(1.0, clip_limit / (grad_norm + 1e-06))

    def owned(weight, along):
        piece_size = weight.shape[along] // wide_count
        return lax.dynamic_slice_in_dim(weight, wide_rank * piece_size, piece_size, along).astype(
            jnp.float32
        )

    olds = (
        owned(query_weight, 0),
        owned(keyval_weight, 1),
        owned(output_weight, 1),
        owned(gateup_weight, 1),
        owned(down_weight, 1),
        owned(norm_gains, 1),
    )
    firsts = (query_first, keyval_first, output_first, gateup_first, down_first, gains_first)
    seconds = (query_second, keyval_second, output_second, gateup_second, down_second, gains_second)
    clipped = tuple((matrix * factor for matrix in reduced))
    results = []
    for number in range(6):
        step_rate = gain_rate if number == 5 else learn_rate
        decay_factor = 0.0 if number == 5 else decay_rate
        results.append(
            adam_update(
                olds[number],
                clipped[number],
                firsts[number],
                seconds[number],
                step_rate,
                decay_factor,
            )
        )
    return (
        layer_out,
        input_grad,
        clipped[0],
        clipped[1],
        clipped[2],
        clipped[3],
        clipped[4],
        clipped[5],
        grad_norm,
        results[0][1],
        results[1][1],
        results[2][1],
        results[3][1],
        results[4][1],
        results[5][1],
        results[0][2],
        results[1][2],
        results[2][2],
        results[3][2],
        results[4][2],
        results[5][2],
        results[0][0],
        results[1][0],
        results[2][0],
        results[3][0],
        results[4][0],
        results[5][0],
    )


def solution(mesh):
    return jax.shard_map(
        shards,
        mesh=mesh,
        in_specs=(
            P(None, "wide", None),
            P(None, "wide", None),
            P(),
            P(None, "narrow"),
            P(None, None, "narrow"),
            P("narrow", None),
            P(None, None, "narrow"),
            P("narrow", None),
            P(),
            P("wide", "narrow"),
            P(None, "wide", "narrow"),
            P("narrow", "wide"),
            P(None, "wide", "narrow"),
            P("narrow", "wide"),
            P(None, "wide"),
            P("wide", "narrow"),
            P(None, "wide", "narrow"),
            P("narrow", "wide"),
            P(None, "wide", "narrow"),
            P("narrow", "wide"),
            P(None, "wide"),
        ),
        out_specs=(
            P(None, "wide", None),
            P(None, "wide", None),
            P("wide", "narrow"),
            P(None, "wide", "narrow"),
            P("narrow", "wide"),
            P(None, "wide", "narrow"),
            P("narrow", "wide"),
            P(None, "wide"),
            P(),
            P("wide", "narrow"),
            P(None, "wide", "narrow"),
            P("narrow", "wide"),
            P(None, "wide", "narrow"),
            P("narrow", "wide"),
            P(None, "wide"),
            P("wide", "narrow"),
            P(None, "wide", "narrow"),
            P("narrow", "wide"),
            P(None, "wide", "narrow"),
            P("narrow", "wide"),
            P(None, "wide"),
            P("wide", "narrow"),
            P(None, "wide", "narrow"),
            P("narrow", "wide"),
            P(None, "wide", "narrow"),
            P("narrow", "wide"),
            P(None, "wide"),
        ),
        check_vma=False,
    )
```

```python
import functools
import math

import jax
import jax.numpy as jnp
import numpy as np
from jax import lax
from jax.experimental import pallas as pl
from jax.experimental.pallas import tpu as pltpu
from jax.sharding import PartitionSpec as P

HD = 64
STEP = 10


norm_eps = 1e-05
rope_theta = 500000.0
rope_factor = 32.0
rope_low = 1.0
rope_high = 4.0
rope_context = 8192.0
clip_limit = 1.0
beta_first = 0.9
beta_second = 0.95
adam_eps = 1e-08
learn_rate = 0.09
gain_rate = 1.2
decay_rate = 0.1
masked_score = -1e30

bf16 = jnp.bfloat16
f32 = jnp.float32
MESH = pl.DeviceIdType.MESH
MB = 1024 * 1024
SLOTS = 7


def lane_tables(positions):
    half_width = HD // 2
    base_freq = rope_theta ** (-np.arange(half_width) * (2.0 / HD))
    wavelen = 2.0 * math.pi / base_freq
    smooth = (rope_context / wavelen - rope_low) / (rope_high - rope_low)
    blended = (1.0 - smooth) * base_freq / rope_factor + smooth * base_freq
    scaled = np.where(
        wavelen < rope_context / rope_high,
        base_freq,
        np.where(wavelen > rope_context / rope_low, base_freq / rope_factor, blended),
    )
    lanes = jnp.asarray(np.tile(scaled, 4), f32)
    sign = jnp.asarray(np.tile(np.repeat([-1.0, 1.0], half_width), 2), f32)
    angles = positions.astype(f32)[:, None] * lanes[None, :]
    return jnp.cos(angles), jnp.sin(angles) * sign[None, :]


def adam_update(weight, gradient, old_first, old_second, step_rate, decay_factor):
    momentum = beta_first * old_first + (1.0 - beta_first) * gradient
    variance = beta_second * old_second + (1.0 - beta_second) * gradient * gradient
    corrected = momentum / (1.0 - beta_first**STEP)
    second_hat = variance / (1.0 - beta_second**STEP)
    updated = weight * (1.0 - step_rate * decay_factor) - step_rate * corrected / (
        jnp.sqrt(second_hat) + adam_eps
    )
    return (updated, momentum, variance)


def dot_nn(a, b):
    return jnp.dot(a, b, preferred_element_type=f32)


def dot_nt(a, b):
    return lax.dot_general(a, b, (((1,), (1,)), ((), ())), preferred_element_type=f32)


def dot_tn(a, b):
    return lax.dot_general(a, b, (((0,), (0,)), ((), ())), preferred_element_type=f32)


def tile(j, size):
    return pl.ds(pl.multiple_of(j * size, size), size)


def greet(targets):
    barrier = pltpu.get_barrier_semaphore()
    for target in targets:
        pl.semaphore_signal(barrier, inc=1, device_id=target, device_id_type=MESH)
    pl.semaphore_wait(barrier, len(targets))


def remote(src, dst, ssem, rsem, there):
    return pltpu.make_async_remote_copy(
        src_ref=src, dst_ref=dst, send_sem=ssem, recv_sem=rsem,
        device_id=there, device_id_type=MESH,
    )


class Grid:
    def __init__(self, axis):
        wide_me, narrow_me = lax.axis_index("wide"), lax.axis_index("narrow")
        self.axis, self.wide_me, self.narrow_me = axis, wide_me, narrow_me
        place = narrow_me if axis == "narrow" else lax.div(wide_me, 2)
        self.core = lax.rem(wide_me, 2)
        self.pair, self.ring = lax.div(place, 4), lax.rem(place, 4)

    def block(self, other, step):
        pair = 1 - self.pair if other else self.pair
        return 4 * pair + lax.rem(self.ring + step + 4, 4)

    def device(self, other, step):
        index = self.block(other, step)
        if self.axis == "narrow":
            return (self.wide_me, index)
        return (2 * index + self.core, self.narrow_me)

    def neighbours(self):
        return [self.device(0, 1), self.device(0, -1), self.device(0, 2), self.device(1, 0)]


def others_of(axis):
    wide_me, narrow_me = lax.axis_index("wide"), lax.axis_index("narrow")
    size = lax.axis_size(axis)
    if axis == "wide":
        return [(lax.rem(wide_me + i, size), narrow_me) for i in range(1, size)]
    return [(wide_me, lax.rem(narrow_me + i, size)) for i in range(1, size)]


def exchange(source, into, axis, ssem, rsem):
    copies = [
        remote(source(there[0]), into.at[i], ssem.at[i], rsem.at[i], there)
        for i, there in enumerate(others_of(axis))
    ]
    for copy in copies:
        copy.start()
    for copy in copies:
        copy.wait()


def mate_of():
    wide_me = lax.axis_index("wide")
    return (wide_me + 1 - 2 * lax.rem(wide_me, 2), lax.axis_index("narrow"))


def mirror_of():
    return (lax.axis_size("wide") - 1 - lax.axis_index("wide"), lax.axis_index("narrow"))


class TreeSum:
    first = (((1, 1), (0, 1)), ((1, -1), (0, -1)), ((1, 2), (1, 0)), ((0, 1), (0, 1)), ((0, -1), (0, -1)))
    second = (((1, 0), (1, 0)), ((0, 2), (0, 2)))

    def __init__(self, grid, part, into, ssem, rsem):
        self.grid, self.part, self.into, self.ssem, self.rsem = grid, part, into, ssem, rsem

    def copy(self, slot):
        block, there = (self.first + self.second)[slot]
        return remote(
            self.part(self.grid.block(*block)), self.into(slot), self.ssem.at[slot],
            self.rsem.at[slot], self.grid.device(*there),
        )

    def start(self):
        for slot in range(5):
            self.copy(slot).start()

    def relay(self, add):
        self.copy(0).wait_recv()
        self.copy(1).wait_recv()
        add(self.grid.block(1, 0), (0, 1))
        self.copy(5).start()
        self.copy(2).wait_recv()
        add(self.grid.block(0, 2), (2,))
        self.copy(6).start()

    def arrive(self):
        for slot in (3, 4, 5, 6):
            self.copy(slot).wait_recv()

    def drain(self):
        for slot in range(SLOTS):
            self.copy(slot).wait_send()


class TreeGather:
    plan = (
        ((0, 0), (1, 0)), ((0, 0), (0, 1)), ((0, 0), (0, -1)), ((0, 0), (0, 2)),
        ((1, 0), (0, 1)), ((1, 0), (0, -1)), ((0, 2), (1, 0)),
    )
    lands = ((1, 0), (0, -1), (0, 1), (0, 2), (1, -1), (1, 1), (1, 2))

    def __init__(self, grid, place, ssem, rsem):
        self.grid, self.place, self.ssem, self.rsem = grid, place, ssem, rsem

    def copy(self, slot):
        block, there = self.plan[slot]
        ref = self.place(self.grid.block(*block))
        return remote(ref, ref, self.ssem.at[slot], self.rsem.at[slot], self.grid.device(*there))

    def start(self):
        for slot in range(4):
            self.copy(slot).start()

    def relay(self):
        self.copy(0).wait_recv()
        self.copy(4).start()
        self.copy(5).start()
        self.copy(3).wait_recv()
        self.copy(6).start()

    def arrive(self):
        for slot in (1, 2, 4, 5, 6):
            self.copy(slot).wait_recv()

    def drain(self):
        for slot in range(SLOTS):
            self.copy(slot).wait_send()


class MateSum:
    def __init__(self, source, own, into, ssem, rsem, lsem=None):
        self.source, self.own, self.into = source, own, into
        self.ssem, self.rsem, self.lsem = ssem, rsem, lsem

    def out(self, k):
        core = lax.rem(lax.axis_index("wide"), 2)
        return remote(
            self.source(2 * k + 1 - core), self.into(k), self.ssem.at[k], self.rsem.at[k], mate_of()
        )

    def start(self):
        def per_block(k, carry):
            self.out(k).start()
            return carry

        lax.fori_loop(0, 8, per_block, 0)

    def add(self):
        core = lax.rem(lax.axis_index("wide"), 2)

        def per_block(k, carry):
            self.out(k).wait_recv()
            self.own(k)[...] = (
                self.source(2 * k + core)[...].astype(f32) + self.into(k)[...].astype(f32)
            ).astype(bf16)
            return carry

        lax.fori_loop(0, 8, per_block, 0)

    def drain(self):
        def per_block(k, carry):
            self.out(k).wait_send()
            return carry

        lax.fori_loop(0, 8, per_block, 0)


def swap_halves(u):
    half = HD // 2
    width = u.shape[-1]
    lane = lax.broadcasted_iota(jnp.int32, u.shape, u.ndim - 1)
    ahead = pltpu.roll(u, width - half, u.ndim - 1)
    behind = pltpu.roll(u, half, u.ndim - 1)
    return jnp.where(lax.rem(lane, HD) < half, ahead, behind)


def inverse_rms(values):
    return lax.rsqrt(jnp.mean(values * values, axis=-1, keepdims=True) + norm_eps)


def head_lanes(pair, odd, high):
    lane = lax.broadcasted_iota(jnp.int32, pair.shape, 1)
    if odd != high:
        pair = pltpu.roll(pair, HD, 1)
    return jnp.where((lane >= HD) == high, pair, 0.0)


def pair_lanes(even, odd):
    lane = lax.broadcasted_iota(jnp.int32, even.shape, 1)
    return jnp.where(lane < HD, even, pltpu.roll(odd, HD, 1))


def block_adder(part, into):
    def add(block, slots):
        total = part(block)[...].astype(f32)
        for slot in slots:
            total = total + into(slot)[...].astype(f32)
        part(block)[...] = total.astype(part(block).dtype)

    return add


class Item:
    def __init__(self, grid, part, into, ssem, rsem, mates=None):
        self.part, self.into, self.mates = part, into, mates
        self.own = grid.block(0, 0)
        self.tree = TreeSum(grid, part, lambda slot: into.at[slot], ssem, rsem)
        self.add = block_adder(part, lambda slot: into.at[slot])

    def relay(self):
        self.tree.relay(self.add)

    def finish(self, out_ref):
        self.tree.arrive()
        height, breadth = out_ref.shape
        span = max(8, min(height, 32768 // breadth))

        def per_tile(j, squares):
            rows = tile(j, span)
            total = self.part(self.own)[rows, :].astype(f32)
            for slot in (3, 4, 5, 6):
                total = total + self.into[slot, rows, :].astype(f32)
            out_ref[rows, :] = total
            return squares + jnp.sum(total * total, axis=0, keepdims=True)

        squares = lax.fori_loop(0, height // span, per_tile, jnp.zeros((1, breadth), f32))
        return jnp.sum(squares, axis=1, keepdims=True)

    def drain(self):
        self.tree.drain()
        if self.mates is not None:
            self.mates.drain()


def key_block(kv, j, bucket, length):
    rows = kv.shape[1] // 2
    block = kv[pl.ds(2 * j, 2), pl.ds(bucket * rows, rows), :].reshape(2 * rows, 2 * HD)
    lane = lax.broadcasted_iota(jnp.int32, block.shape, 1)
    key = 2 * rows * j + lax.broadcasted_iota(jnp.int32, block.shape, 0)
    bias = jnp.where(key < length, 0.0, masked_score)
    masked = jnp.where(lane < HD, block.astype(f32), jnp.where(lane == HD, bias, 0.0)).astype(bf16)
    return block, masked


def head_stack(values, heads, high):
    return jnp.concatenate(
        [
            head_lanes(values[:, (head // 2) * 2 * HD : (head // 2 + 1) * 2 * HD], head % 2 == 1, high)
            for head in range(heads)
        ],
        axis=0,
    )


def forward_kernel(
    len_ref, tok_ref, gains_ref, wq_ref, wkv_ref, cos_ref, sin_ref, wo_hbm, wgu_hbm, wd_hbm, cot_hbm,
    n1_hbm, kv_hbm, qs_ref, os_ref, log_ref, hidden_ref, mixed_ref, dh_ref, gain_ref, dob_ref, gout_ref,
    gate_ref, down_ref, squares_ref, pup_hbm,
    wo, wgu, wd, dyb, n1, kv, q, qm, ob, om, da, n2, dgu, dhb, part1, part2, into1, into2,
    mate_gu, mate_d, gdn, igate, idown,
    in_sem, out_sem, st_sem, kv_s, kv_r, km_s, km_r, ex_s, ex_r, rs_s, rs_r, ag_s, ag_r, mt_s, mt_r, it_s, it_r,
):
    narrow, wide = Grid("narrow"), Grid("wide")
    me, wide_me = narrow.narrow_me, narrow.wide_me
    core = wide.core
    chip = lax.div(wide_me, 2)
    last_chip = lax.axis_size("wide") // 2 - 1
    mate, mirror = mate_of(), mirror_of()
    tokens, width = tok_ref.shape
    rows = tokens // 2
    half = rows // 2
    share = rows // lax.axis_size("narrow")
    units = wd.shape[0]
    heads = wo.shape[0] // HD
    span = 256
    loads = [
        pltpu.make_async_copy(src, dst, in_sem.at[i])
        for i, (src, dst) in enumerate(((wo_hbm, wo), (cot_hbm, dyb), (wd_hbm, wd), (wgu_hbm, wgu)))
    ]
    for load in loads:
        load.start()
    greet(narrow.neighbours() + wide.neighbours() + [mate, mirror])

    def normed(j, carry):
        at = tile(j, 64)
        values = tok_ref[at, :].astype(f32)
        n1[at, :] = (values * inverse_rms(values) * gains_ref[0:1, :].astype(f32)).astype(bf16)
        return carry

    lax.fori_loop(0, tokens // 64, normed, 0)
    cosine = jnp.concatenate([cos_ref[pl.ds(0, rows), :]] * 2, axis=0)
    sine = jnp.concatenate([sin_ref[pl.ds(0, rows), :]] * 2, axis=0)
    value = dot_nt(n1[...], wkv_ref[...])
    lane = lax.broadcasted_iota(jnp.int32, value.shape, 1)
    kv[wide_me] = jnp.where(lane < HD, value * cosine + swap_halves(value) * sine, value).astype(bf16)
    keys = TreeGather(wide, lambda b: kv.at[2 * b + core], kv_s, kv_r)
    keys.start()

    def to_mate(block, i):
        ref = kv.at[2 * block + core]
        return remote(ref, ref, km_s.at[i], km_r.at[i], mate)

    to_mate(chip, 7).start()
    for pair in range(heads // 2):
        columns = pl.ds(pair * 2 * HD, 2 * HD)
        value = dot_nn(n1[...], wq_ref[:, columns])
        q[:, columns] = ((value * cosine + swap_halves(value) * sine) * HD**-0.5).astype(bf16)

    def later(bucket):
        return pl.ds(bucket * rows + half, half)

    queries = [
        remote(q.at[later(b), :], qm.at[b], ex_s.at[0, b], ex_r.at[0, b], mirror) for b in range(2)
    ]
    for copy in queries:
        copy.start()
    store_n1 = pltpu.make_async_copy(n1, n1_hbm, out_sem.at[0])
    store_n1.start()
    keys.relay()
    relayed = [wide.block(1, 0), wide.block(0, 2)]
    for i in range(2):
        to_mate(relayed[i], i).start()
    keys.arrive()
    relayed += [wide.block(*where) for where in ((0, -1), (0, 1), (1, -1), (1, 1), (1, 2))]
    for i in range(2, 7):
        to_mate(relayed[i], i).start()
    for copy in queries:
        copy.wait_recv()
    for b in range(2):
        for g in range(2):
            held = (q[pl.ds(b * rows, half), :] if g == 0 else qm[b]).astype(f32)
            stack = head_stack(held, heads, False)
            lane = lax.broadcasted_iota(jnp.int32, stack.shape, 1)
            qs_ref[b, g] = jnp.where(lane == HD, 1.0, stack).astype(bf16)
    loads[1].wait()
    for b in range(2):
        place = wide_me * rows + lax.broadcasted_iota(jnp.int32, (rows, 1), 0)
        mine = pl.ds(b * rows, rows)
        live = (place < len_ref[b]).astype(f32)
        dyb[mine, :] = (dyb[mine, :].astype(f32) * live).astype(bf16)
    for i in range(7):
        to_mate(relayed[i], i).wait_recv()
    to_mate(chip, 7).wait_recv()
    store_kv = pltpu.make_async_copy(kv, kv_hbm, out_sem.at[1])
    store_kv.start()

    parts = 2
    stack_rows = heads * half
    part_rows = stack_rows // parts

    def attention(b, g):
        length = len_ref[b]
        final = chip if g == 0 else last_chip - chip
        first = wide_me * rows if g == 0 else (2 * last_chip + 1 - wide_me) * rows + half

        def step(masked, j, carry):
            block, scored = key_block(kv, j, b, length)
            lane = lax.broadcasted_iota(jnp.int32, block.shape, 1)
            summed = jnp.where(lane < HD, jnp.ones_like(block), block)
            if masked:
                shape = (part_rows, 2 * rows)
                key = 2 * rows * j + lax.broadcasted_iota(jnp.int32, shape, 1)
                place = first + lax.rem(lax.broadcasted_iota(jnp.int32, shape, 0), half)
                allowed = key <= place
            result = []
            for p in range(parts):
                best, total = carry[p]
                scores = dot_nt(qs_ref[b, g, pl.ds(p * part_rows, part_rows), :], scored)
                if masked:
                    scores = jnp.where(allowed, scores, masked_score)
                new_best = jnp.maximum(best, jnp.max(scores, axis=-1, keepdims=True))
                weights = jnp.exp(scores - new_best).astype(bf16)
                total = total * jnp.exp(best - new_best) + dot_nn(weights, summed)
                result.append((new_best, total))
            return tuple(result)

        carry = tuple(
            (jnp.full((part_rows, 1), masked_score, f32), jnp.zeros((part_rows, 2 * HD), f32))
            for _ in range(parts)
        )
        carry = lax.fori_loop(0, final, functools.partial(step, False), carry)
        carry = step(True, final, carry)
        for p in range(parts):
            best, total = carry[p]
            lane = lax.broadcasted_iota(jnp.int32, total.shape, 1)
            sums = jnp.where(lane < HD, total, pltpu.roll(total, HD, 1))
            out = total / sums
            at = pl.ds(p * part_rows, part_rows)
            os_ref[b, g, at, :] = out
            logs = jnp.transpose(best + jnp.log(sums))
            log_ref[pl.ds(2 * b + g, 1), at] = logs[0:1, :]
        for pair in range(heads // 2):
            even = os_ref[b, g, pl.ds(2 * pair * half, half), :]
            odd = os_ref[b, g, pl.ds((2 * pair + 1) * half, half), :]
            value = pair_lanes(pltpu.roll(even, HD, 1), pltpu.roll(odd, HD, 1)).astype(bf16)
            columns = pl.ds(pair * 2 * HD, 2 * HD)
            if g == 0:
                ob[pl.ds(b * rows, half), columns] = value
            else:
                om[b, :, columns] = value

    def back_to_mirror(b):
        return remote(om.at[b], ob.at[later(b), :], ex_s.at[1, b], ex_r.at[1, b], mirror)

    def mine_in(b):
        return pl.ds(pl.multiple_of(b * rows + me * share, share), share)

    def their_rows(b):
        return lambda block: pl.ds(pl.multiple_of(b * rows + block * share, share), share)

    def sum_of(b, part, into, number):
        where = their_rows(b)
        return TreeSum(
            narrow, lambda block: part.at[where(block), :], lambda slot: into.at[b, slot],
            rs_s.at[number, b], rs_r.at[number, b],
        )

    def adder(b, part, into):
        where = their_rows(b)

        def add(block, slots):
            total = part[where(block), :].astype(f32)
            for slot in slots:
                total = total + into[b, slot].astype(f32)
            part[where(block), :] = total.astype(bf16)

        return add

    def total_of(b, part, into):
        total = part[mine_in(b), :].astype(f32)
        for slot in (3, 4, 5, 6):
            total = total + into[b, slot].astype(f32)
        return total

    def gather_of(b, buffer, number):
        where = their_rows(b)
        return TreeGather(
            narrow, lambda block: buffer.at[where(block), :], ag_s.at[number, b], ag_r.at[number, b]
        )

    sums1 = [sum_of(b, part1, into1, 0) for b in range(2)]
    sums2 = [sum_of(b, part2, into2, 1) for b in range(2)]
    gather1 = [gather_of(b, n2, 0) for b in range(2)]
    gather2 = [gather_of(b, dhb, 1) for b in range(2)]

    def project(b):
        back_to_mirror(b).wait_recv()
        mine = pl.ds(b * rows, rows)
        part1[mine, :] = dot_nn(ob[mine, :], wo[...]).astype(bf16)
        sums1[b].start()

    attention(0, 1)
    back_to_mirror(0).start()
    attention(0, 0)
    loads[0].wait()
    project(0)
    attention(1, 1)
    back_to_mirror(1).start()
    attention(1, 0)
    project(1)
    sums1[0].relay(adder(0, part1, into1))
    loads[2].wait()

    def grad_middle(j, carry):
        da[:, tile(j, span)] = dot_nt(dyb[...], wd[tile(j, span), :])
        return carry

    lax.fori_loop(0, units // span, grad_middle, 0)
    sums1[1].relay(adder(1, part1, into1))
    gain2 = gains_ref[1:2, :].astype(f32)
    gain_ref[...] = jnp.zeros(gain_ref.shape, f32)

    def second_norm(b):
        sums1[b].arrive()
        hidden = tok_ref[mine_in(b), :].astype(f32) + total_of(b, part1, into1)
        hidden_ref[b] = hidden
        n2[mine_in(b), :] = (hidden * inverse_rms(hidden) * gain2).astype(bf16)
        gather1[b].start()

    second_norm(0)
    second_norm(1)
    loads[3].wait()
    gather1[0].relay()
    gather1[1].relay()

    def feed(b):
        gather1[b].arrive()
        mine = pl.ds(b * rows, rows)

        def gate_up(j, carry):
            columns = tile(j, span)
            gate = dot_nn(n2[mine, :], wgu[0, :, columns])
            up = dot_nn(n2[mine, :], wgu[1, :, columns])
            sigmoid = jax.nn.sigmoid(gate)
            activated = gate * sigmoid
            mixed_ref[mine, columns] = (activated * up).astype(bf16)
            grad = da[mine, columns]
            dgu[0, mine, columns] = (
                grad * up * sigmoid * (1.0 + gate * (1.0 - sigmoid))
            ).astype(bf16)
            dgu[1, mine, columns] = (grad * activated).astype(bf16)
            return carry

        lax.fori_loop(0, units // span, gate_up, 0)

        def grad_norm_two(c, carry):
            columns = tile(c, 512)
            part2[mine, columns] = (
                dot_nt(dgu[0, mine, :], wgu[0, columns, :]) + dot_nt(dgu[1, mine, :], wgu[1, columns, :])
            ).astype(bf16)
            return carry

        lax.fori_loop(0, width // 512, grad_norm_two, 0)
        sums2[b].start()

    feed(0)
    feed(1)
    wide_share = width // 16
    mates = [
        MateSum(
            lambda w, i=i: wgu.at[i, tile(w, wide_share), :],
            lambda k, i=i: wgu.at[i, tile(2 * k + core, wide_share), :],
            lambda k, i=i: mate_gu.at[i, k], mt_s.at[i], mt_r.at[i],
        )
        for i in range(2)
    ]
    mates.append(
        MateSum(
            lambda w: gdn.at[w], lambda k: gdn.at[2 * k + core], lambda k: mate_d.at[k],
            mt_s.at[2], mt_r.at[2],
        )
    )
    gate = Item(wide, mates[0].own, igate, it_s.at[0], it_r.at[0], mates[0])
    down = Item(wide, mates[2].own, idown, it_s.at[1], it_r.at[1], mates[2])

    def grad_down(j, carry):
        found = dot_tn(mixed_ref[:, tile(j, span)], dyb[...]).astype(bf16)
        for w in range(16):
            gdn[w, tile(j, span), :] = found[:, w * wide_share : (w + 1) * wide_share]
        return carry

    def grad_gateup(which):
        def per_tile(j, carry):
            wgu[which, tile(j, span), :] = dot_tn(n2[:, tile(j, span)], dgu[which]).astype(bf16)
            return carry

        lax.fori_loop(0, width // span, per_tile, 0)

    def second_norm_back(b):
        sums2[b].arrive()
        total = total_of(b, part2, into2)
        hidden = hidden_ref[b]
        inverse = inverse_rms(hidden)
        z2 = hidden * inverse
        gain_ref[pl.ds(b, 1), :] = jnp.sum(total * z2, axis=0, keepdims=True)
        weighted = total * gain2
        dh = dyb[mine_in(b), :].astype(f32) + inverse * (
            weighted - z2 * jnp.mean(weighted * z2, axis=-1, keepdims=True)
        )
        dh_ref[b] = dh
        dhb[mine_in(b), :] = dh.astype(bf16)
        gather2[b].start()

    lax.fori_loop(0, units // span, grad_down, 0)
    mates[2].start()
    sums2[0].relay(adder(0, part2, into2))
    grad_gateup(0)
    mates[0].start()
    sums2[1].relay(adder(1, part2, into2))
    second_norm_back(0)
    mates[2].add()
    down.tree.start()
    second_norm_back(1)
    mates[0].add()
    gate.tree.start()
    gather2[0].relay()
    grad_gateup(1)
    mates[1].start()
    gather2[1].relay()
    down.relay()
    for b in range(2):
        gather2[b].arrive()
        mine = pl.ds(b * rows, rows)
        dob_ref[mine, :] = dot_nt(dhb[mine, :], wo[...]).astype(bf16)

    def grad_out(j, carry):
        gout_ref[:, tile(j, span)] = dot_tn(ob[...], dhb[:, tile(j, span)]).astype(bf16)
        return carry

    lax.fori_loop(0, width // span, grad_out, 0)
    gate.relay()
    mates[1].add()

    def kept(k):
        return pltpu.make_async_copy(mates[1].own(k), pup_hbm.at[k], st_sem.at[k])

    def keep(k, carry):
        kept(k).start()
        return carry

    lax.fori_loop(0, 8, keep, 0)
    squares = down.finish(down_ref) + gate.finish(gate_ref)
    squares_ref[...] = jnp.broadcast_to(squares, squares_ref.shape)
    for b in range(2):
        sums1[b].drain()
        sums2[b].drain()
        gather1[b].drain()
        gather2[b].drain()
        queries[b].wait_send()
        back_to_mirror(b).wait_send()
    keys.drain()
    for i in range(7):
        to_mate(relayed[i], i).wait_send()
    to_mate(chip, 7).wait_send()
    gate.drain()
    down.drain()
    mates[1].drain()
    store_n1.wait()
    store_kv.wait()

    def per_store(k, carry):
        kept(k).wait()
        return carry

    lax.fori_loop(0, 8, per_store, 0)


def forward(lengths, tokens, gains, wq, wkv, cosine, sine, wo, wgu, wd, cotangent):
    count, width = tokens.shape
    rows = count // 2
    share = rows // 8
    units = wd.shape[0]
    lanes = wq.shape[1]
    heads = lanes // HD
    stack = heads * rows // 2
    wide_count = 16
    wide_share = width // wide_count
    here = pl.BlockSpec(memory_space=pltpu.VMEM)
    anywhere = pl.BlockSpec(memory_space=pl.ANY)
    shape = jax.ShapeDtypeStruct
    dma = pltpu.SemaphoreType.DMA
    vmem = pltpu.VMEM
    return pl.pallas_call(
        forward_kernel,
        out_shape=(
            shape((count, width), bf16),
            shape((wide_count, count, 2 * HD), bf16),
            shape((2, 2, stack, 2 * HD), bf16),
            shape((2, 2, stack, 2 * HD), f32),
            shape((8, stack), f32),
            shape((2, share, width), f32),
            shape((count, units), bf16),
            shape((2, share, width), f32),
            shape((8, width), f32),
            shape((count, lanes), bf16),
            shape((lanes, width), bf16),
            shape((wide_share, units), f32),
            shape((units, wide_share), f32),
            shape((8, wide_share), f32),
            shape((8, wide_share, units), bf16),
        ),
        in_specs=[pl.BlockSpec(memory_space=pltpu.SMEM)] + [here] * 6 + [anywhere] * 4,
        out_specs=(anywhere, anywhere) + (here,) * 12 + (anywhere,),
        scratch_shapes=[
            vmem(wo.shape, bf16),
            vmem(wgu.shape, bf16),
            vmem(wd.shape, bf16),
            vmem((count, width), bf16),
            vmem((count, width), bf16),
            vmem((wide_count, count, 2 * HD), bf16),
            vmem((count, lanes), bf16),
            vmem((2, rows // 2, lanes), bf16),
            vmem((count, lanes), bf16),
            vmem((2, rows // 2, lanes), bf16),
            vmem((count, units), f32),
            vmem((count, width), bf16),
            vmem((2, count, units), bf16),
            vmem((count, width), bf16),
            vmem((count, width), bf16),
            vmem((count, width), bf16),
            vmem((2, SLOTS, share, width), bf16),
            vmem((2, SLOTS, share, width), bf16),
            vmem((2, 8, wide_share, units), bf16),
            vmem((8, units, wide_share), bf16),
            vmem((wide_count, units, wide_share), bf16),
            vmem((SLOTS, wide_share, units), bf16),
            vmem((SLOTS, units, wide_share), bf16),
            dma((4,)),
            dma((2,)),
            dma((8,)),
            dma((SLOTS,)),
            dma((SLOTS,)),
            dma((8,)),
            dma((8,)),
            dma((2, 2)),
            dma((2, 2)),
            dma((2, 2, SLOTS)),
            dma((2, 2, SLOTS)),
            dma((2, 2, SLOTS)),
            dma((2, 2, SLOTS)),
            dma((3, 8)),
            dma((3, 8)),
            dma((2, SLOTS)),
            dma((2, SLOTS)),
        ],
        compiler_params=pltpu.CompilerParams(
            collective_id=1, has_side_effects=True, vmem_limit_bytes=63 * MB
        ),
        name="forward",
    )(lengths, tokens, gains, wq, wkv, cosine, sine, wo, wgu, wd, cotangent)


def backward_kernel(
    len_ref, tok_hbm, gains_ref, wq_ref, wkv_ref, cos_ref, sin_ref,
    qs_ref, os_ref, log_ref, hidden_ref, mixed_ref, dh_ref, gain2_ref, dob_ref, gout_ref,
    squares_ref, kv_hbm, n1_hbm, wd_hbm, pup_hbm,
    layer_ref, grad_ref, q_ref, pair_ref, out_ref, up_ref, gains_out_ref, norm_ref,
    kv, n1, wd, tok, pup, pout, pq, pkv, iup, iout, iq, ikv,
    mout, mq, mkv, gq, gkv, part3, part4, into3, into4, acc, dkv, dkm, dkin, dkv_low, dq, dqm, dm,
    dos, qclean, delta, dqacc, gpart, gin, near_own, near, norm_own, norm_in, pair,
    ld_sem, rs_s, rs_r, ag_s, ag_r, dm_s, dm_r, dt_s, dt_r, im_s, im_r, it_s, it_r, ex_s, ex_r,
    g_s, g_r, h_s, h_r, w_s, w_r,
):
    narrow, wide = Grid("narrow"), Grid("wide")
    me, wide_me = narrow.narrow_me, narrow.wide_me
    core = wide.core
    chip = lax.div(wide_me, 2)
    last_chip = lax.axis_size("wide") // 2 - 1
    peers = lax.axis_size("narrow")
    mate, mirror = mate_of(), mirror_of()
    tokens, width = layer_ref.shape
    rows = tokens // 2
    half = rows // 2
    share = rows // peers
    heads = wq_ref.shape[1] // HD
    span = 256
    wide_share = width // 16

    def mine_in(b):
        return pl.ds(pl.multiple_of(b * rows + me * share, share), share)

    def later(b):
        return pl.ds(b * rows + half, half)

    moves = (
        (kv_hbm, kv), (wd_hbm, wd), (pup_hbm, pup), (n1_hbm, n1),
        (tok_hbm.at[mine_in(0), :], tok.at[0]), (tok_hbm.at[mine_in(1), :], tok.at[1]),
    )
    loads = [pltpu.make_async_copy(src, dst, ld_sem.at[i]) for i, (src, dst) in enumerate(moves)]
    for load in loads:
        load.start()
    greet(others_of("narrow") + others_of("wide"))

    grads_there = [
        remote(dob_ref.at[later(b), :], dm.at[b], ex_s.at[0, b], ex_r.at[0, b], mirror) for b in range(2)
    ]
    for copy in grads_there:
        copy.start()

    def mates_of(source, own, into, number):
        return MateSum(
            source, lambda k: own.at[k], lambda k: into.at[k], im_s.at[number], im_r.at[number]
        )

    up = Item(wide, lambda b: pup.at[b], iup, it_s.at[0], it_r.at[0])
    out = Item(
        wide, lambda b: pout.at[b], iout, it_s.at[1], it_r.at[1],
        mates_of(lambda w: gout_ref.at[:, tile(w, wide_share)], pout, mout, 0),
    )
    query = Item(
        wide, lambda b: pq.at[b], iq, it_s.at[2], it_r.at[2],
        mates_of(lambda w: gq.at[tile(w, wide_share), :], pq, mq, 1),
    )
    keyval = Item(
        wide, lambda b: pkv.at[b], ikv, it_s.at[3], it_r.at[3],
        mates_of(lambda w: gkv.at[tile(w, wide_share), :], pkv, mkv, 2),
    )
    out.mates.start()

    def their_rows(b):
        return lambda block: pl.ds(pl.multiple_of(b * rows + block * share, share), share)

    def sum_of(b, part, into, number):
        where = their_rows(b)
        return TreeSum(
            narrow, lambda block: part.at[where(block), :], lambda slot: into.at[b, slot],
            rs_s.at[number, b], rs_r.at[number, b],
        )

    def adder(b, part, into):
        where = their_rows(b)
        return block_adder(lambda block: part.at[where(block), :], lambda slot: into.at[b, slot])

    def total_of(b, part, into):
        total = part[mine_in(b), :].astype(f32)
        for slot in (3, 4, 5, 6):
            total = total + into[b, slot].astype(f32)
        return total

    def gather_of(b, buffer, number):
        where = their_rows(b)
        return TreeGather(
            narrow, lambda block: buffer.at[where(block), :], ag_s.at[number, b], ag_r.at[number, b]
        )

    sums3 = [sum_of(b, part3, into3, 0) for b in range(2)]
    sums4 = [sum_of(b, part4, into4, 1) for b in range(2)]
    gather3 = [gather_of(b, layer_ref, 0) for b in range(2)]
    gather4 = [gather_of(b, grad_ref, 1) for b in range(2)]

    loads[1].wait()
    for b in range(2):
        mine = pl.ds(b * rows, rows)

        def feed(c, carry):
            part3[mine, tile(c, 512)] = dot_nn(mixed_ref[mine, :], wd[:, tile(c, 512)]).astype(bf16)
            return carry

        lax.fori_loop(0, width // 512, feed, 0)
        sums3[b].start()
    loads[2].wait()
    up.tree.start()
    loads[0].wait()
    stack_rows = heads * half
    parts = 2
    part_rows = stack_rows // parts

    def attention(b, g):
        length = len_ref[b]
        final = chip if g == 0 else last_chip - chip
        first = wide_me * rows if g == 0 else (2 * last_chip + 1 - wide_me) * rows + half
        held = (dob_ref[pl.ds(b * rows, half), :] if g == 0 else dm[b]).astype(f32)
        stack = head_stack(held, heads, True)
        dos[...] = stack.astype(bf16)
        for p in range(parts):
            at = pl.ds(p * part_rows, part_rows)
            product = stack[p * part_rows : (p + 1) * part_rows] * os_ref[b, g, at, :]
            delta[:, at] = jnp.sum(jnp.transpose(product), axis=0, keepdims=True)
        lane = lax.broadcasted_iota(jnp.int32, qclean.shape, 1)
        qclean[...] = jnp.where(lane < HD, qs_ref[b, g].astype(f32), 0.0).astype(bf16)
        dqacc[...] = jnp.zeros(dqacc.shape, f32)

        def step(masked, j, carry):
            block, scored = key_block(kv, j, b, length)
            if masked:
                shape = (2 * rows, part_rows)
                key = 2 * rows * j + lax.broadcasted_iota(jnp.int32, shape, 0)
                place = first + lax.rem(lax.broadcasted_iota(jnp.int32, shape, 1), half)
                allowed = key <= place
            total = acc[j]
            for p in range(parts):
                at = pl.ds(p * part_rows, part_rows)
                scores = dot_nt(scored, qs_ref[b, g, at, :])
                if masked:
                    scores = jnp.where(allowed, scores, masked_score)
                chances = jnp.exp(scores - log_ref[pl.ds(2 * b + g, 1), at])
                slope = (chances * (dot_nt(block, dos[at, :]) - delta[:, at])).astype(bf16)
                total = total + dot_nn(slope, qclean[at, :]) + dot_nn(chances.astype(bf16), dos[at, :])
                dqacc[at, :] = dqacc[at, :] + dot_tn(slope, block)
            acc[j] = total
            return carry

        lax.fori_loop(0, final, functools.partial(step, False), 0)
        step(True, final, 0)
        for pair in range(heads // 2):
            even = dqacc[pl.ds(2 * pair * half, half), :]
            odd = dqacc[pl.ds((2 * pair + 1) * half, half), :]
            value = pair_lanes(even, odd) * HD**-0.5
            table = pl.ds(0, half) if g == 0 else pl.ds(rows, half)
            value = (value * cos_ref[table, :] - swap_halves(value) * sin_ref[table, :]).astype(bf16)
            columns = pl.ds(pair * 2 * HD, 2 * HD)
            if g == 0:
                dq[pl.ds(b * rows, half), columns] = value
            else:
                dqm[b, :, columns] = value

    def query_back(b):
        return remote(dqm.at[b], dq.at[later(b), :], ex_s.at[1, b], ex_r.at[1, b], mirror)

    def clear():
        def per_block(j, carry):
            acc[j] = jnp.zeros(acc.shape[1:], f32)
            return carry

        lax.fori_loop(0, acc.shape[0], per_block, 0)

    pair_mates = [
        MateSum(
            lambda w, b=b: dkv.at[b, w], lambda k, b=b: dkv.at[b, 2 * k + core],
            lambda k, b=b: dkm.at[b, k], dm_s.at[b], dm_r.at[b],
        )
        for b in range(2)
    ]
    pair_trees = [
        TreeSum(
            wide, lambda block, b=b: dkv.at[b, 2 * block + core], lambda slot, b=b: dkin.at[b, slot],
            dt_s.at[b], dt_r.at[b],
        )
        for b in range(2)
    ]

    def pair_relay(b):
        pair_trees[b].relay(
            block_adder(lambda block: dkv.at[b, 2 * block + core], lambda slot: dkin.at[b, slot])
        )

    def pair_send(b):
        def per_block(j, carry):
            dkv[b, pl.ds(2 * j, 2)] = acc[j].astype(bf16).reshape(2, rows, 2 * HD)
            return carry

        lax.fori_loop(0, acc.shape[0], per_block, 0)
        pair_mates[b].start()

    def pair_mid(b):
        pair_mates[b].add()
        pair_trees[b].start()

    def pair_total(b):
        pair_trees[b].arrive()
        total = dkv[b, wide_me].astype(f32)
        for slot in (3, 4, 5, 6):
            total = total + dkin[b, slot].astype(f32)
        mine = pl.ds(b * rows, rows)
        lane = lax.broadcasted_iota(jnp.int32, total.shape, 1)
        table = pl.ds(0, rows)
        turned = total * cos_ref[table, :] - swap_halves(total) * sin_ref[table, :]
        dkv_low[mine, :] = jnp.where(lane < HD, turned, total).astype(bf16)

    def norm_one_back(b):
        mine = pl.ds(b * rows, rows)

        def per_chunk(c, carry):
            columns = tile(c, 512)
            part4[mine, columns] = (
                dot_nt(dq[mine, :], wq_ref[columns, :]) + dot_nn(dkv_low[mine, :], wkv_ref[:, columns])
            ).astype(bf16)
            return carry

        lax.fori_loop(0, width // 512, per_chunk, 0)
        sums4[b].start()

    def result_rows(b):
        sums3[b].arrive()
        layer_ref[mine_in(b), :] = (hidden_ref[b] + total_of(b, part3, into3)).astype(bf16)
        gather3[b].start()

    gains1 = gains_ref[0:1, :].astype(f32)

    def input_rows(b):
        sums4[b].arrive()
        total = total_of(b, part4, into4)
        values = tok[b].astype(f32)
        inverse = inverse_rms(values)
        z1 = values * inverse
        weighted = total * gains1
        grad_ref[mine_in(b), :] = (
            dh_ref[b] + inverse * (weighted - z1 * jnp.mean(weighted * z1, axis=-1, keepdims=True))
        ).astype(bf16)
        gather4[b].start()
        return jnp.sum(total * z1, axis=0, keepdims=True)

    clear()
    for copy in grads_there:
        copy.wait_recv()
    attention(0, 1)
    query_back(0).start()
    attention(0, 0)
    pair_send(0)
    sums3[0].relay(adder(0, part3, into3))
    sums3[1].relay(adder(1, part3, into3))
    clear()
    attention(1, 1)
    query_back(1).start()
    pair_mid(0)
    result_rows(0)
    result_rows(1)
    attention(1, 0)
    pair_send(1)
    pair_relay(0)
    pair_mid(1)
    pair_total(0)
    query_back(0).wait_recv()
    norm_one_back(0)
    gather3[0].relay()
    gather3[1].relay()
    query_back(1).wait_recv()
    loads[3].wait()

    def grad_query(j, carry):
        gq[tile(j, span), :] = dot_tn(n1[:, tile(j, span)], dq[...]).astype(bf16)
        return carry

    pair_relay(1)
    lax.fori_loop(0, width // span, grad_query, 0)
    query.mates.start()
    sums4[0].relay(adder(0, part4, into4))
    pair_total(1)
    norm_one_back(1)

    def grad_keyval(j, carry):
        gkv[tile(j, span), :] = dot_tn(n1[:, tile(j, span)], dkv_low[...]).astype(bf16)
        return carry

    query.mates.add()
    query.tree.start()
    out.mates.add()
    out.tree.start()
    lax.fori_loop(0, width // span, grad_keyval, 0)
    keyval.mates.start()
    up.relay()
    loads[4].wait()
    loads[5].wait()
    gain1 = input_rows(0)
    keyval.mates.add()
    keyval.tree.start()
    sums4[1].relay(adder(1, part4, into4))
    query.relay()
    out.relay()
    gather4[0].relay()
    keyval.relay()
    squares = squares_ref[0:1, 0:1] + up.finish(up_ref)
    gain1 = gain1 + input_rows(1)

    row = lax.broadcasted_iota(jnp.int32, gpart.shape, 0)
    gain2 = gain2_ref[0:1, :] + gain2_ref[1:2, :]
    gpart[...] = jnp.where(row == 0, gain1, jnp.where(row == 1, gain2, 0.0))
    gain_copies = [
        remote(gpart.at[:, tile(there[0], wide_share)], gin.at[i], g_s.at[i], g_r.at[i], there)
        for i, there in enumerate(others_of("wide"))
    ]
    for copy in gain_copies:
        copy.start()
    squares = squares + query.finish(q_ref) + out.finish(out_ref)
    share_kv = keyval.finish(pair)
    pair_ref[...] = jnp.transpose(pair[...])
    squares = squares + share_kv
    gather4[1].relay()
    for copy in gain_copies:
        copy.wait()
    total = gpart[:, tile(wide_me, wide_share)]
    for i in range(len(gain_copies)):
        total = total + gin[i]
    row = lax.broadcasted_iota(jnp.int32, total.shape, 0)
    near_own[...] = jnp.where(row < 2, total, jnp.broadcast_to(squares, total.shape))
    exchange(lambda index: near_own, near, "narrow", h_s, h_r)
    total = near_own[...]
    for i in range(peers - 1):
        total = total + near[i]
    gains_out_ref[...] = total
    kept = jnp.where(row < 2, total, 0.0)
    gain_squares = jnp.sum(jnp.sum(kept * kept, axis=1, keepdims=True), axis=0, keepdims=True)
    norm_own[...] = total[2:3, :] + jnp.broadcast_to(gain_squares, norm_own.shape)
    exchange(lambda index: norm_own, norm_in, "wide", w_s, w_r)
    total = norm_own[...]
    for i in range(len(gain_copies)):
        total = total + norm_in[i]
    norm_ref[...] = jnp.sqrt(total)
    for b in range(2):
        gather3[b].arrive()
        gather4[b].arrive()
        for each in (sums3[b], sums4[b], gather3[b], gather4[b], pair_mates[b], pair_trees[b]):
            each.drain()
        grads_there[b].wait_send()
        query_back(b).wait_send()
    for item in (up, out, query, keyval):
        item.drain()


def backward(
    lengths, tokens, gains, wq, wkv, cosine, sine, qs, outs, logs, hidden, mixed, dh, gain2,
    dob, gout, squares, kv, n1, wd, pup,
):
    count, width = n1.shape
    rows = count // 2
    share = rows // 8
    units = wd.shape[0]
    lanes = wq.shape[1]
    stack = qs.shape[2]
    wide_count = 16
    wide_share = width // wide_count
    here = pl.BlockSpec(memory_space=pltpu.VMEM)
    anywhere = pl.BlockSpec(memory_space=pl.ANY)
    shape = jax.ShapeDtypeStruct
    dma = pltpu.SemaphoreType.DMA
    vmem = pltpu.VMEM
    blocks = (
        (wide_share, units), (lanes, wide_share),
        (wide_share, lanes), (wide_share, 2 * HD),
    )
    return pl.pallas_call(
        backward_kernel,
        out_shape=(
            shape((count, width), bf16),
            shape((count, width), bf16),
            shape((wide_share, lanes), f32),
            shape((2 * HD, wide_share), f32),
            shape((lanes, wide_share), f32),
            shape((wide_share, units), f32),
            shape((8, wide_share), f32),
            shape((8, wide_share), f32),
        ),
        in_specs=[pl.BlockSpec(memory_space=pltpu.SMEM), anywhere] + [here] * 15 + [anywhere] * 4,
        out_specs=(here,) * 8,
        scratch_shapes=[
            vmem(kv.shape, bf16),
            vmem((count, width), bf16),
            vmem(wd.shape, bf16),
            vmem((2, share, width), bf16),
            *[vmem((8, *block), bf16) for block in blocks],
            *[vmem((SLOTS, *block), bf16) for block in blocks],
            *[vmem((8, *block), bf16) for block in blocks[1:]],
            vmem((width, lanes), bf16),
            vmem((width, 2 * HD), bf16),
            vmem((count, width), bf16),
            vmem((count, width), bf16),
            vmem((2, SLOTS, share, width), bf16),
            vmem((2, SLOTS, share, width), bf16),
            vmem((8, 2 * rows, 2 * HD), f32),
            vmem((2, wide_count, rows, 2 * HD), bf16),
            vmem((2, 8, rows, 2 * HD), bf16),
            vmem((2, SLOTS, rows, 2 * HD), bf16),
            vmem((count, 2 * HD), bf16),
            vmem((count, lanes), bf16),
            vmem((2, rows // 2, lanes), bf16),
            vmem((2, rows // 2, lanes), bf16),
            vmem((stack, 2 * HD), bf16),
            vmem((stack, 2 * HD), bf16),
            vmem((1, stack), f32),
            vmem((stack, 2 * HD), f32),
            vmem((8, width), f32),
            vmem((wide_count - 1, 8, wide_share), f32),
            vmem((8, wide_share), f32),
            vmem((7, 8, wide_share), f32),
            vmem((8, wide_share), f32),
            vmem((wide_count - 1, 8, wide_share), f32),
            vmem((wide_share, 2 * HD), f32),
            dma((6,)),
            dma((2, 2, SLOTS)),
            dma((2, 2, SLOTS)),
            dma((2, 2, SLOTS)),
            dma((2, 2, SLOTS)),
            dma((2, 8)),
            dma((2, 8)),
            dma((2, SLOTS)),
            dma((2, SLOTS)),
            dma((3, 8)),
            dma((3, 8)),
            dma((4, SLOTS)),
            dma((4, SLOTS)),
            dma((2, 2)),
            dma((2, 2)),
            dma((wide_count - 1,)),
            dma((wide_count - 1,)),
            dma((7,)),
            dma((7,)),
            dma((wide_count - 1,)),
            dma((wide_count - 1,)),
        ],
        compiler_params=pltpu.CompilerParams(
            collective_id=2, has_side_effects=True, vmem_limit_bytes=63 * MB
        ),
        name="backward",
    )(
        lengths, tokens, gains, wq, wkv, cosine, sine, qs, outs, logs, hidden, mixed, dh,
        gain2, dob, gout, squares, kv, n1, wd, pup,
    )


def update_kernel(
    norm_ref, gains_sum_ref, gains_ref, gains_first_ref, gains_second_ref, *refs
):
    count = 6
    grads, weights, firsts, seconds = (refs[i * count : (i + 1) * count] for i in range(4))
    refs = refs[4 * count :]
    (layer, grad), refs = refs[:2], refs[2:]
    outs, refs = [refs[i * count : (i + 1) * count] for i in range(4)], refs[4 * count :]
    (layer_out, grad_out), refs = refs[:2], refs[2:]
    gain_outs, refs = refs[:4], refs[4:]
    held, refs = [refs[i * count : (i + 1) * count] for i in range(5)], refs[5 * count :]
    rows_held, in_sem, out_sem, copy_sem = refs
    wide_me = lax.axis_index("wide")
    at = tile(wide_me, 128)
    slices = (
        lambda ref: ref.at[:, at], lambda ref: ref.at[0, at, :], lambda ref: ref.at[1, at, :],
        lambda ref: ref.at[:, at], lambda ref: ref.at[at, :], lambda ref: ref.at[:, at],
    )
    halves = (None, 0, 1, None, None, None)
    loads, stores = [], []
    for i in range(count):
        def whole(ref):
            return ref if halves[i] is None else ref.at[halves[i]]

        sources = (grads[i], slices[i](weights[i]), whole(firsts[i]), whole(seconds[i]))
        loads.append(
            [pltpu.make_async_copy(src, held[n][i], in_sem.at[n, i]) for n, src in enumerate(sources)]
        )
        targets = (
            (held[0][i], outs[0][i]), (held[2][i], outs[1][i]), (held[3][i], outs[2][i]),
            (held[4][i], outs[3][i]),
        )
        stores.append(
            [
                pltpu.make_async_copy(src, whole(dst), out_sem.at[n, i])
                for n, (src, dst) in enumerate(targets)
            ]
        )
    for group in loads:
        for load in group:
            load.start()
    moved_in = [
        pltpu.make_async_copy(src, rows_held.at[n], copy_sem.at[n]) for n, src in enumerate((layer, grad))
    ]
    moved_out = [
        pltpu.make_async_copy(rows_held.at[n], dst, copy_sem.at[2 + n])
        for n, dst in enumerate((layer_out, grad_out))
    ]
    for copy in moved_in:
        copy.start()
    factor = jnp.minimum(1.0, clip_limit / (norm_ref[0:1, 0:1] + 1e-06))

    for i in range(count):
        for load in loads[i]:
            load.wait()
        height, breadth = held[0][i].shape
        span = max(8, min(height, 16384 // breadth))

        def step(j, carry):
            rows = tile(j, span)
            clipped = held[0][i][rows, :] * factor
            updated, momentum, variance = adam_update(
                held[1][i][rows, :].astype(f32), clipped, held[2][i][rows, :], held[3][i][rows, :],
                learn_rate, decay_rate,
            )
            held[0][i][rows, :] = clipped
            held[2][i][rows, :] = momentum
            held[3][i][rows, :] = variance
            held[4][i][rows, :] = updated
            return carry

        lax.fori_loop(0, height // span, step, 0)
        for store in stores[i]:
            store.start()
    for before, after in zip(moved_in, moved_out):
        before.wait()
        after.start()
    clipped = gains_sum_ref[0:2, :] * factor
    updated, momentum, variance = adam_update(
        gains_ref[:, at].astype(f32), clipped, gains_first_ref[...], gains_second_ref[...], gain_rate, 0.0
    )
    for ref, value in zip(gain_outs, (clipped, momentum, variance, updated)):
        ref[...] = value
    for group in stores:
        for store in group:
            store.wait()
    for copy in moved_out:
        copy.wait()


def update(norm, gains_sum, gains, gains_first, gains_second, grads, weights, firsts, seconds, layer, grad):
    here = pl.BlockSpec(memory_space=pltpu.VMEM)
    anywhere = pl.BlockSpec(memory_space=pl.ANY)
    shape = jax.ShapeDtypeStruct
    like = [shape(first.shape, f32) for first in firsts]
    kept = [like[0], like[1], like[3], like[4], like[5]]
    blocks = [grad_part.shape for grad_part in grads]
    small = shape(gains_first.shape, f32)
    dma = pltpu.SemaphoreType.DMA

    def body(*refs):
        head, rest = refs[:5], refs[5:]
        ins, rest = rest[:6], rest[6:]
        groups = []
        for _ in range(3):
            down, gateup, out, query, keyval = rest[:5]
            groups += [down, gateup, gateup, out, query, keyval]
            rest = rest[5:]
        moved, rest = rest[:2], rest[2:]
        outs = []
        for _ in range(4):
            down, gateup, out, query, keyval = rest[:5]
            outs += [down, gateup, gateup, out, query, keyval]
            rest = rest[5:]
        update_kernel(*head, *ins, *groups, *moved, *outs, *rest)

    def five(arrays):
        return [arrays[0], arrays[1], arrays[3], arrays[4], arrays[5]]

    return pl.pallas_call(
        body,
        out_shape=tuple(kept * 4 + [shape(layer.shape, bf16), shape(grad.shape, bf16)] + [small] * 4),
        in_specs=[here] * 5 + [anywhere] * 23,
        out_specs=tuple([anywhere] * 22 + [here] * 4),
        scratch_shapes=[
            *[pltpu.VMEM(block, f32) for block in blocks],
            *[pltpu.VMEM(block, bf16) for block in blocks],
            *[pltpu.VMEM(block, f32) for block in blocks * 3],
            pltpu.VMEM((2, *layer.shape), bf16),
            dma((4, 6)),
            dma((4, 6)),
            dma((4,)),
        ],
        compiler_params=pltpu.CompilerParams(vmem_limit_bytes=63 * MB),
        name="update",
    )(
        norm, gains_sum, gains, gains_first, gains_second, *grads, *five(weights), *five(firsts),
        *five(seconds), layer, grad,
    )


def shards(
    tokens,
    cotangent,
    lengths,
    query_weight,
    keyval_weight,
    output_weight,
    gateup_weight,
    down_weight,
    norm_gains,
    query_first,
    keyval_first,
    output_first,
    gateup_first,
    down_first,
    gains_first,
    query_second,
    keyval_second,
    output_second,
    gateup_second,
    down_second,
    gains_second,
):
    bucket_count, row_count, model_width = tokens.shape
    wide_count = lax.axis_size("wide")
    wide_rank = lax.axis_index("wide")
    token_count = bucket_count * row_count
    half = row_count // 2
    mirror_rank = wide_count - 1 - wide_rank
    positions = jnp.concatenate(
        [
            wide_rank * row_count + jnp.arange(row_count, dtype=jnp.int32),
            mirror_rank * row_count + half + jnp.arange(half, dtype=jnp.int32),
        ]
    )
    cosine, sine = lane_tables(positions)
    inputs = tokens.reshape(token_count, model_width)
    units = down_weight.shape[0]

    def turned(values):
        return values.transpose(0, 2, 1).reshape(2 * HD, -1)

    def turned_back(values):
        return values.reshape(2, HD, -1).transpose(0, 2, 1)

    pair_weight = turned(keyval_weight)
    (
        normed_one, pairs, query_stack, out_stack, logs, hidden, mixed, grad_hidden, gain_two, grad_heads,
        output_grad, gate_sum, down_sum, squares, up_part,
    ) = forward(
        lengths, inputs, norm_gains, query_weight, pair_weight, cosine, sine, output_weight,
        gateup_weight, down_weight, cotangent.reshape(token_count, model_width),
    )
    layer_rows, grad_rows, query_sum, pair_sum, output_sum, up_sum, gains_sum, norm = backward(
        lengths, inputs, norm_gains, query_weight, pair_weight, cosine, sine, query_stack, out_stack,
        logs, hidden, mixed, grad_hidden, gain_two, grad_heads, output_grad, squares, pairs, normed_one,
        down_weight, up_part,
    )
    results = update(
        norm, gains_sum, norm_gains, gains_first, gains_second,
        (down_sum, gate_sum, up_sum, output_sum, query_sum, pair_sum),
        (down_weight, gateup_weight, gateup_weight, output_weight, query_weight, pair_weight),
        (down_first, gateup_first, gateup_first, output_first, query_first, turned(keyval_first)),
        (down_second, gateup_second, gateup_second, output_second, query_second, turned(keyval_second)),
        layer_rows, grad_rows,
    )
    layer_out = results[20].reshape(bucket_count, row_count, model_width)
    input_grad = results[21].reshape(bucket_count, row_count, model_width)
    kinds = []
    for kind in range(4):
        down, gateup, output, query, pair = results[5 * kind : 5 * kind + 5]
        kinds.append((query, turned_back(pair), output, gateup, down, results[22 + kind]))
    clipped, momentum, variance, updated = kinds
    return (
        layer_out, input_grad, *clipped, norm[0, 0], *momentum, *variance, *updated,
    )


def solution(mesh):
    return jax.shard_map(
        shards,
        mesh=mesh,
        in_specs=(
            P(None, "wide", None),
            P(None, "wide", None),
            P(),
            P(None, "narrow"),
            P(None, None, "narrow"),
            P("narrow", None),
            P(None, None, "narrow"),
            P("narrow", None),
            P(),
            P("wide", "narrow"),
            P(None, "wide", "narrow"),
            P("narrow", "wide"),
            P(None, "wide", "narrow"),
            P("narrow", "wide"),
            P(None, "wide"),
            P("wide", "narrow"),
            P(None, "wide", "narrow"),
            P("narrow", "wide"),
            P(None, "wide", "narrow"),
            P("narrow", "wide"),
            P(None, "wide"),
        ),
        out_specs=(
            P(None, "wide", None),
            P(None, "wide", None),
            P("wide", "narrow"),
            P(None, "wide", "narrow"),
            P("narrow", "wide"),
            P(None, "wide", "narrow"),
            P("narrow", "wide"),
            P(None, "wide"),
            P(),
            P("wide", "narrow"),
            P(None, "wide", "narrow"),
            P("narrow", "wide"),
            P(None, "wide", "narrow"),
            P("narrow", "wide"),
            P(None, "wide"),
            P("wide", "narrow"),
            P(None, "wide", "narrow"),
            P("narrow", "wide"),
            P(None, "wide", "narrow"),
            P("narrow", "wide"),
            P(None, "wide"),
            P("wide", "narrow"),
            P(None, "wide", "narrow"),
            P("narrow", "wide"),
            P(None, "wide", "narrow"),
            P("narrow", "wide"),
            P(None, "wide"),
        ),
        check_vma=False,
    )
```

```python
import functools
import math

import jax
import jax.numpy as jnp
import numpy as np
from jax import lax
from jax.experimental import pallas as pl
from jax.experimental.pallas import tpu as pltpu
from jax.sharding import PartitionSpec as P

HD = 64
STEP = 10


norm_eps = 1e-05
rope_theta = 500000.0
rope_factor = 32.0
rope_low = 1.0
rope_high = 4.0
rope_context = 8192.0
clip_limit = 1.0
beta_first = 0.9
beta_second = 0.95
adam_eps = 1e-08
learn_rate = 0.09
gain_rate = 1.2
decay_rate = 0.1
masked_score = -1e30

bf16 = jnp.bfloat16
f32 = jnp.float32
MESH = pl.DeviceIdType.MESH
MB = 1024 * 1024
SLOTS = 7


def rotation_tables(wide_count, row_count):
    half_width = HD // 2
    base_freq = rope_theta ** (-np.arange(half_width) * (2.0 / HD))
    wavelen = 2.0 * math.pi / base_freq
    smooth = (rope_context / wavelen - rope_low) / (rope_high - rope_low)
    blended = (1.0 - smooth) * base_freq / rope_factor + smooth * base_freq
    scaled = np.where(
        wavelen < rope_context / rope_high,
        base_freq,
        np.where(wavelen > rope_context / rope_low, base_freq / rope_factor, blended),
    )
    lanes = np.tile(scaled, 4)[None, :]
    inside = np.arange(row_count)[:, None] * lanes
    starts = np.arange(wide_count)[:, None] * row_count * lanes
    sign = np.tile(np.repeat([-1.0, 1.0], half_width), 2)[None, :]
    tables = (np.cos(inside), np.sin(inside), np.cos(starts), np.sin(starts), sign)
    return tuple(jnp.asarray(table, f32) for table in tables)


def adam_update(weight, gradient, old_first, old_second, step_rate, decay_factor):
    momentum = beta_first * old_first + (1.0 - beta_first) * gradient
    variance = beta_second * old_second + (1.0 - beta_second) * gradient * gradient
    corrected = momentum / (1.0 - beta_first**STEP)
    second_hat = variance / (1.0 - beta_second**STEP)
    updated = weight * (1.0 - step_rate * decay_factor) - step_rate * corrected / (
        jnp.sqrt(second_hat) + adam_eps
    )
    return (updated, momentum, variance)


def dot_nn(a, b):
    return jnp.dot(a, b, preferred_element_type=f32)


def dot_nt(a, b):
    return lax.dot_general(a, b, (((1,), (1,)), ((), ())), preferred_element_type=f32)


def dot_tn(a, b):
    return lax.dot_general(a, b, (((0,), (0,)), ((), ())), preferred_element_type=f32)


def tile(j, size):
    return pl.ds(pl.multiple_of(j * size, size), size)


def greet(targets):
    barrier = pltpu.get_barrier_semaphore()
    for target in targets:
        pl.semaphore_signal(barrier, inc=1, device_id=target, device_id_type=MESH)


def met(targets):
    pl.semaphore_wait(pltpu.get_barrier_semaphore(), len(targets))


def rotation(tables, rank, first, count):
    cos_in, sin_in, cos_rank, sin_rank, sign = tables
    rows = pl.ds(first, count)
    c_in, s_in = cos_in[rows, :], sin_in[rows, :]
    c_rank, s_rank = cos_rank[pl.ds(rank, 1), :], sin_rank[pl.ds(rank, 1), :]
    return c_in * c_rank - s_in * s_rank, (s_in * c_rank + c_in * s_rank) * sign[...]


def remote(src, dst, ssem, rsem, there):
    return pltpu.make_async_remote_copy(
        src_ref=src, dst_ref=dst, send_sem=ssem, recv_sem=rsem,
        device_id=there, device_id_type=MESH,
    )


class Grid:
    def __init__(self, axis):
        wide_me, narrow_me = lax.axis_index("wide"), lax.axis_index("narrow")
        self.axis, self.wide_me, self.narrow_me = axis, wide_me, narrow_me
        place = narrow_me if axis == "narrow" else lax.div(wide_me, 2)
        self.core = lax.rem(wide_me, 2)
        self.pair, self.ring = lax.div(place, 4), lax.rem(place, 4)

    def block(self, other, step):
        pair = 1 - self.pair if other else self.pair
        return 4 * pair + lax.rem(self.ring + step + 4, 4)

    def device(self, other, step):
        index = self.block(other, step)
        if self.axis == "narrow":
            return (self.wide_me, index)
        return (2 * index + self.core, self.narrow_me)

    def neighbours(self):
        return [self.device(0, 1), self.device(0, -1), self.device(0, 2), self.device(1, 0)]


def others_of(axis):
    wide_me, narrow_me = lax.axis_index("wide"), lax.axis_index("narrow")
    size = lax.axis_size(axis)
    if axis == "wide":
        return [(lax.rem(wide_me + i, size), narrow_me) for i in range(1, size)]
    return [(wide_me, lax.rem(narrow_me + i, size)) for i in range(1, size)]


def exchange(source, into, axis, ssem, rsem):
    copies = [
        remote(source(there[0]), into.at[i], ssem.at[i], rsem.at[i], there)
        for i, there in enumerate(others_of(axis))
    ]
    for copy in copies:
        copy.start()
    for copy in copies:
        copy.wait()


def mate_of():
    wide_me = lax.axis_index("wide")
    return (wide_me + 1 - 2 * lax.rem(wide_me, 2), lax.axis_index("narrow"))


def mirror_of():
    return (lax.axis_size("wide") - 1 - lax.axis_index("wide"), lax.axis_index("narrow"))


class TreeSum:
    first = (((1, 1), (0, 1)), ((1, -1), (0, -1)), ((1, 2), (1, 0)), ((0, 1), (0, 1)), ((0, -1), (0, -1)))
    second = (((1, 0), (1, 0)), ((0, 2), (0, 2)))

    def __init__(self, grid, part, into, ssem, rsem):
        self.grid, self.part, self.into, self.ssem, self.rsem = grid, part, into, ssem, rsem

    def copy(self, slot):
        block, there = (self.first + self.second)[slot]
        return remote(
            self.part(self.grid.block(*block)), self.into(slot), self.ssem.at[slot],
            self.rsem.at[slot], self.grid.device(*there),
        )

    def start(self):
        for slot in range(5):
            self.copy(slot).start()

    def relay(self, add):
        self.copy(0).wait_recv()
        self.copy(1).wait_recv()
        add(self.grid.block(1, 0), (0, 1))
        self.copy(5).start()
        self.copy(2).wait_recv()
        add(self.grid.block(0, 2), (2,))
        self.copy(6).start()

    def arrive(self):
        for slot in (3, 4, 5, 6):
            self.copy(slot).wait_recv()

    def drain(self):
        for slot in range(SLOTS):
            self.copy(slot).wait_send()


class TreeGather:
    plan = (
        ((0, 0), (1, 0)), ((0, 0), (0, 1)), ((0, 0), (0, -1)), ((0, 0), (0, 2)),
        ((1, 0), (0, 1)), ((1, 0), (0, -1)), ((0, 2), (1, 0)),
    )
    lands = ((1, 0), (0, -1), (0, 1), (0, 2), (1, -1), (1, 1), (1, 2))

    def __init__(self, grid, place, ssem, rsem):
        self.grid, self.place, self.ssem, self.rsem = grid, place, ssem, rsem

    def copy(self, slot):
        block, there = self.plan[slot]
        ref = self.place(self.grid.block(*block))
        return remote(ref, ref, self.ssem.at[slot], self.rsem.at[slot], self.grid.device(*there))

    def start(self):
        for slot in range(4):
            self.copy(slot).start()

    def relay(self):
        self.copy(0).wait_recv()
        self.copy(4).start()
        self.copy(5).start()
        self.copy(3).wait_recv()
        self.copy(6).start()

    def arrive(self):
        for slot in (1, 2, 4, 5, 6):
            self.copy(slot).wait_recv()

    def drain(self):
        for slot in range(SLOTS):
            self.copy(slot).wait_send()


class MateSum:
    def __init__(self, source, own, into, ssem, rsem, lsem=None):
        self.source, self.own, self.into = source, own, into
        self.ssem, self.rsem, self.lsem = ssem, rsem, lsem

    def out(self, k):
        core = lax.rem(lax.axis_index("wide"), 2)
        return remote(
            self.source(2 * k + 1 - core), self.into(k), self.ssem.at[k], self.rsem.at[k], mate_of()
        )

    def start(self):
        def per_block(k, carry):
            self.out(k).start()
            return carry

        lax.fori_loop(0, 8, per_block, 0)

    def add(self):
        core = lax.rem(lax.axis_index("wide"), 2)

        def per_block(k, carry):
            self.out(k).wait_recv()
            self.own(k)[...] = (
                self.source(2 * k + core)[...].astype(f32) + self.into(k)[...].astype(f32)
            ).astype(bf16)
            return carry

        lax.fori_loop(0, 8, per_block, 0)

    def drain(self):
        def per_block(k, carry):
            self.out(k).wait_send()
            return carry

        lax.fori_loop(0, 8, per_block, 0)


def swap_halves(u):
    half = HD // 2
    width = u.shape[-1]
    lane = lax.broadcasted_iota(jnp.int32, u.shape, u.ndim - 1)
    ahead = pltpu.roll(u, width - half, u.ndim - 1)
    behind = pltpu.roll(u, half, u.ndim - 1)
    return jnp.where(lax.rem(lane, HD) < half, ahead, behind)


def inverse_rms(values):
    return lax.rsqrt(jnp.mean(values * values, axis=-1, keepdims=True) + norm_eps)


def head_lanes(pair, odd, high):
    lane = lax.broadcasted_iota(jnp.int32, pair.shape, 1)
    if odd != high:
        pair = pltpu.roll(pair, HD, 1)
    return jnp.where((lane >= HD) == high, pair, 0.0)


def pair_lanes(even, odd):
    lane = lax.broadcasted_iota(jnp.int32, even.shape, 1)
    return jnp.where(lane < HD, even, pltpu.roll(odd, HD, 1))


def block_adder(part, into):
    def add(block, slots):
        total = part(block)[...].astype(f32)
        for slot in slots:
            total = total + into(slot)[...].astype(f32)
        part(block)[...] = total.astype(part(block).dtype)

    return add


class Item:
    def __init__(self, grid, part, into, ssem, rsem, mates=None):
        self.part, self.into, self.mates = part, into, mates
        self.own = grid.block(0, 0)
        self.tree = TreeSum(grid, part, lambda slot: into.at[slot], ssem, rsem)
        self.add = block_adder(part, lambda slot: into.at[slot])

    def relay(self):
        self.tree.relay(self.add)

    def finish(self, out_ref):
        self.tree.arrive()
        height, breadth = out_ref.shape
        span = max(8, min(height, 32768 // breadth))

        def per_tile(j, squares):
            rows = tile(j, span)
            total = self.part(self.own)[rows, :].astype(f32)
            for slot in (3, 4, 5, 6):
                total = total + self.into[slot, rows, :].astype(f32)
            out_ref[rows, :] = total
            return squares + jnp.sum(total * total, axis=0, keepdims=True)

        squares = lax.fori_loop(0, height // span, per_tile, jnp.zeros((1, breadth), f32))
        return jnp.sum(squares, axis=1, keepdims=True)

    def drain(self):
        self.tree.drain()
        if self.mates is not None:
            self.mates.drain()


def key_block(kv, j, bucket, length):
    rows = kv.shape[1] // 2
    block = kv[pl.ds(2 * j, 2), pl.ds(bucket * rows, rows), :].reshape(2 * rows, 2 * HD)
    lane = lax.broadcasted_iota(jnp.int32, block.shape, 1)
    key = 2 * rows * j + lax.broadcasted_iota(jnp.int32, block.shape, 0)
    bias = jnp.where(key < length, 0.0, masked_score)
    masked = jnp.where(lane < HD, block.astype(f32), jnp.where(lane == HD, bias, 0.0)).astype(bf16)
    return block, masked


def head_stack(values, heads, high):
    return jnp.concatenate(
        [
            head_lanes(values[:, (head // 2) * 2 * HD : (head // 2 + 1) * 2 * HD], head % 2 == 1, high)
            for head in range(heads)
        ],
        axis=0,
    )


def forward_kernel(
    len_ref, tok_ref, gains_ref, wkv_ref, tab0, tab1, tab2, tab3, tab4, wq_hbm, wo_hbm, wgu_hbm, wd_hbm,
    cot_hbm,
    log_ref, dh_ref, gain_ref, dob_ref, gout_ref, down_ref, squares_ref,
    n1_hbm, kv_hbm, qs_hbm, os_hbm, hidden_hbm, mixed_hbm, pgate_hbm, pup_hbm,
    wq_ref, qs_ref, os_ref, hidden_ref, mixed_ref,
    wo, wgu, wd, dyb, n1, kv, q, qm, ob, om, da, n2, dgu, dhb, part1, part2, into1, into2,
    mate_gu, mate_d, gdn, idown,
    in_sem, out_sem, st_sem, kv_s, kv_r, km_s, km_r, ex_s, ex_r, rs_s, rs_r, ag_s, ag_r, mt_s, mt_r, it_s, it_r,
):
    narrow, wide = Grid("narrow"), Grid("wide")
    me, wide_me = narrow.narrow_me, narrow.wide_me
    core = wide.core
    chip = lax.div(wide_me, 2)
    last_chip = lax.axis_size("wide") // 2 - 1
    mate, mirror = mate_of(), mirror_of()
    tokens, width = tok_ref.shape
    rows = tokens // 2
    half = rows // 2
    share = rows // lax.axis_size("narrow")
    units = wd.shape[0]
    heads = wo.shape[0] // HD
    span = 256
    loads = [
        pltpu.make_async_copy(src, dst, in_sem.at[i])
        for i, (src, dst) in enumerate(
            ((wo_hbm, wo), (cot_hbm, dyb), (wd_hbm, wd), (wgu_hbm, wgu), (wq_hbm, wq_ref))
        )
    ]
    partners = narrow.neighbours() + wide.neighbours() + [mate, mirror]
    greet(partners)
    for i in (4, 1, 0, 2, 3):
        loads[i].start()

    def normed(j, carry):
        at = tile(j, 64)
        values = tok_ref[at, :].astype(f32)
        n1[at, :] = (values * inverse_rms(values) * gains_ref[0:1, :].astype(f32)).astype(bf16)
        return carry

    lax.fori_loop(0, tokens // 64, normed, 0)
    cosine, sine = rotation((tab0, tab1, tab2, tab3, tab4), wide_me, 0, rows)
    cosine, sine = jnp.concatenate([cosine] * 2, axis=0), jnp.concatenate([sine] * 2, axis=0)
    value = dot_nt(n1[...], wkv_ref[...])
    lane = lax.broadcasted_iota(jnp.int32, value.shape, 1)
    kv[wide_me] = jnp.where(lane < HD, value * cosine + swap_halves(value) * sine, value).astype(bf16)
    met(partners)

    def keys_at(b):
        bucket = pl.ds(b * rows, rows)
        return lambda block: kv.at[2 * block + core, bucket, :]

    keys = [TreeGather(wide, keys_at(b), kv_s.at[b], kv_r.at[b]) for b in range(2)]

    def to_mate(b, block, i):
        ref = keys_at(b)(block)
        return remote(ref, ref, km_s.at[b, i], km_r.at[b, i], mate)

    for b in range(2):
        keys[b].start()
        to_mate(b, chip, 7).start()
    loads[4].wait()
    for pair in range(heads // 2):
        columns = pl.ds(pair * 2 * HD, 2 * HD)
        value = dot_nn(n1[...], wq_ref[:, columns])
        q[:, columns] = ((value * cosine + swap_halves(value) * sine) * HD**-0.5).astype(bf16)

    def later(bucket):
        return pl.ds(bucket * rows + half, half)

    queries = [
        remote(q.at[later(b), :], qm.at[b], ex_s.at[0, b], ex_r.at[0, b], mirror) for b in range(2)
    ]
    for copy in queries:
        copy.start()

    def store(src, dst, i):
        return pltpu.make_async_copy(src, dst, out_sem.at[i])

    store(n1, n1_hbm, 0).start()
    relayed = [
        wide.block(*where) for where in ((1, 0), (0, 2), (0, -1), (0, 1), (1, -1), (1, 1), (1, 2))
    ]

    def keys_relay(b):
        keys[b].relay()
        for i in range(2):
            to_mate(b, relayed[i], i).start()

    def keys_arrive(b):
        keys[b].arrive()
        for i in range(2, 7):
            to_mate(b, relayed[i], i).start()

    def keys_complete(b):
        for i in range(7):
            to_mate(b, relayed[i], i).wait_recv()
        to_mate(b, chip, 7).wait_recv()

    def stack_queries(b, g):
        held = (q[pl.ds(b * rows, half), :] if g == 0 else qm[b]).astype(f32)
        stack = head_stack(held, heads, False)
        lane = lax.broadcasted_iota(jnp.int32, stack.shape, 1)
        qs_ref[b, g] = jnp.where(lane == HD, 1.0, stack).astype(bf16)

    for b in range(2):
        stack_queries(b, 0)
    keys_relay(0)
    loads[1].wait()
    for b in range(2):
        place = wide_me * rows + lax.broadcasted_iota(jnp.int32, (rows, 1), 0)
        mine = pl.ds(b * rows, rows)
        live = (place < len_ref[b]).astype(f32)
        dyb[mine, :] = (dyb[mine, :].astype(f32) * live).astype(bf16)
    keys_relay(1)
    for b in range(2):
        queries[b].wait_recv()
        stack_queries(b, 1)
    keys_arrive(0)

    stack_rows = heads * half

    def attention(b, g):
        length = len_ref[b]
        final = chip if g == 0 else last_chip - chip
        first = wide_me * rows if g == 0 else (2 * last_chip + 1 - wide_me) * rows + half

        def step(masked, j, carry):
            block, scored = key_block(kv, j, b, length)
            lane = lax.broadcasted_iota(jnp.int32, block.shape, 1)
            summed = jnp.where(lane < HD, jnp.ones_like(block), block)
            scores = dot_nt(qs_ref[b, g], scored)
            if masked:
                key = 2 * rows * j + lax.broadcasted_iota(jnp.int32, scores.shape, 1)
                place = first + lax.rem(lax.broadcasted_iota(jnp.int32, scores.shape, 0), half)
                scores = jnp.where(key <= place, scores, masked_score)
            best, total = carry
            new_best = jnp.maximum(best, jnp.max(scores, axis=-1, keepdims=True))
            weights = jnp.exp(scores - new_best).astype(bf16)
            return new_best, total * jnp.exp(best - new_best) + dot_nn(weights, summed)

        carry = (jnp.full((stack_rows, 1), masked_score, f32), jnp.zeros((stack_rows, 2 * HD), f32))
        carry = lax.fori_loop(0, final, functools.partial(step, False), carry)
        best, total = step(True, final, carry)
        lane = lax.broadcasted_iota(jnp.int32, total.shape, 1)
        sums = jnp.where(lane < HD, total, pltpu.roll(total, HD, 1))
        os_ref[b, g] = total / sums
        logs = jnp.transpose(best + jnp.log(sums))
        log_ref[pl.ds(2 * b + g, 1), :] = logs[0:1, :]
        for pair in range(heads // 2):
            even = os_ref[b, g, pl.ds(2 * pair * half, half), :]
            odd = os_ref[b, g, pl.ds((2 * pair + 1) * half, half), :]
            value = pair_lanes(pltpu.roll(even, HD, 1), pltpu.roll(odd, HD, 1)).astype(bf16)
            columns = pl.ds(pair * 2 * HD, 2 * HD)
            if g == 0:
                ob[pl.ds(b * rows, half), columns] = value
            else:
                om[b, :, columns] = value

    def back_to_mirror(b):
        return remote(om.at[b], ob.at[later(b), :], ex_s.at[1, b], ex_r.at[1, b], mirror)

    def mine_in(b):
        return pl.ds(pl.multiple_of(b * rows + me * share, share), share)

    def their_rows(b):
        return lambda block: pl.ds(pl.multiple_of(b * rows + block * share, share), share)

    def sum_of(b, part, into, number):
        where = their_rows(b)
        return TreeSum(
            narrow, lambda block: part.at[where(block), :], lambda slot: into.at[b, slot],
            rs_s.at[number, b], rs_r.at[number, b],
        )

    def adder(b, part, into):
        where = their_rows(b)

        def add(block, slots):
            total = part[where(block), :].astype(f32)
            for slot in slots:
                total = total + into[b, slot].astype(f32)
            part[where(block), :] = total.astype(bf16)

        return add

    def total_of(b, part, into):
        total = part[mine_in(b), :].astype(f32)
        for slot in (3, 4, 5, 6):
            total = total + into[b, slot].astype(f32)
        return total

    def gather_of(b, buffer, number):
        where = their_rows(b)
        return TreeGather(
            narrow, lambda block: buffer.at[where(block), :], ag_s.at[number, b], ag_r.at[number, b]
        )

    sums1 = [sum_of(b, part1, into1, 0) for b in range(2)]
    sums2 = [sum_of(b, part2, into2, 1) for b in range(2)]
    gather1 = [gather_of(b, n2, 0) for b in range(2)]
    gather2 = [gather_of(b, dhb, 1) for b in range(2)]

    def project(b):
        back_to_mirror(b).wait_recv()
        mine = pl.ds(b * rows, rows)
        part1[mine, :] = dot_nn(ob[mine, :], wo[...]).astype(bf16)
        sums1[b].start()

    keys_complete(0)
    attention(0, 1)
    back_to_mirror(0).start()
    keys_arrive(1)
    attention(0, 0)
    loads[0].wait()
    project(0)
    keys_complete(1)
    store(kv, kv_hbm, 1).start()
    attention(1, 1)
    back_to_mirror(1).start()
    attention(1, 0)
    store(os_ref, os_hbm, 2).start()
    store(qs_ref, qs_hbm, 3).start()
    project(1)
    sums1[0].relay(adder(0, part1, into1))
    loads[2].wait()

    def grad_middle(j, carry):
        da[:, tile(j, span)] = dot_nt(dyb[...], wd[tile(j, span), :])
        return carry

    lax.fori_loop(0, units // span, grad_middle, 0)
    sums1[1].relay(adder(1, part1, into1))
    gain2 = gains_ref[1:2, :].astype(f32)
    gain_ref[...] = jnp.zeros(gain_ref.shape, f32)

    def second_norm(b):
        sums1[b].arrive()
        hidden = tok_ref[mine_in(b), :].astype(f32) + total_of(b, part1, into1)
        hidden_ref[b] = hidden
        n2[mine_in(b), :] = (hidden * inverse_rms(hidden) * gain2).astype(bf16)
        gather1[b].start()

    second_norm(0)
    second_norm(1)
    loads[3].wait()
    gather1[0].relay()
    gather1[1].relay()

    def feed(b):
        gather1[b].arrive()
        mine = pl.ds(b * rows, rows)

        def gate_up(j, carry):
            columns = tile(j, span)
            gate = dot_nn(n2[mine, :], wgu[0, :, columns])
            up = dot_nn(n2[mine, :], wgu[1, :, columns])
            sigmoid = jax.nn.sigmoid(gate)
            activated = gate * sigmoid
            mixed_ref[mine, columns] = (activated * up).astype(bf16)
            grad = da[mine, columns]
            dgu[0, mine, columns] = (
                grad * up * sigmoid * (1.0 + gate * (1.0 - sigmoid))
            ).astype(bf16)
            dgu[1, mine, columns] = (grad * activated).astype(bf16)
            return carry

        lax.fori_loop(0, units // span, gate_up, 0)

        def grad_norm_two(c, carry):
            columns = tile(c, 512)
            part2[mine, columns] = (
                dot_nt(dgu[0, mine, :], wgu[0, columns, :]) + dot_nt(dgu[1, mine, :], wgu[1, columns, :])
            ).astype(bf16)
            return carry

        lax.fori_loop(0, width // 512, grad_norm_two, 0)
        sums2[b].start()

    feed(0)
    feed(1)
    store(hidden_ref, hidden_hbm, 4).start()
    store(mixed_ref, mixed_hbm, 5).start()
    wide_share = width // 16
    mates = [
        MateSum(
            lambda w, i=i: wgu.at[i, tile(w, wide_share), :],
            lambda k, i=i: wgu.at[i, tile(2 * k + core, wide_share), :],
            lambda k, i=i: mate_gu.at[i, k], mt_s.at[i], mt_r.at[i],
        )
        for i in range(2)
    ]
    mates.append(
        MateSum(
            lambda w: gdn.at[w], lambda k: gdn.at[2 * k + core], lambda k: mate_d.at[k],
            mt_s.at[2], mt_r.at[2],
        )
    )
    down = Item(wide, mates[2].own, idown, it_s, it_r, mates[2])

    def grad_down(j, carry):
        found = dot_tn(mixed_ref[:, tile(j, span)], dyb[...]).astype(bf16)
        for w in range(16):
            gdn[w, tile(j, span), :] = found[:, w * wide_share : (w + 1) * wide_share]
        return carry

    def grad_gateup(which):
        def per_tile(j, carry):
            wgu[which, tile(j, span), :] = dot_tn(n2[:, tile(j, span)], dgu[which]).astype(bf16)
            return carry

        lax.fori_loop(0, width // span, per_tile, 0)

    def second_norm_back(b):
        sums2[b].arrive()
        total = total_of(b, part2, into2)
        hidden = hidden_ref[b]
        inverse = inverse_rms(hidden)
        z2 = hidden * inverse
        gain_ref[pl.ds(b, 1), :] = jnp.sum(total * z2, axis=0, keepdims=True)
        weighted = total * gain2
        dh = dyb[mine_in(b), :].astype(f32) + inverse * (
            weighted - z2 * jnp.mean(weighted * z2, axis=-1, keepdims=True)
        )
        dh_ref[b] = dh
        dhb[mine_in(b), :] = dh.astype(bf16)
        gather2[b].start()

    def kept(which, out_hbm, k):
        return pltpu.make_async_copy(mates[which].own(k), out_hbm.at[k], st_sem.at[which, k])

    def keep(which, out_hbm):
        mates[which].add()

        def per_block(k, carry):
            kept(which, out_hbm, k).start()
            return carry

        lax.fori_loop(0, 8, per_block, 0)

    lax.fori_loop(0, units // span, grad_down, 0)
    mates[2].start()
    sums2[0].relay(adder(0, part2, into2))
    grad_gateup(0)
    mates[2].add()
    down.tree.start()
    mates[0].start()
    sums2[1].relay(adder(1, part2, into2))
    second_norm_back(0)
    second_norm_back(1)
    gather2[0].relay()
    grad_gateup(1)
    mates[1].start()
    gather2[1].relay()
    down.relay()
    keep(0, pgate_hbm)
    for b in range(2):
        gather2[b].arrive()
        mine = pl.ds(b * rows, rows)
        dob_ref[mine, :] = dot_nt(dhb[mine, :], wo[...]).astype(bf16)

    def grad_out(j, carry):
        gout_ref[:, tile(j, span)] = dot_tn(ob[...], dhb[:, tile(j, span)]).astype(bf16)
        return carry

    lax.fori_loop(0, width // span, grad_out, 0)
    keep(1, pup_hbm)
    squares_ref[...] = jnp.broadcast_to(down.finish(down_ref), squares_ref.shape)
    for b in range(2):
        sums1[b].drain()
        sums2[b].drain()
        gather1[b].drain()
        gather2[b].drain()
        queries[b].wait_send()
        back_to_mirror(b).wait_send()
        keys[b].drain()
        for i in range(7):
            to_mate(b, relayed[i], i).wait_send()
        to_mate(b, chip, 7).wait_send()
    down.drain()
    mates[0].drain()
    mates[1].drain()
    for i, (src, dst) in enumerate(
        ((n1, n1_hbm), (kv, kv_hbm), (os_ref, os_hbm), (qs_ref, qs_hbm), (hidden_ref, hidden_hbm),
         (mixed_ref, mixed_hbm))
    ):
        store(src, dst, i).wait()
    for which, out_hbm in ((0, pgate_hbm), (1, pup_hbm)):
        def per_store(k, carry):
            kept(which, out_hbm, k).wait()
            return carry

        lax.fori_loop(0, 8, per_store, 0)


def forward(lengths, tokens, gains, wkv, tables, wq, wo, wgu, wd, cotangent):
    count, width = tokens.shape
    rows = count // 2
    share = rows // 8
    units = wd.shape[0]
    lanes = wq.shape[1]
    heads = lanes // HD
    stack = heads * rows // 2
    wide_count = 16
    wide_share = width // wide_count
    here = pl.BlockSpec(memory_space=pltpu.VMEM)
    anywhere = pl.BlockSpec(memory_space=pl.ANY)
    shape = jax.ShapeDtypeStruct
    dma = pltpu.SemaphoreType.DMA
    vmem = pltpu.VMEM
    return pl.pallas_call(
        forward_kernel,
        out_shape=(
            shape((8, stack), f32),
            shape((2, share, width), f32),
            shape((8, width), f32),
            shape((count, lanes), bf16),
            shape((lanes, width), bf16),
            shape((units, wide_share), f32),
            shape((8, wide_share), f32),
            shape((count, width), bf16),
            shape((wide_count, count, 2 * HD), bf16),
            shape((2, 2, stack, 2 * HD), bf16),
            shape((2, 2, stack, 2 * HD), f32),
            shape((2, share, width), f32),
            shape((count, units), bf16),
            shape((8, wide_share, units), bf16),
            shape((8, wide_share, units), bf16),
        ),
        in_specs=[pl.BlockSpec(memory_space=pltpu.SMEM)] + [here] * 8 + [anywhere] * 5,
        out_specs=(here,) * 7 + (anywhere,) * 8,
        scratch_shapes=[
            vmem(wq.shape, bf16),
            vmem((2, 2, stack, 2 * HD), bf16),
            vmem((2, 2, stack, 2 * HD), f32),
            vmem((2, share, width), f32),
            vmem((count, units), bf16),
            vmem(wo.shape, bf16),
            vmem(wgu.shape, bf16),
            vmem(wd.shape, bf16),
            vmem((count, width), bf16),
            vmem((count, width), bf16),
            vmem((wide_count, count, 2 * HD), bf16),
            vmem((count, lanes), bf16),
            vmem((2, rows // 2, lanes), bf16),
            vmem((count, lanes), bf16),
            vmem((2, rows // 2, lanes), bf16),
            vmem((count, units), f32),
            vmem((count, width), bf16),
            vmem((2, count, units), bf16),
            vmem((count, width), bf16),
            vmem((count, width), bf16),
            vmem((count, width), bf16),
            vmem((2, SLOTS, share, width), bf16),
            vmem((2, SLOTS, share, width), bf16),
            vmem((2, 8, wide_share, units), bf16),
            vmem((8, units, wide_share), bf16),
            vmem((wide_count, units, wide_share), bf16),
            vmem((SLOTS, units, wide_share), bf16),
            dma((5,)),
            dma((6,)),
            dma((2, 8)),
            dma((2, SLOTS)),
            dma((2, SLOTS)),
            dma((2, 8)),
            dma((2, 8)),
            dma((2, 2)),
            dma((2, 2)),
            dma((2, 2, SLOTS)),
            dma((2, 2, SLOTS)),
            dma((2, 2, SLOTS)),
            dma((2, 2, SLOTS)),
            dma((3, 8)),
            dma((3, 8)),
            dma((SLOTS,)),
            dma((SLOTS,)),
        ],
        compiler_params=pltpu.CompilerParams(
            collective_id=1, has_side_effects=True, vmem_limit_bytes=63 * MB
        ),
        name="forward",
    )(lengths, tokens, gains, wkv, *tables, wq, wo, wgu, wd, cotangent)


def backward_kernel(
    len_ref, gains_ref, tab0, tab1, tab2, tab3, tab4, log_ref, mixed_ref, gain2_ref, dob_ref, squares_ref,
    qs_ref, os_ref, tok_hbm, wq_hbm, wkv_hbm, hidden_hbm, dh_hbm, gout_hbm, kv_hbm, n1_hbm, wd_hbm,
    pgate_hbm, pup_hbm,
    q_ref, pair_ref, out_ref, gate_ref, up_ref, gains_out_ref, norm_ref, layer_hbm, grad_hbm,
    layer_ref, grad_ref, wq_ref, wkv_ref, hidden_ref, dh_ref, gout_ref, cos_ref, sin_ref, pgate, igate,
    kv, n1, wd, tok, pup, pout, pq, pkv, iup, iout, iq, ikv,
    mout, mq, mkv, gq, gkv, part3, part4, into3, into4, acc, dkv, dkm, dkin, dkv_low, dq, dqm, dm,
    dos, qclean, delta, dqacc, grow, gpart, gnear, gwide, spart, snear, pair,
    ld_sem, out_sem, rs_s, rs_r, ag_s, ag_r, dm_s, dm_r, dt_s, dt_r, im_s, im_r, it_s, it_r, ex_s, ex_r,
    g_s, g_r, h_s, h_r,
):
    narrow, wide = Grid("narrow"), Grid("wide")
    me, wide_me = narrow.narrow_me, narrow.wide_me
    core = wide.core
    chip = lax.div(wide_me, 2)
    last_chip = lax.axis_size("wide") // 2 - 1
    peers = lax.axis_size("narrow")
    mate, mirror = mate_of(), mirror_of()
    tokens, width = layer_ref.shape
    rows = tokens // 2
    half = rows // 2
    share = rows // peers
    heads = wq_ref.shape[1] // HD
    span = 256
    wide_share = width // 16

    def mine_in(b):
        return pl.ds(pl.multiple_of(b * rows + me * share, share), share)

    def later(b):
        return pl.ds(b * rows + half, half)

    moves = (
        (kv_hbm, kv), (wd_hbm, wd), (pup_hbm, pup), (n1_hbm, n1),
        (tok_hbm.at[mine_in(0), :], tok.at[0]), (tok_hbm.at[mine_in(1), :], tok.at[1]),
        (pgate_hbm, pgate), (gout_hbm, gout_ref), (hidden_hbm, hidden_ref), (wq_hbm, wq_ref),
        (wkv_hbm, wkv_ref), (dh_hbm, dh_ref),
    )
    loads = [pltpu.make_async_copy(src, dst, ld_sem.at[i]) for i, (src, dst) in enumerate(moves)]
    partners = others_of("narrow") + others_of("wide")
    greet(partners)
    for i in (1, 0, 2, 6, 7, 8, 9, 10, 3, 4, 5, 11):
        loads[i].start()
    tables = (tab0, tab1, tab2, tab3, tab4)
    cos_ref[pl.ds(0, rows), :], sin_ref[pl.ds(0, rows), :] = rotation(tables, wide_me, 0, rows)
    cos_ref[pl.ds(rows, half), :], sin_ref[pl.ds(rows, half), :] = rotation(
        tables, 2 * last_chip + 1 - wide_me, half, half
    )
    loads[1].wait()

    def feed(c, carry):
        part3[:, tile(c, 512)] = dot_nn(mixed_ref[...], wd[:, tile(c, 512)]).astype(bf16)
        return carry

    lax.fori_loop(0, width // 512, feed, 0)
    met(partners)

    grads_there = [
        remote(dob_ref.at[later(b), :], dm.at[b], ex_s.at[0, b], ex_r.at[0, b], mirror) for b in range(2)
    ]
    for copy in grads_there:
        copy.start()

    def mates_of(source, own, into, number):
        return MateSum(
            source, lambda k: own.at[k], lambda k: into.at[k], im_s.at[number], im_r.at[number]
        )

    up = Item(wide, lambda b: pup.at[b], iup, it_s.at[0], it_r.at[0])
    gate = Item(wide, lambda b: pgate.at[b], igate, it_s.at[4], it_r.at[4])
    out = Item(
        wide, lambda b: pout.at[b], iout, it_s.at[1], it_r.at[1],
        mates_of(lambda w: gout_ref.at[:, tile(w, wide_share)], pout, mout, 0),
    )
    query = Item(
        wide, lambda b: pq.at[b], iq, it_s.at[2], it_r.at[2],
        mates_of(lambda w: gq.at[tile(w, wide_share), :], pq, mq, 1),
    )
    keyval = Item(
        wide, lambda b: pkv.at[b], ikv, it_s.at[3], it_r.at[3],
        mates_of(lambda w: gkv.at[tile(w, wide_share), :], pkv, mkv, 2),
    )
    def their_rows(b):
        return lambda block: pl.ds(pl.multiple_of(b * rows + block * share, share), share)

    def sum_of(b, part, into, number):
        where = their_rows(b)
        return TreeSum(
            narrow, lambda block: part.at[where(block), :], lambda slot: into.at[b, slot],
            rs_s.at[number, b], rs_r.at[number, b],
        )

    def adder(b, part, into):
        where = their_rows(b)
        return block_adder(lambda block: part.at[where(block), :], lambda slot: into.at[b, slot])

    def total_of(b, part, into):
        total = part[mine_in(b), :].astype(f32)
        for slot in (3, 4, 5, 6):
            total = total + into[b, slot].astype(f32)
        return total

    def gather_of(b, buffer, number):
        where = their_rows(b)
        return TreeGather(
            narrow, lambda block: buffer.at[where(block), :], ag_s.at[number, b], ag_r.at[number, b]
        )

    sums3 = [sum_of(b, part3, into3, 0) for b in range(2)]
    sums4 = [sum_of(b, part4, into4, 1) for b in range(2)]
    gather3 = [gather_of(b, layer_ref, 0) for b in range(2)]
    gather4 = [gather_of(b, grad_ref, 1) for b in range(2)]

    for b in range(2):
        sums3[b].start()
    for i, item in ((2, up), (6, gate)):
        loads[i].wait()
        item.tree.start()
    loads[7].wait()
    out.mates.start()
    loads[0].wait()
    stack_rows = heads * half

    def attention(b, g):
        length = len_ref[b]
        final = chip if g == 0 else last_chip - chip
        first = wide_me * rows if g == 0 else (2 * last_chip + 1 - wide_me) * rows + half
        held = (dob_ref[pl.ds(b * rows, half), :] if g == 0 else dm[b]).astype(f32)
        stack = head_stack(held, heads, True)
        dos[...] = stack.astype(bf16)
        delta[...] = jnp.sum(jnp.transpose(stack * os_ref[b, g]), axis=0, keepdims=True)
        lane = lax.broadcasted_iota(jnp.int32, qclean.shape, 1)
        qclean[...] = jnp.where(lane < HD, qs_ref[b, g].astype(f32), 0.0).astype(bf16)
        both = jnp.concatenate([qclean[...], dos[...]], axis=0)
        dqacc[...] = jnp.zeros(dqacc.shape, f32)

        def step(masked, j, carry):
            block, scored = key_block(kv, j, b, length)
            scores = dot_nt(scored, qs_ref[b, g])
            if masked:
                key = 2 * rows * j + lax.broadcasted_iota(jnp.int32, scores.shape, 0)
                place = first + lax.rem(lax.broadcasted_iota(jnp.int32, scores.shape, 1), half)
                scores = jnp.where(key <= place, scores, masked_score)
            chances = jnp.exp(scores - log_ref[pl.ds(2 * b + g, 1), :])
            slope = (chances * (dot_nt(block, dos[...]) - delta[...])).astype(bf16)
            acc[j] = acc[j] + dot_nn(jnp.concatenate([slope, chances.astype(bf16)], axis=1), both)
            dqacc[...] = dqacc[...] + dot_tn(slope, block)
            return carry

        lax.fori_loop(0, final, functools.partial(step, False), 0)
        step(True, final, 0)
        for pair in range(heads // 2):
            even = dqacc[pl.ds(2 * pair * half, half), :]
            odd = dqacc[pl.ds((2 * pair + 1) * half, half), :]
            value = pair_lanes(even, odd) * HD**-0.5
            table = pl.ds(0, half) if g == 0 else pl.ds(rows, half)
            value = (value * cos_ref[table, :] - swap_halves(value) * sin_ref[table, :]).astype(bf16)
            columns = pl.ds(pair * 2 * HD, 2 * HD)
            if g == 0:
                dq[pl.ds(b * rows, half), columns] = value
            else:
                dqm[b, :, columns] = value

    def query_back(b):
        return remote(dqm.at[b], dq.at[later(b), :], ex_s.at[1, b], ex_r.at[1, b], mirror)

    def clear():
        def per_block(j, carry):
            acc[j] = jnp.zeros(acc.shape[1:], f32)
            return carry

        lax.fori_loop(0, acc.shape[0], per_block, 0)

    pair_mates = [
        MateSum(
            lambda w, b=b: dkv.at[b, w], lambda k, b=b: dkv.at[b, 2 * k + core],
            lambda k, b=b: dkm.at[b, k], dm_s.at[b], dm_r.at[b],
        )
        for b in range(2)
    ]
    pair_trees = [
        TreeSum(
            wide, lambda block, b=b: dkv.at[b, 2 * block + core], lambda slot, b=b: dkin.at[b, slot],
            dt_s.at[b], dt_r.at[b],
        )
        for b in range(2)
    ]

    def pair_relay(b):
        pair_trees[b].relay(
            block_adder(lambda block: dkv.at[b, 2 * block + core], lambda slot: dkin.at[b, slot])
        )

    def pair_send(b):
        def per_block(j, carry):
            dkv[b, pl.ds(2 * j, 2)] = acc[j].astype(bf16).reshape(2, rows, 2 * HD)
            return carry

        lax.fori_loop(0, acc.shape[0], per_block, 0)
        pair_mates[b].start()

    def pair_mid(b):
        pair_mates[b].add()
        pair_trees[b].start()

    def pair_total(b):
        pair_trees[b].arrive()
        total = dkv[b, wide_me].astype(f32)
        for slot in (3, 4, 5, 6):
            total = total + dkin[b, slot].astype(f32)
        mine = pl.ds(b * rows, rows)
        lane = lax.broadcasted_iota(jnp.int32, total.shape, 1)
        table = pl.ds(0, rows)
        turned = total * cos_ref[table, :] - swap_halves(total) * sin_ref[table, :]
        dkv_low[mine, :] = jnp.where(lane < HD, turned, total).astype(bf16)

    def norm_one_back(b):
        mine = pl.ds(b * rows, rows)

        def per_chunk(c, carry):
            columns = tile(c, 512)
            part4[mine, columns] = (
                dot_nt(dq[mine, :], wq_ref[columns, :]) + dot_nn(dkv_low[mine, :], wkv_ref[:, columns])
            ).astype(bf16)
            return carry

        lax.fori_loop(0, width // 512, per_chunk, 0)
        sums4[b].start()

    def result_rows(b):
        sums3[b].arrive()
        layer_ref[mine_in(b), :] = (hidden_ref[b] + total_of(b, part3, into3)).astype(bf16)
        gather3[b].start()

    gains1 = gains_ref[0:1, :].astype(f32)

    def input_rows(b):
        sums4[b].arrive()
        total = total_of(b, part4, into4)
        values = tok[b].astype(f32)
        inverse = inverse_rms(values)
        z1 = values * inverse
        weighted = total * gains1
        grad_ref[mine_in(b), :] = (
            dh_ref[b] + inverse * (weighted - z1 * jnp.mean(weighted * z1, axis=-1, keepdims=True))
        ).astype(bf16)
        grow[pl.ds(b, 1), :] = jnp.sum(total * z1, axis=0, keepdims=True)

    clear()
    for copy in grads_there:
        copy.wait_recv()
    attention(0, 1)
    query_back(0).start()
    attention(0, 0)
    pair_send(0)
    sums3[0].relay(adder(0, part3, into3))
    sums3[1].relay(adder(1, part3, into3))
    clear()
    attention(1, 1)
    query_back(1).start()
    pair_mid(0)
    loads[8].wait()
    result_rows(0)
    result_rows(1)
    up.relay()
    attention(1, 0)
    pair_send(1)
    pair_relay(0)
    loads[9].wait()
    loads[10].wait()
    pair_mid(1)
    pair_total(0)
    query_back(0).wait_recv()
    norm_one_back(0)
    gather3[0].relay()
    gather3[1].relay()
    query_back(1).wait_recv()
    loads[3].wait()

    def grad_query(j, carry):
        gq[tile(j, span), :] = dot_tn(n1[:, tile(j, span)], dq[...]).astype(bf16)
        return carry

    pair_relay(1)
    lax.fori_loop(0, width // span, grad_query, 0)
    query.mates.start()
    sums4[0].relay(adder(0, part4, into4))
    pair_total(1)
    norm_one_back(1)

    def grad_keyval(j, carry):
        gkv[tile(j, span), :] = dot_tn(n1[:, tile(j, span)], dkv_low[...]).astype(bf16)
        return carry

    query.mates.add()
    query.tree.start()
    gate.relay()
    out.mates.add()
    out.tree.start()
    lax.fori_loop(0, width // span, grad_keyval, 0)
    keyval.mates.start()
    loads[4].wait()
    loads[5].wait()
    loads[11].wait()
    input_rows(0)
    gather4[0].start()
    keyval.mates.add()
    keyval.tree.start()
    sums4[1].relay(adder(1, part4, into4))
    query.relay()
    out.relay()
    squares = squares_ref[0:1, 0:1] + up.finish(up_ref) + gate.finish(gate_ref)
    gather4[0].relay()
    keyval.relay()

    input_rows(1)
    for w in range(16):
        lanes = pl.ds(w * wide_share, wide_share)
        gpart[pl.ds(w, 1), :] = grow[0:1, lanes] + grow[1:2, lanes]
        gpart[pl.ds(16 + w, 1), :] = gain2_ref[0:1, lanes] + gain2_ref[1:2, lanes]
    near_gains = [
        remote(gpart, gnear.at[i], h_s.at[0, i], h_r.at[0, i], there)
        for i, there in enumerate(others_of("narrow"))
    ]
    for copy in near_gains:
        copy.start()
    gather4[1].start()
    squares = squares + query.finish(q_ref) + out.finish(out_ref) + keyval.finish(pair)
    spart[...] = jnp.broadcast_to(squares, spart.shape)
    near_squares = [
        remote(spart, snear.at[i], h_s.at[1, i], h_r.at[1, i], there)
        for i, there in enumerate(others_of("narrow"))
    ]
    for copy in near_squares:
        copy.start()
    pair_ref[...] = jnp.transpose(pair[...])
    for b in range(2):
        gather3[b].arrive()
    layer_store = pltpu.make_async_copy(layer_ref, layer_hbm, out_sem.at[0])
    layer_store.start()
    for copy in near_gains:
        copy.wait()
    total = gpart[pl.ds(0, 32), :]
    for i in range(peers - 1):
        total = total + gnear[i, pl.ds(0, 32), :]
    for copy in near_squares:
        copy.wait()
    square = spart[...]
    for i in range(peers - 1):
        square = square + snear[i]
    gpart[pl.ds(0, 32), :] = total
    gpart[pl.ds(32, 8), :] = square
    gain_copies = [
        remote(gpart, gwide.at[i], g_s.at[i], g_r.at[i], there)
        for i, there in enumerate(others_of("wide"))
    ]
    for copy in gain_copies:
        copy.start()
    gather4[1].relay()
    for copy in gain_copies:
        copy.wait()
    total = gpart[...]
    for i in range(len(gain_copies)):
        total = total + gwide[i]
    gpart[...] = total
    row = lax.broadcasted_iota(jnp.int32, total.shape, 0)
    kept = jnp.where(row < 32, total, 0.0)
    gain_squares = jnp.sum(jnp.sum(kept * kept, axis=1, keepdims=True), axis=0, keepdims=True)
    norm_ref[...] = jnp.sqrt(total[32:40, :] + gain_squares)
    row = lax.broadcasted_iota(jnp.int32, gains_out_ref.shape, 0)
    gains_out_ref[...] = jnp.where(
        row == 0, gpart[pl.ds(wide_me, 1), :], gpart[pl.ds(16 + wide_me, 1), :]
    )
    for b in range(2):
        gather4[b].arrive()
    grad_store = pltpu.make_async_copy(grad_ref, grad_hbm, out_sem.at[1])
    grad_store.start()
    for b in range(2):
        for each in (sums3[b], sums4[b], gather3[b], gather4[b], pair_mates[b], pair_trees[b]):
            each.drain()
        grads_there[b].wait_send()
        query_back(b).wait_send()
    for item in (gate, up, out, query, keyval):
        item.drain()
    layer_store.wait()
    grad_store.wait()


def backward(
    lengths, gains, tables, logs, mixed, gain2, dob, squares, qs, outs, tokens, wq, wkv, hidden, dh, gout,
    kv, n1, wd, pgate, pup,
):
    count, width = n1.shape
    rows = count // 2
    share = rows // 8
    units = wd.shape[0]
    lanes = wq.shape[1]
    stack = qs.shape[2]
    wide_count = 16
    wide_share = width // wide_count
    here = pl.BlockSpec(memory_space=pltpu.VMEM)
    anywhere = pl.BlockSpec(memory_space=pl.ANY)
    shape = jax.ShapeDtypeStruct
    dma = pltpu.SemaphoreType.DMA
    vmem = pltpu.VMEM
    blocks = (
        (wide_share, units), (lanes, wide_share), (wide_share, lanes), (wide_share, 2 * HD),
    )
    return pl.pallas_call(
        backward_kernel,
        out_shape=(
            shape((wide_share, lanes), f32),
            shape((2 * HD, wide_share), f32),
            shape((lanes, wide_share), f32),
            shape((wide_share, units), f32),
            shape((wide_share, units), f32),
            shape((8, wide_share), f32),
            shape((8, wide_share), f32),
            shape((count, width), bf16),
            shape((count, width), bf16),
        ),
        in_specs=[pl.BlockSpec(memory_space=pltpu.SMEM)] + [here] * 13 + [anywhere] * 11,
        out_specs=(here,) * 7 + (anywhere,) * 2,
        scratch_shapes=[
            vmem((count, width), bf16),
            vmem((count, width), bf16),
            vmem(wq.shape, bf16),
            vmem(wkv.shape, bf16),
            vmem(hidden.shape, f32),
            vmem(dh.shape, f32),
            vmem(gout.shape, bf16),
            vmem((rows + rows // 2, 2 * HD), f32),
            vmem((rows + rows // 2, 2 * HD), f32),
            vmem(pgate.shape, bf16),
            vmem((SLOTS, wide_share, units), bf16),
            vmem(kv.shape, bf16),
            vmem((count, width), bf16),
            vmem(wd.shape, bf16),
            vmem((2, share, width), bf16),
            *[vmem((8, *block), bf16) for block in blocks],
            *[vmem((SLOTS, *block), bf16) for block in blocks],
            *[vmem((8, *block), bf16) for block in blocks[1:]],
            vmem((width, lanes), bf16),
            vmem((width, 2 * HD), bf16),
            vmem((count, width), bf16),
            vmem((count, width), bf16),
            vmem((2, SLOTS, share, width), bf16),
            vmem((2, SLOTS, share, width), bf16),
            vmem((8, 2 * rows, 2 * HD), f32),
            vmem((2, wide_count, rows, 2 * HD), bf16),
            vmem((2, 8, rows, 2 * HD), bf16),
            vmem((2, SLOTS, rows, 2 * HD), bf16),
            vmem((count, 2 * HD), bf16),
            vmem((count, lanes), bf16),
            vmem((2, rows // 2, lanes), bf16),
            vmem((2, rows // 2, lanes), bf16),
            vmem((stack, 2 * HD), bf16),
            vmem((stack, 2 * HD), bf16),
            vmem((1, stack), f32),
            vmem((stack, 2 * HD), f32),
            vmem((8, width), f32),
            vmem((40, wide_share), f32),
            vmem((7, 40, wide_share), f32),
            vmem((wide_count - 1, 40, wide_share), f32),
            vmem((8, wide_share), f32),
            vmem((7, 8, wide_share), f32),
            vmem((wide_share, 2 * HD), f32),
            dma((12,)),
            dma((2,)),
            dma((2, 2, SLOTS)),
            dma((2, 2, SLOTS)),
            dma((2, 2, SLOTS)),
            dma((2, 2, SLOTS)),
            dma((2, 8)),
            dma((2, 8)),
            dma((2, SLOTS)),
            dma((2, SLOTS)),
            dma((3, 8)),
            dma((3, 8)),
            dma((5, SLOTS)),
            dma((5, SLOTS)),
            dma((2, 2)),
            dma((2, 2)),
            dma((wide_count - 1,)),
            dma((wide_count - 1,)),
            dma((2, 7)),
            dma((2, 7)),
        ],
        compiler_params=pltpu.CompilerParams(
            collective_id=2, has_side_effects=True, vmem_limit_bytes=63 * MB
        ),
        name="backward",
    )(
        lengths, gains, *tables, logs, mixed, gain2, dob, squares, qs, outs, tokens, wq, wkv, hidden, dh,
        gout, kv, n1, wd, pgate, pup,
    )


def update_kernel(
    norm_ref, gains_sum_ref, gains_ref, gains_first_ref, gains_second_ref, *refs
):
    count = 6
    grads, weights, firsts, seconds = (refs[i * count : (i + 1) * count] for i in range(4))
    refs = refs[4 * count :]
    (layer, grad), refs = refs[:2], refs[2:]
    outs, refs = [refs[i * count : (i + 1) * count] for i in range(4)], refs[4 * count :]
    (layer_out, grad_out), refs = refs[:2], refs[2:]
    gain_outs, norm_out, refs = refs[:4], refs[4], refs[5:]
    norm_out[0, 0] = norm_ref[0, 0]
    held, refs = [refs[i * count : (i + 1) * count] for i in range(5)], refs[5 * count :]
    rows_held, in_sem, out_sem, copy_sem = refs
    wide_me = lax.axis_index("wide")
    at = tile(wide_me, 128)
    slices = (
        lambda ref: ref.at[:, at], lambda ref: ref.at[0, at, :], lambda ref: ref.at[1, at, :],
        lambda ref: ref.at[:, at], lambda ref: ref.at[at, :], lambda ref: ref.at[:, at],
    )
    halves = (None, 0, 1, None, None, None)
    loads, stores = [], []
    for i in range(count):
        def whole(ref):
            return ref if halves[i] is None else ref.at[halves[i]]

        sources = (grads[i], slices[i](weights[i]), whole(firsts[i]), whole(seconds[i]))
        loads.append(
            [pltpu.make_async_copy(src, held[n][i], in_sem.at[n, i]) for n, src in enumerate(sources)]
        )
        targets = (
            (held[0][i], outs[0][i]), (held[2][i], outs[1][i]), (held[3][i], outs[2][i]),
            (held[4][i], outs[3][i]),
        )
        stores.append(
            [
                pltpu.make_async_copy(src, whole(dst), out_sem.at[n, i])
                for n, (src, dst) in enumerate(targets)
            ]
        )
    for group in loads:
        for load in group:
            load.start()
    moved_in = [
        pltpu.make_async_copy(src, rows_held.at[n], copy_sem.at[n]) for n, src in enumerate((layer, grad))
    ]
    moved_out = [
        pltpu.make_async_copy(rows_held.at[n], dst, copy_sem.at[2 + n])
        for n, dst in enumerate((layer_out, grad_out))
    ]
    for copy in moved_in:
        copy.start()
    factor = jnp.minimum(1.0, clip_limit / (norm_ref[0:1, 0:1] + 1e-06))

    for i in range(count):
        for load in loads[i]:
            load.wait()
        height, breadth = held[0][i].shape
        span = max(8, min(height, 16384 // breadth))

        def step(j, carry):
            rows = tile(j, span)
            clipped = held[0][i][rows, :] * factor
            updated, momentum, variance = adam_update(
                held[1][i][rows, :].astype(f32), clipped, held[2][i][rows, :], held[3][i][rows, :],
                learn_rate, decay_rate,
            )
            held[0][i][rows, :] = clipped
            held[2][i][rows, :] = momentum
            held[3][i][rows, :] = variance
            held[4][i][rows, :] = updated
            return carry

        lax.fori_loop(0, height // span, step, 0)
        for store in stores[i]:
            store.start()
    for before, after in zip(moved_in, moved_out):
        before.wait()
        after.start()
    clipped = gains_sum_ref[0:2, :] * factor
    updated, momentum, variance = adam_update(
        gains_ref[:, at].astype(f32), clipped, gains_first_ref[...], gains_second_ref[...], gain_rate, 0.0
    )
    for ref, value in zip(gain_outs, (clipped, momentum, variance, updated)):
        ref[...] = value
    for group in stores:
        for store in group:
            store.wait()
    for copy in moved_out:
        copy.wait()


def update(norm, gains_sum, gains, gains_first, gains_second, grads, weights, firsts, seconds, layer, grad):
    here = pl.BlockSpec(memory_space=pltpu.VMEM)
    anywhere = pl.BlockSpec(memory_space=pl.ANY)
    shape = jax.ShapeDtypeStruct
    like = [shape(first.shape, f32) for first in firsts]
    kept = [like[0], like[1], like[3], like[4], like[5]]
    blocks = [grad_part.shape for grad_part in grads]
    small = shape(gains_first.shape, f32)
    dma = pltpu.SemaphoreType.DMA

    def body(*refs):
        head, rest = refs[:5], refs[5:]
        ins, rest = rest[:6], rest[6:]
        groups = []
        for _ in range(3):
            down, gateup, out, query, keyval = rest[:5]
            groups += [down, gateup, gateup, out, query, keyval]
            rest = rest[5:]
        moved, rest = rest[:2], rest[2:]
        outs = []
        for _ in range(4):
            down, gateup, out, query, keyval = rest[:5]
            outs += [down, gateup, gateup, out, query, keyval]
            rest = rest[5:]
        update_kernel(*head, *ins, *groups, *moved, *outs, *rest)

    def five(arrays):
        return [arrays[0], arrays[1], arrays[3], arrays[4], arrays[5]]

    return pl.pallas_call(
        body,
        out_shape=tuple(kept * 4 + [shape(layer.shape, bf16), shape(grad.shape, bf16)] + [small] * 4 + [shape((1, 1), f32)]),
        in_specs=[here] * 5 + [anywhere] * 23,
        out_specs=tuple([anywhere] * 22 + [here] * 4 + [pl.BlockSpec(memory_space=pltpu.SMEM)]),
        scratch_shapes=[
            *[pltpu.VMEM(block, f32) for block in blocks],
            *[pltpu.VMEM(block, bf16) for block in blocks],
            *[pltpu.VMEM(block, f32) for block in blocks * 3],
            pltpu.VMEM((2, *layer.shape), bf16),
            dma((4, 6)),
            dma((4, 6)),
            dma((4,)),
        ],
        compiler_params=pltpu.CompilerParams(vmem_limit_bytes=63 * MB),
        name="update",
    )(
        norm, gains_sum, gains, gains_first, gains_second, *grads, *five(weights), *five(firsts),
        *five(seconds), layer, grad,
    )


def shards(
    tokens,
    cotangent,
    lengths,
    query_weight,
    keyval_weight,
    output_weight,
    gateup_weight,
    down_weight,
    norm_gains,
    query_first,
    keyval_first,
    output_first,
    gateup_first,
    down_first,
    gains_first,
    query_second,
    keyval_second,
    output_second,
    gateup_second,
    down_second,
    gains_second,
):
    bucket_count, row_count, model_width = tokens.shape
    wide_count = lax.axis_size("wide")
    token_count = bucket_count * row_count
    tables = rotation_tables(wide_count, row_count)
    inputs = tokens.reshape(token_count, model_width)
    units = down_weight.shape[0]

    def turned(values):
        return values.transpose(0, 2, 1).reshape(2 * HD, -1)

    def turned_back(values):
        return values.reshape(2, HD, -1).transpose(0, 2, 1)

    pair_weight = turned(keyval_weight)
    (
        logs, grad_hidden, gain_two, grad_heads, output_grad, down_sum, squares, normed_one, pairs,
        query_stack, out_stack, hidden, mixed, gate_part, up_part,
    ) = forward(
        lengths, inputs, norm_gains, pair_weight, tables, query_weight, output_weight, gateup_weight,
        down_weight, cotangent.reshape(token_count, model_width),
    )
    query_sum, pair_sum, output_sum, gate_sum, up_sum, gains_sum, norm, layer_rows, grad_rows = backward(
        lengths, norm_gains, tables, logs, mixed, gain_two, grad_heads, squares, query_stack, out_stack,
        inputs, query_weight, pair_weight, hidden, grad_hidden, output_grad, pairs, normed_one, down_weight,
        gate_part, up_part,
    )
    results = update(
        norm, gains_sum, norm_gains, gains_first, gains_second,
        (down_sum, gate_sum, up_sum, output_sum, query_sum, pair_sum),
        (down_weight, gateup_weight, gateup_weight, output_weight, query_weight, pair_weight),
        (down_first, gateup_first, gateup_first, output_first, query_first, turned(keyval_first)),
        (down_second, gateup_second, gateup_second, output_second, query_second, turned(keyval_second)),
        layer_rows, grad_rows,
    )
    layer_out = results[20].reshape(bucket_count, row_count, model_width)
    input_grad = results[21].reshape(bucket_count, row_count, model_width)
    kinds = []
    for kind in range(4):
        down, gateup, output, query, pair = results[5 * kind : 5 * kind + 5]
        kinds.append((query, turned_back(pair), output, gateup, down, results[22 + kind]))
    clipped, momentum, variance, updated = kinds
    return (
        layer_out, input_grad, *clipped, results[26].reshape(()), *momentum, *variance, *updated,
    )


def solution(mesh):
    return jax.shard_map(
        shards,
        mesh=mesh,
        in_specs=(
            P(None, "wide", None),
            P(None, "wide", None),
            P(),
            P(None, "narrow"),
            P(None, None, "narrow"),
            P("narrow", None),
            P(None, None, "narrow"),
            P("narrow", None),
            P(),
            P("wide", "narrow"),
            P(None, "wide", "narrow"),
            P("narrow", "wide"),
            P(None, "wide", "narrow"),
            P("narrow", "wide"),
            P(None, "wide"),
            P("wide", "narrow"),
            P(None, "wide", "narrow"),
            P("narrow", "wide"),
            P(None, "wide", "narrow"),
            P("narrow", "wide"),
            P(None, "wide"),
        ),
        out_specs=(
            P(None, "wide", None),
            P(None, "wide", None),
            P("wide", "narrow"),
            P(None, "wide", "narrow"),
            P("narrow", "wide"),
            P(None, "wide", "narrow"),
            P("narrow", "wide"),
            P(None, "wide"),
            P(),
            P("wide", "narrow"),
            P(None, "wide", "narrow"),
            P("narrow", "wide"),
            P(None, "wide", "narrow"),
            P("narrow", "wide"),
            P(None, "wide"),
            P("wide", "narrow"),
            P(None, "wide", "narrow"),
            P("narrow", "wide"),
            P(None, "wide", "narrow"),
            P("narrow", "wide"),
            P(None, "wide"),
            P("wide", "narrow"),
            P(None, "wide", "narrow"),
            P("narrow", "wide"),
            P(None, "wide", "narrow"),
            P("narrow", "wide"),
            P(None, "wide"),
        ),
        check_vma=False,
    )
```

```python
import functools
import math

import jax
import jax.numpy as jnp
import numpy as np
from jax import lax
from jax.experimental import pallas as pl
from jax.experimental.pallas import tpu as pltpu
from jax.sharding import PartitionSpec as P

HD = 64
STEP = 10


norm_eps = 1e-05
rope_theta = 500000.0
rope_factor = 32.0
rope_low = 1.0
rope_high = 4.0
rope_context = 8192.0
clip_limit = 1.0
beta_first = 0.9
beta_second = 0.95
adam_eps = 1e-08
learn_rate = 0.09
gain_rate = 1.2
decay_rate = 0.1
masked_score = -1e30

bf16 = jnp.bfloat16
f32 = jnp.float32
MESH = pl.DeviceIdType.MESH
MB = 1024 * 1024
SLOTS = 7
EARLY = (0,)


def rotation_tables(wide_count, row_count):
    half_width = HD // 2
    base_freq = rope_theta ** (-np.arange(half_width) * (2.0 / HD))
    wavelen = 2.0 * math.pi / base_freq
    smooth = (rope_context / wavelen - rope_low) / (rope_high - rope_low)
    blended = (1.0 - smooth) * base_freq / rope_factor + smooth * base_freq
    scaled = np.where(
        wavelen < rope_context / rope_high,
        base_freq,
        np.where(wavelen > rope_context / rope_low, base_freq / rope_factor, blended),
    )
    lanes = np.tile(scaled, 4)[None, :]
    inside = np.arange(row_count)[:, None] * lanes
    starts = np.arange(wide_count)[:, None] * row_count * lanes
    sign = np.tile(np.repeat([-1.0, 1.0], half_width), 2)[None, :]
    tables = (np.cos(inside), np.sin(inside), np.cos(starts), np.sin(starts), sign)
    return tuple(jnp.asarray(table, f32) for table in tables)


def adam_update(weight, gradient, old_first, old_second, step_rate, decay_factor):
    momentum = beta_first * old_first + (1.0 - beta_first) * gradient
    variance = beta_second * old_second + (1.0 - beta_second) * gradient * gradient
    corrected = momentum / (1.0 - beta_first**STEP)
    second_hat = variance / (1.0 - beta_second**STEP)
    updated = weight * (1.0 - step_rate * decay_factor) - step_rate * corrected / (
        jnp.sqrt(second_hat) + adam_eps
    )
    return (updated, momentum, variance)


def dot_nn(a, b):
    return jnp.dot(a, b, preferred_element_type=f32)


def dot_nt(a, b):
    return lax.dot_general(a, b, (((1,), (1,)), ((), ())), preferred_element_type=f32)


def dot_tn(a, b):
    return lax.dot_general(a, b, (((0,), (0,)), ((), ())), preferred_element_type=f32)


def tile(j, size):
    return pl.ds(pl.multiple_of(j * size, size), size)


def greet(targets):
    barrier = pltpu.get_barrier_semaphore()
    for target in targets:
        pl.semaphore_signal(barrier, inc=1, device_id=target, device_id_type=MESH)


def met(targets):
    pl.semaphore_wait(pltpu.get_barrier_semaphore(), len(targets))


def rotation(tables, rank, first, count):
    cos_in, sin_in, cos_rank, sin_rank, sign = tables
    rows = pl.ds(first, count)
    c_in, s_in = cos_in[rows, :], sin_in[rows, :]
    c_rank, s_rank = cos_rank[pl.ds(rank, 1), :], sin_rank[pl.ds(rank, 1), :]
    return c_in * c_rank - s_in * s_rank, (s_in * c_rank + c_in * s_rank) * sign[...]


def remote(src, dst, ssem, rsem, there):
    return pltpu.make_async_remote_copy(
        src_ref=src, dst_ref=dst, send_sem=ssem, recv_sem=rsem,
        device_id=there, device_id_type=MESH,
    )


class Grid:
    def __init__(self, axis):
        wide_me, narrow_me = lax.axis_index("wide"), lax.axis_index("narrow")
        self.axis, self.wide_me, self.narrow_me = axis, wide_me, narrow_me
        place = narrow_me if axis == "narrow" else lax.div(wide_me, 2)
        self.core = lax.rem(wide_me, 2)
        self.pair, self.ring = lax.div(place, 4), lax.rem(place, 4)

    def block(self, other, step):
        pair = 1 - self.pair if other else self.pair
        return 4 * pair + lax.rem(self.ring + step + 4, 4)

    def device(self, other, step):
        index = self.block(other, step)
        if self.axis == "narrow":
            return (self.wide_me, index)
        return (2 * index + self.core, self.narrow_me)

    def neighbours(self):
        return [self.device(0, 1), self.device(0, -1), self.device(0, 2), self.device(1, 0)]


def others_of(axis):
    wide_me, narrow_me = lax.axis_index("wide"), lax.axis_index("narrow")
    size = lax.axis_size(axis)
    if axis == "wide":
        return [(lax.rem(wide_me + i, size), narrow_me) for i in range(1, size)]
    return [(wide_me, lax.rem(narrow_me + i, size)) for i in range(1, size)]


def exchange(source, into, axis, ssem, rsem):
    copies = [
        remote(source(there[0]), into.at[i], ssem.at[i], rsem.at[i], there)
        for i, there in enumerate(others_of(axis))
    ]
    for copy in copies:
        copy.start()
    for copy in copies:
        copy.wait()


def mate_of():
    wide_me = lax.axis_index("wide")
    return (wide_me + 1 - 2 * lax.rem(wide_me, 2), lax.axis_index("narrow"))


def mirror_of():
    return (lax.axis_size("wide") - 1 - lax.axis_index("wide"), lax.axis_index("narrow"))


class Relay:
    def __init__(self, grid, ssem, rsem):
        self.grid, self.ssem, self.rsem = grid, ssem, rsem

    def copy(self, i):
        block, there = self.routes[i]
        src, dst = self.source(self.grid.block(*block)), self.target(i, self.grid.block(*block))
        return remote(src, dst, self.ssem.at[i], self.rsem.at[i], self.grid.device(*there))

    def send(self, *numbers):
        for i in numbers:
            self.copy(i).start()

    def take(self, *numbers):
        for i in numbers:
            self.copy(i).wait_recv()

    def drain(self, numbers=range(7)):
        for i in numbers:
            self.copy(i).wait_send()


class SumRelay(Relay):
    def __init__(self, grid, part, into, ssem, rsem):
        super().__init__(grid, ssem, rsem)
        self.source, self.into = part, into

    def target(self, i, block):
        return self.into(self.slots[i])

    def add(self, block, slots):
        ref = self.source(self.grid.block(*block))
        total = ref[...].astype(f32)
        for slot in slots:
            total = total + self.into(slot)[...].astype(f32)
        ref[...] = total.astype(ref.dtype)

    def total(self, rows):
        total = self.source(self.grid.block(0, 0))[rows, :].astype(f32)
        for slot in self.final:
            total = total + self.into(slot)[rows, :].astype(f32)
        return total


class FarSum(SumRelay):
    routes = (
        ((1, 1), (0, 1)), ((1, -1), (0, -1)), ((1, 2), (1, 0)),
        ((0, 1), (0, 1)), ((0, -1), (0, -1)), ((1, 0), (1, 0)), ((0, 2), (0, 2)),
    )
    slots = (0, 1, 2, 3, 4, 5, 6)
    final = (3, 4, 5, 6)

    def start(self):
        self.send(0, 1, 2, 3, 4)

    def relay(self, taken=False):
        if not taken:
            self.take(0, 1)
        self.add((1, 0), (0, 1))
        self.send(5)
        if not taken:
            self.take(2)
        self.add((0, 2), (2,))
        self.send(6)

    def arrive(self, taken=False):
        self.take(*((5, 6) if taken else (3, 4, 5, 6)))


class CrossSum(SumRelay):
    routes = (
        ((1, 1), (0, 1)), ((1, -1), (0, -1)), ((1, 2), (0, 2)),
        ((0, 1), (0, 1)), ((0, -1), (0, -1)), ((0, 2), (0, 2)), ((1, 0), (1, 0)),
    )
    slots = (0, 1, 2, 3, 4, 5, 6)
    final = (3, 4, 5, 6)

    def start(self):
        self.send(0, 1, 2, 3, 4, 5)

    def relay(self):
        self.take(0, 1, 2)
        self.add((1, 0), (0, 1, 2))
        self.send(6)

    def arrive(self):
        self.take(3, 4, 5, 6)


class FarGather(Relay):
    routes = (
        ((0, 0), (1, 0)), ((0, 0), (0, 1)), ((0, 0), (0, -1)), ((0, 0), (0, 2)),
        ((1, 0), (0, 1)), ((1, 0), (0, -1)), ((0, 2), (1, 0)),
    )

    def __init__(self, grid, place, ssem, rsem):
        super().__init__(grid, ssem, rsem)
        self.source = place

    def target(self, i, block):
        return self.source(block)

    def start(self):
        self.send(0, 1, 2, 3)

    def relay(self):
        self.take(0)
        self.send(4, 5)
        self.take(3)
        self.send(6)

    def arrive(self):
        self.take(1, 2, 4, 5, 6)


class MateSum:
    def __init__(self, source, own, into, ssem, rsem, lsem=None):
        self.source, self.own, self.into = source, own, into
        self.ssem, self.rsem, self.lsem = ssem, rsem, lsem

    def out(self, k):
        core = lax.rem(lax.axis_index("wide"), 2)
        return remote(
            self.source(2 * k + 1 - core), self.into(k), self.ssem.at[k], self.rsem.at[k], mate_of()
        )

    def start(self):
        def per_block(k, carry):
            self.out(k).start()
            return carry

        lax.fori_loop(0, 8, per_block, 0)

    def add(self):
        core = lax.rem(lax.axis_index("wide"), 2)

        def per_block(k, carry):
            self.out(k).wait_recv()
            self.own(k)[...] = (
                self.source(2 * k + core)[...].astype(f32) + self.into(k)[...].astype(f32)
            ).astype(bf16)
            return carry

        lax.fori_loop(0, 8, per_block, 0)

    def drain(self):
        def per_block(k, carry):
            self.out(k).wait_send()
            return carry

        lax.fori_loop(0, 8, per_block, 0)


def swap_halves(u):
    half = HD // 2
    width = u.shape[-1]
    lane = lax.broadcasted_iota(jnp.int32, u.shape, u.ndim - 1)
    ahead = pltpu.roll(u, width - half, u.ndim - 1)
    behind = pltpu.roll(u, half, u.ndim - 1)
    return jnp.where(lax.rem(lane, HD) < half, ahead, behind)


def inverse_rms(values):
    return lax.rsqrt(jnp.mean(values * values, axis=-1, keepdims=True) + norm_eps)


def head_lanes(pair, odd, high):
    lane = lax.broadcasted_iota(jnp.int32, pair.shape, 1)
    if odd != high:
        pair = pltpu.roll(pair, HD, 1)
    return jnp.where((lane >= HD) == high, pair, 0.0)


def pair_lanes(even, odd):
    lane = lax.broadcasted_iota(jnp.int32, even.shape, 1)
    return jnp.where(lane < HD, even, pltpu.roll(odd, HD, 1))


class Item:
    def __init__(self, tree, grid, part, into, ssem, rsem, mates=None):
        self.tree = tree(grid, part, lambda slot: into.at[slot], ssem, rsem)
        self.mates = mates

    def finish(self, out_ref):
        self.tree.arrive()
        height, breadth = out_ref.shape
        span = max(8, min(height, 32768 // breadth))

        def per_tile(j, squares):
            rows = tile(j, span)
            total = self.tree.total(rows)
            out_ref[rows, :] = total
            return squares + jnp.sum(total * total, axis=0, keepdims=True)

        squares = lax.fori_loop(0, height // span, per_tile, jnp.zeros((1, breadth), f32))
        return jnp.sum(squares, axis=1, keepdims=True)

    def drain(self):
        self.tree.drain()
        if self.mates is not None:
            self.mates.drain()


def key_block(kv, j, bucket, length):
    rows = kv.shape[1] // 2
    block = kv[pl.ds(2 * j, 2), pl.ds(bucket * rows, rows), :].reshape(2 * rows, 2 * HD)
    lane = lax.broadcasted_iota(jnp.int32, block.shape, 1)
    key = 2 * rows * j + lax.broadcasted_iota(jnp.int32, block.shape, 0)
    bias = jnp.where(key < length, 0.0, masked_score)
    masked = jnp.where(lane < HD, block.astype(f32), jnp.where(lane == HD, bias, 0.0)).astype(bf16)
    return block, masked


def head_stack(values, heads, high):
    return jnp.concatenate(
        [
            head_lanes(values[:, (head // 2) * 2 * HD : (head // 2 + 1) * 2 * HD], head % 2 == 1, high)
            for head in range(heads)
        ],
        axis=0,
    )


def forward_kernel(
    len_ref, tok_ref, gains_ref, wkv_ref, tab0, tab1, tab2, tab3, tab4, wq_hbm, wo_hbm, wgu_hbm, wd_hbm,
    cot_hbm,
    log_ref, dh_ref, gain_ref, dob_ref, gout_ref, down_ref, squares_ref,
    n1_hbm, kv_hbm, qs_hbm, os_hbm, hidden_hbm, part_hbm, into_hbm, pgate_hbm, pup_hbm,
    wq_ref, qs_ref, os_ref, hidden_ref, mixed_ref,
    wo, wgu, wd, dyb, n1, kv, q, qm, ob, om, da, n2, dgu, dhb, part1, part2, into1, into2,
    mate_gu, mate_d, gdn, idown,
    in_sem, out_sem, st_sem, kv_s, kv_r, km_s, km_r, ex_s, ex_r, rs_s, rs_r, ag_s, ag_r, mt_s, mt_r, it_s, it_r,
):
    narrow, wide = Grid("narrow"), Grid("wide")
    me, wide_me = narrow.narrow_me, narrow.wide_me
    core = wide.core
    chip = lax.div(wide_me, 2)
    last_chip = lax.axis_size("wide") // 2 - 1
    mate, mirror = mate_of(), mirror_of()
    tokens, width = tok_ref.shape
    rows = tokens // 2
    half = rows // 2
    share = rows // lax.axis_size("narrow")
    units = wd.shape[0]
    heads = wo.shape[0] // HD
    span = 256
    loads = [
        pltpu.make_async_copy(src, dst, in_sem.at[i])
        for i, (src, dst) in enumerate(
            ((wo_hbm, wo), (cot_hbm, dyb), (wd_hbm, wd), (wgu_hbm, wgu), (wq_hbm, wq_ref))
        )
    ]
    partners = narrow.neighbours() + wide.neighbours() + [mate, mirror]
    greet(partners)
    for i in (4, 1, 0, 2, 3):
        loads[i].start()

    def normed(j, carry):
        at = tile(j, 64)
        values = tok_ref[at, :].astype(f32)
        n1[at, :] = (values * inverse_rms(values) * gains_ref[0:1, :].astype(f32)).astype(bf16)
        return carry

    lax.fori_loop(0, tokens // 64, normed, 0)
    cosine, sine = rotation((tab0, tab1, tab2, tab3, tab4), wide_me, 0, rows)
    cosine, sine = jnp.concatenate([cosine] * 2, axis=0), jnp.concatenate([sine] * 2, axis=0)
    value = dot_nt(n1[...], wkv_ref[...])
    lane = lax.broadcasted_iota(jnp.int32, value.shape, 1)
    kv[wide_me] = jnp.where(lane < HD, value * cosine + swap_halves(value) * sine, value).astype(bf16)
    met(partners)

    def keys_at(b):
        bucket = pl.ds(b * rows, rows)
        return lambda block: kv.at[2 * block + core, bucket, :]

    keys = [FarGather(wide, keys_at(b), kv_s.at[b], kv_r.at[b]) for b in range(2)]

    def to_mate(b, block, i):
        ref = keys_at(b)(block)
        return remote(ref, ref, km_s.at[b, i], km_r.at[b, i], mate)

    keys[0].start()
    to_mate(0, chip, 7).start()
    loads[4].wait()
    for pair in range(heads // 2):
        columns = pl.ds(pair * 2 * HD, 2 * HD)
        value = dot_nn(n1[...], wq_ref[:, columns])
        q[:, columns] = ((value * cosine + swap_halves(value) * sine) * HD**-0.5).astype(bf16)

    def later(bucket):
        return pl.ds(bucket * rows + half, half)

    queries = [
        remote(q.at[later(b), :], qm.at[b], ex_s.at[0, b], ex_r.at[0, b], mirror) for b in range(2)
    ]
    for copy in queries:
        copy.start()

    def store(src, dst, i):
        return pltpu.make_async_copy(src, dst, out_sem.at[i])

    store(n1, n1_hbm, 0).start()
    relayed = [
        wide.block(*where) for where in ((1, 0), (0, 2), (0, -1), (0, 1), (1, -1), (1, 1), (1, 2))
    ]

    def keys_relay(b):
        keys[b].relay()
        for i in range(2):
            to_mate(b, relayed[i], i).start()

    def keys_arrive(b):
        keys[b].arrive()
        for i in range(2, 7):
            to_mate(b, relayed[i], i).start()

    def keys_complete(b):
        for i in range(7):
            to_mate(b, relayed[i], i).wait_recv()
        to_mate(b, chip, 7).wait_recv()

    def stack_queries(b, g):
        held = (q[pl.ds(b * rows, half), :] if g == 0 else qm[b]).astype(f32)
        stack = head_stack(held, heads, False)
        lane = lax.broadcasted_iota(jnp.int32, stack.shape, 1)
        qs_ref[b, g] = jnp.where(lane == HD, 1.0, stack).astype(bf16)

    for b in range(2):
        stack_queries(b, 0)
    keys_relay(0)
    keys[1].start()
    to_mate(1, chip, 7).start()
    loads[1].wait()
    for b in range(2):
        place = wide_me * rows + lax.broadcasted_iota(jnp.int32, (rows, 1), 0)
        mine = pl.ds(b * rows, rows)
        live = (place < len_ref[b]).astype(f32)
        dyb[mine, :] = (dyb[mine, :].astype(f32) * live).astype(bf16)
    loads[2].wait()

    def grad_middle(j, carry):
        da[:, tile(j, span)] = dot_nt(dyb[...], wd[tile(j, span), :])
        return carry

    lax.fori_loop(0, units // span, grad_middle, 0)
    for b in range(2):
        queries[b].wait_recv()
        stack_queries(b, 1)
    keys_arrive(0)
    keys_relay(1)

    stack_rows = heads * half

    def attention(b, g):
        length = len_ref[b]
        final = chip if g == 0 else last_chip - chip
        first = wide_me * rows if g == 0 else (2 * last_chip + 1 - wide_me) * rows + half

        def step(masked, j, carry):
            block, scored = key_block(kv, j, b, length)
            lane = lax.broadcasted_iota(jnp.int32, block.shape, 1)
            summed = jnp.where(lane < HD, jnp.ones_like(block), block)
            scores = dot_nt(qs_ref[b, g], scored)
            if masked:
                key = 2 * rows * j + lax.broadcasted_iota(jnp.int32, scores.shape, 1)
                place = first + lax.rem(lax.broadcasted_iota(jnp.int32, scores.shape, 0), half)
                scores = jnp.where(key <= place, scores, masked_score)
            best, total = carry
            new_best = jnp.maximum(best, jnp.max(scores, axis=-1, keepdims=True))
            weights = jnp.exp(scores - new_best).astype(bf16)
            return new_best, total * jnp.exp(best - new_best) + dot_nn(weights, summed)

        carry = (jnp.full((stack_rows, 1), masked_score, f32), jnp.zeros((stack_rows, 2 * HD), f32))
        carry = lax.fori_loop(0, final, functools.partial(step, False), carry)
        best, total = step(True, final, carry)
        lane = lax.broadcasted_iota(jnp.int32, total.shape, 1)
        sums = jnp.where(lane < HD, total, pltpu.roll(total, HD, 1))
        os_ref[b, g] = total / sums
        logs = jnp.transpose(best + jnp.log(sums))
        log_ref[pl.ds(2 * b + g, 1), :] = logs[0:1, :]
        for pair in range(heads // 2):
            even = os_ref[b, g, pl.ds(2 * pair * half, half), :]
            odd = os_ref[b, g, pl.ds((2 * pair + 1) * half, half), :]
            value = pair_lanes(pltpu.roll(even, HD, 1), pltpu.roll(odd, HD, 1)).astype(bf16)
            columns = pl.ds(pair * 2 * HD, 2 * HD)
            if g == 0:
                ob[pl.ds(b * rows, half), columns] = value
            else:
                om[b, :, columns] = value

    def back_to_mirror(b):
        return remote(om.at[b], ob.at[later(b), :], ex_s.at[1, b], ex_r.at[1, b], mirror)

    def mine_in(b):
        return pl.ds(pl.multiple_of(b * rows + me * share, share), share)

    def their_rows(b):
        return lambda block: pl.ds(pl.multiple_of(b * rows + block * share, share), share)

    def sum_of(b, part, into, number):
        where = their_rows(b)
        return FarSum(
            narrow, lambda block: part.at[where(block), :], lambda slot: into.at[b, slot],
            rs_s.at[number, b], rs_r.at[number, b],
        )

    def gather_of(b, buffer, number):
        where = their_rows(b)
        return FarGather(
            narrow, lambda block: buffer.at[where(block), :], ag_s.at[number, b], ag_r.at[number, b]
        )

    whole = pl.ds(0, share)
    sums1 = [sum_of(b, part1, into1, 0) for b in range(2)]
    sums2 = [sum_of(b, part2, into2, 1) for b in range(2)]
    sums3 = [sum_of(b, part1, into1, 2) for b in range(2)]
    gather1 = [gather_of(b, n2, 0) for b in range(2)]
    gather2 = [gather_of(b, dhb, 1) for b in range(2)]

    def project(b):
        back_to_mirror(b).wait_recv()
        mine = pl.ds(b * rows, rows)
        part1[mine, :] = dot_nn(ob[mine, :], wo[...]).astype(bf16)
        sums1[b].start()

    keys_complete(0)
    attention(0, 1)
    back_to_mirror(0).start()
    keys_arrive(1)
    attention(0, 0)
    loads[0].wait()
    project(0)
    keys_complete(1)
    store(kv, kv_hbm, 1).start()
    attention(1, 1)
    back_to_mirror(1).start()
    attention(1, 0)
    store(os_ref, os_hbm, 2).start()
    store(qs_ref, qs_hbm, 3).start()
    project(1)
    sums1[0].relay()
    sums1[1].relay()
    gain2 = gains_ref[1:2, :].astype(f32)
    gain_ref[...] = jnp.zeros(gain_ref.shape, f32)

    def second_norm(b):
        sums1[b].arrive()
        hidden = tok_ref[mine_in(b), :].astype(f32) + sums1[b].total(whole)
        hidden_ref[b] = hidden
        n2[mine_in(b), :] = (hidden * inverse_rms(hidden) * gain2).astype(bf16)
        gather1[b].start()

    second_norm(0)
    second_norm(1)
    loads[3].wait()
    gather1[0].relay()
    gather1[1].relay()

    def feed(b):
        gather1[b].arrive()
        mine = pl.ds(b * rows, rows)

        def gate_up(j, carry):
            columns = tile(j, span)
            gate = dot_nn(n2[mine, :], wgu[0, :, columns])
            up = dot_nn(n2[mine, :], wgu[1, :, columns])
            sigmoid = jax.nn.sigmoid(gate)
            activated = gate * sigmoid
            mixed_ref[mine, columns] = (activated * up).astype(bf16)
            grad = da[mine, columns]
            dgu[0, mine, columns] = (
                grad * up * sigmoid * (1.0 + gate * (1.0 - sigmoid))
            ).astype(bf16)
            dgu[1, mine, columns] = (grad * activated).astype(bf16)
            return carry

        lax.fori_loop(0, units // span, gate_up, 0)

        def grad_norm_two(c, carry):
            columns = tile(c, 512)
            part2[mine, columns] = (
                dot_nt(dgu[0, mine, :], wgu[0, columns, :]) + dot_nt(dgu[1, mine, :], wgu[1, columns, :])
            ).astype(bf16)
            return carry

        lax.fori_loop(0, width // 512, grad_norm_two, 0)
        sums2[b].start()

    feed(0)
    feed(1)
    store(hidden_ref, hidden_hbm, 4).start()
    wide_share = width // 16
    mates = [
        MateSum(
            lambda w, i=i: wgu.at[i, tile(w, wide_share), :],
            lambda k, i=i: wgu.at[i, tile(2 * k + core, wide_share), :],
            lambda k, i=i: mate_gu.at[i, k], mt_s.at[i], mt_r.at[i],
        )
        for i in range(2)
    ]
    mates.append(
        MateSum(
            lambda w: gdn.at[w], lambda k: gdn.at[2 * k + core], lambda k: mate_d.at[k],
            mt_s.at[2], mt_r.at[2],
        )
    )
    down = Item(
        CrossSum, wide, mates[2].own, idown, it_s, it_r, mates[2]
    )

    def grad_down(j, carry):
        found = dot_tn(mixed_ref[:, tile(j, span)], dyb[...]).astype(bf16)
        for w in range(16):
            gdn[w, tile(j, span), :] = found[:, w * wide_share : (w + 1) * wide_share]
        return carry

    def grad_gateup(which):
        def per_tile(j, carry):
            wgu[which, tile(j, span), :] = dot_tn(n2[:, tile(j, span)], dgu[which]).astype(bf16)
            return carry

        lax.fori_loop(0, width // span, per_tile, 0)

    def second_norm_back(b):
        sums2[b].arrive()
        total = sums2[b].total(whole)
        hidden = hidden_ref[b]
        inverse = inverse_rms(hidden)
        z2 = hidden * inverse
        gain_ref[pl.ds(b, 1), :] = jnp.sum(total * z2, axis=0, keepdims=True)
        weighted = total * gain2
        dh = dyb[mine_in(b), :].astype(f32) + inverse * (
            weighted - z2 * jnp.mean(weighted * z2, axis=-1, keepdims=True)
        )
        dh_ref[b] = dh
        dhb[mine_in(b), :] = dh.astype(bf16)
        gather2[b].start()

    def kept(which, out_hbm, k):
        return pltpu.make_async_copy(mates[which].own(k), out_hbm.at[k], st_sem.at[which, k])

    def keep(which, out_hbm):
        mates[which].add()

        def per_block(k, carry):
            kept(which, out_hbm, k).start()
            return carry

        lax.fori_loop(0, 8, per_block, 0)

    def feed_down(c, carry):
        part1[:, tile(c, 512)] = dot_nn(mixed_ref[...], wd[:, tile(c, 512)]).astype(bf16)
        return carry

    def grad_heads(b):
        gather2[b].arrive()
        mine = pl.ds(b * rows, rows)
        dob_ref[mine, :] = dot_nt(dhb[mine, :], wo[...]).astype(bf16)

    def grad_out(j, carry):
        gout_ref[:, tile(j, span)] = dot_tn(ob[...], dhb[:, tile(j, span)]).astype(bf16)
        return carry

    sums2[0].relay()
    lax.fori_loop(0, units // span, grad_down, 0)
    mates[2].start()
    grad_gateup(0)
    mates[0].start()
    sums2[1].relay()
    second_norm_back(0)
    mates[2].add()
    down.tree.start()
    sums1[0].drain()
    sums1[1].drain()
    lax.fori_loop(0, width // 512, feed_down, 0)
    second_norm_back(1)
    gather2[0].relay()
    store(part1, part_hbm, 5).start()
    grad_gateup(1)
    mates[1].start()
    gather2[1].relay()
    for b in EARLY:
        sums3[b].start()
    keep(0, pgate_hbm)
    down.tree.relay()
    grad_heads(0)
    grad_heads(1)
    lax.fori_loop(0, width // span, grad_out, 0)
    keep(1, pup_hbm)
    squares_ref[...] = jnp.broadcast_to(down.finish(down_ref), squares_ref.shape)
    for b in EARLY:
        sums3[b].take(0, 1, 2, 3, 4)
        sums3[b].drain(range(5))
        store(into1.at[b, pl.ds(0, 5)], into_hbm.at[b], 6 + b).start()
    for b in range(2):
        sums2[b].drain()
        gather1[b].drain()
        gather2[b].drain()
        queries[b].wait_send()
        back_to_mirror(b).wait_send()
        keys[b].drain()
        for i in range(7):
            to_mate(b, relayed[i], i).wait_send()
        to_mate(b, chip, 7).wait_send()
    down.drain()
    mates[0].drain()
    mates[1].drain()
    for i, (src, dst) in enumerate(
        ((n1, n1_hbm), (kv, kv_hbm), (os_ref, os_hbm), (qs_ref, qs_hbm), (hidden_ref, hidden_hbm),
         (part1, part_hbm))
    ):
        store(src, dst, i).wait()
    for b in EARLY:
        store(into1.at[b, pl.ds(0, 5)], into_hbm.at[b], 6 + b).wait()
    for which, out_hbm in ((0, pgate_hbm), (1, pup_hbm)):
        def per_store(k, carry):
            kept(which, out_hbm, k).wait()
            return carry

        lax.fori_loop(0, 8, per_store, 0)


def forward(lengths, tokens, gains, wkv, tables, wq, wo, wgu, wd, cotangent):
    count, width = tokens.shape
    rows = count // 2
    share = rows // 8
    units = wd.shape[0]
    lanes = wq.shape[1]
    heads = lanes // HD
    stack = heads * rows // 2
    wide_count = 16
    wide_share = width // wide_count
    here = pl.BlockSpec(memory_space=pltpu.VMEM)
    anywhere = pl.BlockSpec(memory_space=pl.ANY)
    shape = jax.ShapeDtypeStruct
    dma = pltpu.SemaphoreType.DMA
    vmem = pltpu.VMEM
    return pl.pallas_call(
        forward_kernel,
        out_shape=(
            shape((8, stack), f32),
            shape((2, share, width), f32),
            shape((8, width), f32),
            shape((count, lanes), bf16),
            shape((lanes, width), bf16),
            shape((units, wide_share), f32),
            shape((8, wide_share), f32),
            shape((count, width), bf16),
            shape((wide_count, count, 2 * HD), bf16),
            shape((2, 2, stack, 2 * HD), bf16),
            shape((2, 2, stack, 2 * HD), f32),
            shape((2, share, width), f32),
            shape((count, width), bf16),
            shape((2, 5, share, width), bf16),
            shape((8, wide_share, units), bf16),
            shape((8, wide_share, units), bf16),
        ),
        in_specs=[pl.BlockSpec(memory_space=pltpu.SMEM)] + [here] * 8 + [anywhere] * 5,
        out_specs=(here,) * 7 + (anywhere,) * 9,
        scratch_shapes=[
            vmem(wq.shape, bf16),
            vmem((2, 2, stack, 2 * HD), bf16),
            vmem((2, 2, stack, 2 * HD), f32),
            vmem((2, share, width), f32),
            vmem((count, units), bf16),
            vmem(wo.shape, bf16),
            vmem(wgu.shape, bf16),
            vmem(wd.shape, bf16),
            vmem((count, width), bf16),
            vmem((count, width), bf16),
            vmem((wide_count, count, 2 * HD), bf16),
            vmem((count, lanes), bf16),
            vmem((2, rows // 2, lanes), bf16),
            vmem((count, lanes), bf16),
            vmem((2, rows // 2, lanes), bf16),
            vmem((count, units), f32),
            vmem((count, width), bf16),
            vmem((2, count, units), bf16),
            vmem((count, width), bf16),
            vmem((count, width), bf16),
            vmem((count, width), bf16),
            vmem((2, SLOTS, share, width), bf16),
            vmem((2, SLOTS, share, width), bf16),
            vmem((2, 8, wide_share, units), bf16),
            vmem((8, units, wide_share), bf16),
            vmem((wide_count, units, wide_share), bf16),
            vmem((SLOTS, units, wide_share), bf16),
            dma((5,)),
            dma((8,)),
            dma((2, 8)),
            dma((2, SLOTS)),
            dma((2, SLOTS)),
            dma((2, 8)),
            dma((2, 8)),
            dma((2, 2)),
            dma((2, 2)),
            dma((3, 2, SLOTS)),
            dma((3, 2, SLOTS)),
            dma((2, 2, SLOTS)),
            dma((2, 2, SLOTS)),
            dma((3, 8)),
            dma((3, 8)),
            dma((SLOTS,)),
            dma((SLOTS,)),
        ],
        compiler_params=pltpu.CompilerParams(
            collective_id=1, has_side_effects=True, vmem_limit_bytes=63 * MB
        ),
        name="forward",
    )(lengths, tokens, gains, wkv, *tables, wq, wo, wgu, wd, cotangent)


def backward_kernel(
    len_ref, gains_ref, tab0, tab1, tab2, tab3, tab4, log_ref, gain2_ref, dob_ref, squares_ref,
    qs_ref, os_ref, tok_hbm, wq_hbm, wkv_hbm, hidden_hbm, dh_hbm, gout_hbm, kv_hbm, n1_hbm, part_hbm, into_hbm,
    pgate_hbm, pup_hbm,
    q_ref, pair_ref, out_ref, gate_ref, up_ref, gains_out_ref, norm_ref, layer_hbm, grad_hbm,
    layer_ref, grad_ref, wq_ref, wkv_ref, hidden_ref, dh_ref, gout_ref, cos_ref, sin_ref, pgate, igate,
    kv, n1, tok, pup, pout, pq, pkv, iup, iout, iq, ikv,
    mout, mq, mkv, gq, gkv, part3, part4, into3, into4, acc, dkv, dkm, dkin, dkv_low, dq, dqm, dm,
    dos, qclean, delta, dqacc, grow, gpart, gnear, gwide, pair,
    ld_sem, out_sem, rs_s, rs_r, ag_s, ag_r, dm_s, dm_r, dt_s, dt_r, im_s, im_r, it_s, it_r, ex_s, ex_r,
    g_s, g_r, h_s, h_r,
):
    narrow, wide = Grid("narrow"), Grid("wide")
    me, wide_me = narrow.narrow_me, narrow.wide_me
    core = wide.core
    chip = lax.div(wide_me, 2)
    last_chip = lax.axis_size("wide") // 2 - 1
    peers = lax.axis_size("narrow")
    mate, mirror = mate_of(), mirror_of()
    tokens, width = layer_ref.shape
    rows = tokens // 2
    half = rows // 2
    share = rows // peers
    heads = wq_ref.shape[1] // HD
    span = 256
    wide_share = width // 16

    def mine_in(b):
        return pl.ds(pl.multiple_of(b * rows + me * share, share), share)

    def later(b):
        return pl.ds(b * rows + half, half)

    moves = (
        (kv_hbm, kv), (part_hbm, part3), (pup_hbm, pup), (n1_hbm, n1),
        (tok_hbm.at[mine_in(0), :], tok.at[0]), (tok_hbm.at[mine_in(1), :], tok.at[1]),
        (pgate_hbm, pgate), (gout_hbm, gout_ref), (hidden_hbm, hidden_ref), (wq_hbm, wq_ref),
        (wkv_hbm, wkv_ref), (dh_hbm, dh_ref), (into_hbm.at[0], into3.at[0, pl.ds(0, 5)]),
        (into_hbm.at[1], into3.at[1, pl.ds(0, 5)]),
    )
    loads = [pltpu.make_async_copy(src, dst, ld_sem.at[i]) for i, (src, dst) in enumerate(moves)]
    partners = others_of("narrow") + others_of("wide")
    greet(partners)
    waits_early = [12 + b for b in EARLY]
    for i in [1] + waits_early + [0, 2, 6, 7, 8, 9, 10, 3, 4, 5, 11]:
        loads[i].start()
    tables = (tab0, tab1, tab2, tab3, tab4)
    cos_ref[pl.ds(0, rows), :], sin_ref[pl.ds(0, rows), :] = rotation(tables, wide_me, 0, rows)
    cos_ref[pl.ds(rows, half), :], sin_ref[pl.ds(rows, half), :] = rotation(
        tables, 2 * last_chip + 1 - wide_me, half, half
    )
    met(partners)

    grads_there = [
        remote(dob_ref.at[later(b), :], dm.at[b], ex_s.at[0, b], ex_r.at[0, b], mirror) for b in range(2)
    ]
    for copy in grads_there:
        copy.start()

    def mates_of(source, own, into, number):
        return MateSum(
            source, lambda k: own.at[k], lambda k: into.at[k], im_s.at[number], im_r.at[number]
        )

    up = Item(FarSum, wide, lambda b: pup.at[b], iup, it_s.at[0], it_r.at[0])
    gate = Item(FarSum, wide, lambda b: pgate.at[b], igate, it_s.at[4], it_r.at[4])
    out = Item(
        FarSum, wide, lambda b: pout.at[b], iout, it_s.at[1], it_r.at[1],
        mates_of(lambda w: gout_ref.at[:, tile(w, wide_share)], pout, mout, 0),
    )
    query = Item(
        FarSum, wide, lambda b: pq.at[b], iq, it_s.at[2], it_r.at[2],
        mates_of(lambda w: gq.at[tile(w, wide_share), :], pq, mq, 1),
    )
    keyval = Item(
        FarSum, wide, lambda b: pkv.at[b], ikv, it_s.at[3], it_r.at[3],
        mates_of(lambda w: gkv.at[tile(w, wide_share), :], pkv, mkv, 2),
    )
    def their_rows(b):
        return lambda block: pl.ds(pl.multiple_of(b * rows + block * share, share), share)

    def sum_of(kind, b, part, into, number):
        where = their_rows(b)
        return kind(
            narrow, lambda block: part.at[where(block), :], lambda slot: into.at[b, slot],
            rs_s.at[number, b], rs_r.at[number, b],
        )

    def gather_of(kind, b, buffer, number):
        where = their_rows(b)
        return kind(
            narrow, lambda block: buffer.at[where(block), :], ag_s.at[number, b], ag_r.at[number, b]
        )

    whole = pl.ds(0, share)
    sums3 = [sum_of(FarSum, b, part3, into3, 0) for b in range(2)]
    sums4 = [sum_of(FarSum, b, part4, into4, 1) for b in range(2)]
    gather3 = [gather_of(FarGather, b, layer_ref, 0) for b in range(2)]
    gather4 = [gather_of(FarGather, b, grad_ref, 1) for b in range(2)]

    loads[1].wait()
    for b in range(2):
        if b in EARLY:
            loads[12 + b].wait()
            sums3[b].relay(taken=True)
        else:
            sums3[b].start()
    for i, item in ((2, up), (6, gate)):
        loads[i].wait()
        item.tree.start()
    loads[7].wait()
    out.mates.start()
    loads[0].wait()
    stack_rows = heads * half

    def attention(b, g):
        length = len_ref[b]
        final = chip if g == 0 else last_chip - chip
        first = wide_me * rows if g == 0 else (2 * last_chip + 1 - wide_me) * rows + half
        held = (dob_ref[pl.ds(b * rows, half), :] if g == 0 else dm[b]).astype(f32)
        stack = head_stack(held, heads, True)
        dos[...] = stack.astype(bf16)
        delta[...] = jnp.sum(jnp.transpose(stack * os_ref[b, g]), axis=0, keepdims=True)
        lane = lax.broadcasted_iota(jnp.int32, qclean.shape, 1)
        qclean[...] = jnp.where(lane < HD, qs_ref[b, g].astype(f32), 0.0).astype(bf16)
        both = jnp.concatenate([qclean[...], dos[...]], axis=0)
        dqacc[...] = jnp.zeros(dqacc.shape, f32)

        def step(masked, j, carry):
            block, scored = key_block(kv, j, b, length)
            scores = dot_nt(scored, qs_ref[b, g])
            if masked:
                key = 2 * rows * j + lax.broadcasted_iota(jnp.int32, scores.shape, 0)
                place = first + lax.rem(lax.broadcasted_iota(jnp.int32, scores.shape, 1), half)
                scores = jnp.where(key <= place, scores, masked_score)
            chances = jnp.exp(scores - log_ref[pl.ds(2 * b + g, 1), :])
            slope = (chances * (dot_nt(block, dos[...]) - delta[...])).astype(bf16)
            acc[j] = acc[j] + dot_nn(jnp.concatenate([slope, chances.astype(bf16)], axis=1), both)
            dqacc[...] = dqacc[...] + dot_tn(slope, block)
            return carry

        lax.fori_loop(0, final, functools.partial(step, False), 0)
        step(True, final, 0)
        for pair in range(heads // 2):
            even = dqacc[pl.ds(2 * pair * half, half), :]
            odd = dqacc[pl.ds((2 * pair + 1) * half, half), :]
            value = pair_lanes(even, odd) * HD**-0.5
            table = pl.ds(0, half) if g == 0 else pl.ds(rows, half)
            value = (value * cos_ref[table, :] - swap_halves(value) * sin_ref[table, :]).astype(bf16)
            columns = pl.ds(pair * 2 * HD, 2 * HD)
            if g == 0:
                dq[pl.ds(b * rows, half), columns] = value
            else:
                dqm[b, :, columns] = value

    def query_back(b):
        return remote(dqm.at[b], dq.at[later(b), :], ex_s.at[1, b], ex_r.at[1, b], mirror)

    def clear():
        def per_block(j, carry):
            acc[j] = jnp.zeros(acc.shape[1:], f32)
            return carry

        lax.fori_loop(0, acc.shape[0], per_block, 0)

    pair_mates = [
        MateSum(
            lambda w, b=b: dkv.at[b, w], lambda k, b=b: dkv.at[b, 2 * k + core],
            lambda k, b=b: dkm.at[b, k], dm_s.at[b], dm_r.at[b],
        )
        for b in range(2)
    ]
    pair_trees = [
        FarSum(
            wide, lambda block, b=b: dkv.at[b, 2 * block + core], lambda slot, b=b: dkin.at[b, slot],
            dt_s.at[b], dt_r.at[b],
        )
        for b in range(2)
    ]

    def pair_relay(b):
        pair_trees[b].relay()

    def pair_send(b):
        def per_block(j, carry):
            dkv[b, pl.ds(2 * j, 2)] = acc[j].astype(bf16).reshape(2, rows, 2 * HD)
            return carry

        lax.fori_loop(0, acc.shape[0], per_block, 0)
        pair_mates[b].start()

    def pair_mid(b):
        pair_mates[b].add()
        pair_trees[b].start()

    def pair_total(b):
        pair_trees[b].arrive()
        total = pair_trees[b].total(pl.ds(0, rows))
        mine = pl.ds(b * rows, rows)
        lane = lax.broadcasted_iota(jnp.int32, total.shape, 1)
        table = pl.ds(0, rows)
        turned = total * cos_ref[table, :] - swap_halves(total) * sin_ref[table, :]
        dkv_low[mine, :] = jnp.where(lane < HD, turned, total).astype(bf16)

    def norm_one_back(b):
        mine = pl.ds(b * rows, rows)

        def per_chunk(c, carry):
            columns = tile(c, 512)
            part4[mine, columns] = (
                dot_nt(dq[mine, :], wq_ref[columns, :]) + dot_nn(dkv_low[mine, :], wkv_ref[:, columns])
            ).astype(bf16)
            return carry

        lax.fori_loop(0, width // 512, per_chunk, 0)
        sums4[b].start()

    def result_rows(b):
        sums3[b].arrive(taken=b in EARLY)
        layer_ref[mine_in(b), :] = (hidden_ref[b] + sums3[b].total(whole)).astype(bf16)
        gather3[b].start()

    gains1 = gains_ref[0:1, :].astype(f32)

    def input_rows(b):
        sums4[b].arrive()
        total = sums4[b].total(whole)
        values = tok[b].astype(f32)
        inverse = inverse_rms(values)
        z1 = values * inverse
        weighted = total * gains1
        grad_ref[mine_in(b), :] = (
            dh_ref[b] + inverse * (weighted - z1 * jnp.mean(weighted * z1, axis=-1, keepdims=True))
        ).astype(bf16)
        grow[pl.ds(b, 1), :] = jnp.sum(total * z1, axis=0, keepdims=True)

    clear()
    attention(0, 0)
    for copy in grads_there:
        copy.wait_recv()
    attention(0, 1)
    query_back(0).start()
    pair_send(0)
    if 0 not in EARLY:
        sums3[0].relay()
    if 1 not in EARLY:
        sums3[1].relay()
    clear()
    attention(1, 1)
    query_back(1).start()
    pair_mid(0)
    loads[8].wait()
    result_rows(0)
    result_rows(1)
    up.tree.relay()
    attention(1, 0)
    pair_send(1)
    pair_relay(0)
    loads[9].wait()
    loads[10].wait()
    pair_mid(1)
    pair_total(0)
    query_back(0).wait_recv()
    norm_one_back(0)
    gather3[0].relay()
    gather3[1].relay()
    query_back(1).wait_recv()
    loads[3].wait()

    def grad_query(j, carry):
        gq[tile(j, span), :] = dot_tn(n1[:, tile(j, span)], dq[...]).astype(bf16)
        return carry

    pair_relay(1)
    lax.fori_loop(0, width // span, grad_query, 0)
    query.mates.start()
    sums4[0].relay()
    pair_total(1)
    norm_one_back(1)

    def grad_keyval(j, carry):
        gkv[tile(j, span), :] = dot_tn(n1[:, tile(j, span)], dkv_low[...]).astype(bf16)
        return carry

    query.mates.add()
    query.tree.start()
    gate.tree.relay()
    out.mates.add()
    out.tree.start()
    lax.fori_loop(0, width // span, grad_keyval, 0)
    keyval.mates.start()
    loads[4].wait()
    loads[5].wait()
    loads[11].wait()
    input_rows(0)
    gather4[0].start()
    keyval.mates.add()
    keyval.tree.start()
    sums4[1].relay()
    query.tree.relay()
    out.tree.relay()
    squares = squares_ref[0:1, 0:1] + up.finish(up_ref) + gate.finish(gate_ref)
    gather4[0].relay()
    keyval.tree.relay()
    input_rows(1)
    squares = squares + query.finish(q_ref) + out.finish(out_ref) + keyval.finish(pair)

    for w in range(16):
        lanes = pl.ds(w * wide_share, wide_share)
        gpart[pl.ds(w, 1), :] = grow[0:1, lanes] + grow[1:2, lanes]
        gpart[pl.ds(16 + w, 1), :] = gain2_ref[0:1, lanes] + gain2_ref[1:2, lanes]
    gpart[pl.ds(32, 8), :] = jnp.broadcast_to(squares, (8, wide_share))
    near_gains = [
        remote(gpart, gnear.at[i], h_s.at[i], h_r.at[i], there)
        for i, there in enumerate(others_of("narrow"))
    ]
    for copy in near_gains:
        copy.start()
    gather4[1].start()
    pair_ref[...] = jnp.transpose(pair[...])
    for copy in near_gains:
        copy.wait()
    total = gpart[...]
    for i in range(peers - 1):
        total = total + gnear[i]
    gpart[...] = total
    gain_copies = [
        remote(gpart, gwide.at[i], g_s.at[i], g_r.at[i], there)
        for i, there in enumerate(others_of("wide"))
    ]
    for copy in gain_copies:
        copy.start()
    gather4[1].relay()
    for b in range(2):
        gather3[b].arrive()
    layer_store = pltpu.make_async_copy(layer_ref, layer_hbm, out_sem.at[0])
    layer_store.start()
    for copy in gain_copies:
        copy.wait()
    total = gpart[...]
    for i in range(len(gain_copies)):
        total = total + gwide[i]
    gpart[...] = total
    row = lax.broadcasted_iota(jnp.int32, total.shape, 0)
    kept = jnp.where(row < 32, total, 0.0)
    gain_squares = jnp.sum(jnp.sum(kept * kept, axis=1, keepdims=True), axis=0, keepdims=True)
    norm_ref[...] = jnp.sqrt(total[32:40, :] + gain_squares)
    row = lax.broadcasted_iota(jnp.int32, gains_out_ref.shape, 0)
    gains_out_ref[...] = jnp.where(
        row == 0, gpart[pl.ds(wide_me, 1), :], gpart[pl.ds(16 + wide_me, 1), :]
    )
    for b in range(2):
        gather4[b].arrive()
    grad_store = pltpu.make_async_copy(grad_ref, grad_hbm, out_sem.at[1])
    grad_store.start()
    for b in range(2):
        sums3[b].drain((5, 6) if b in EARLY else range(7))
        for each in (sums4[b], gather3[b], gather4[b], pair_mates[b], pair_trees[b]):
            each.drain()
        grads_there[b].wait_send()
        query_back(b).wait_send()
    for item in (gate, up, out, query, keyval):
        item.drain()
    layer_store.wait()
    grad_store.wait()


def backward(
    lengths, gains, tables, logs, gain2, dob, squares, qs, outs, tokens, wq, wkv, hidden, dh, gout,
    kv, n1, part, into, pgate, pup,
):
    count, width = n1.shape
    rows = count // 2
    share = rows // 8
    units = pgate.shape[2]
    lanes = wq.shape[1]
    stack = qs.shape[2]
    wide_count = 16
    wide_share = width // wide_count
    here = pl.BlockSpec(memory_space=pltpu.VMEM)
    anywhere = pl.BlockSpec(memory_space=pl.ANY)
    shape = jax.ShapeDtypeStruct
    dma = pltpu.SemaphoreType.DMA
    vmem = pltpu.VMEM
    blocks = (
        (wide_share, units), (lanes, wide_share), (wide_share, lanes), (wide_share, 2 * HD),
    )
    return pl.pallas_call(
        backward_kernel,
        out_shape=(
            shape((wide_share, lanes), f32),
            shape((2 * HD, wide_share), f32),
            shape((lanes, wide_share), f32),
            shape((wide_share, units), f32),
            shape((wide_share, units), f32),
            shape((8, wide_share), f32),
            shape((8, wide_share), f32),
            shape((count, width), bf16),
            shape((count, width), bf16),
        ),
        in_specs=[pl.BlockSpec(memory_space=pltpu.SMEM)] + [here] * 12 + [anywhere] * 12,
        out_specs=(here,) * 7 + (anywhere,) * 2,
        scratch_shapes=[
            vmem((count, width), bf16),
            vmem((count, width), bf16),
            vmem(wq.shape, bf16),
            vmem(wkv.shape, bf16),
            vmem(hidden.shape, f32),
            vmem(dh.shape, f32),
            vmem(gout.shape, bf16),
            vmem((rows + rows // 2, 2 * HD), f32),
            vmem((rows + rows // 2, 2 * HD), f32),
            vmem(pgate.shape, bf16),
            vmem((SLOTS, wide_share, units), bf16),
            vmem(kv.shape, bf16),
            vmem((count, width), bf16),
            vmem((2, share, width), bf16),
            *[vmem((8, *block), bf16) for block in blocks],
            *[vmem((SLOTS, *block), bf16) for block in blocks],
            *[vmem((8, *block), bf16) for block in blocks[1:]],
            vmem((width, lanes), bf16),
            vmem((width, 2 * HD), bf16),
            vmem((count, width), bf16),
            vmem((count, width), bf16),
            vmem((2, SLOTS, share, width), bf16),
            vmem((2, SLOTS, share, width), bf16),
            vmem((8, 2 * rows, 2 * HD), f32),
            vmem((2, wide_count, rows, 2 * HD), bf16),
            vmem((2, 8, rows, 2 * HD), bf16),
            vmem((2, SLOTS, rows, 2 * HD), bf16),
            vmem((count, 2 * HD), bf16),
            vmem((count, lanes), bf16),
            vmem((2, rows // 2, lanes), bf16),
            vmem((2, rows // 2, lanes), bf16),
            vmem((stack, 2 * HD), bf16),
            vmem((stack, 2 * HD), bf16),
            vmem((1, stack), f32),
            vmem((stack, 2 * HD), f32),
            vmem((8, width), f32),
            vmem((40, wide_share), f32),
            vmem((7, 40, wide_share), f32),
            vmem((wide_count - 1, 40, wide_share), f32),
            vmem((wide_share, 2 * HD), f32),
            dma((14,)),
            dma((2,)),
            dma((2, 2, SLOTS)),
            dma((2, 2, SLOTS)),
            dma((2, 2, SLOTS)),
            dma((2, 2, SLOTS)),
            dma((2, 8)),
            dma((2, 8)),
            dma((2, SLOTS)),
            dma((2, SLOTS)),
            dma((3, 8)),
            dma((3, 8)),
            dma((5, SLOTS)),
            dma((5, SLOTS)),
            dma((2, 2)),
            dma((2, 2)),
            dma((wide_count - 1,)),
            dma((wide_count - 1,)),
            dma((7,)),
            dma((7,)),
        ],
        compiler_params=pltpu.CompilerParams(
            collective_id=2, has_side_effects=True, vmem_limit_bytes=63 * MB
        ),
        name="backward",
    )(
        lengths, gains, *tables, logs, gain2, dob, squares, qs, outs, tokens, wq, wkv, hidden, dh,
        gout, kv, n1, part, into, pgate, pup,
    )


def update_kernel(
    norm_ref, gains_sum_ref, gains_ref, gains_first_ref, gains_second_ref, *refs
):
    count = 6
    grads, weights, firsts, seconds = (refs[i * count : (i + 1) * count] for i in range(4))
    refs = refs[4 * count :]
    (layer, grad), refs = refs[:2], refs[2:]
    outs, refs = [refs[i * count : (i + 1) * count] for i in range(4)], refs[4 * count :]
    (layer_out, grad_out), refs = refs[:2], refs[2:]
    gain_outs, norm_out, refs = refs[:4], refs[4], refs[5:]
    norm_out[0, 0] = norm_ref[0, 0]
    held, refs = [refs[i * count : (i + 1) * count] for i in range(5)], refs[5 * count :]
    rows_held, in_sem, out_sem, copy_sem = refs
    wide_me = lax.axis_index("wide")
    at = tile(wide_me, 128)
    slices = (
        lambda ref: ref.at[:, at], lambda ref: ref.at[0, at, :], lambda ref: ref.at[1, at, :],
        lambda ref: ref.at[:, at], lambda ref: ref.at[at, :], lambda ref: ref.at[:, at],
    )
    halves = (None, 0, 1, None, None, None)
    loads, stores = [], []
    for i in range(count):
        def whole(ref):
            return ref if halves[i] is None else ref.at[halves[i]]

        sources = (grads[i], slices[i](weights[i]), whole(firsts[i]), whole(seconds[i]))
        loads.append(
            [pltpu.make_async_copy(src, held[n][i], in_sem.at[n, i]) for n, src in enumerate(sources)]
        )
        targets = (
            (held[0][i], outs[0][i]), (held[2][i], outs[1][i]), (held[3][i], outs[2][i]),
            (held[4][i], outs[3][i]),
        )
        stores.append(
            [
                pltpu.make_async_copy(src, whole(dst), out_sem.at[n, i])
                for n, (src, dst) in enumerate(targets)
            ]
        )
    for group in loads:
        for load in group:
            load.start()
    moved_in = [
        pltpu.make_async_copy(src, rows_held.at[n], copy_sem.at[n]) for n, src in enumerate((layer, grad))
    ]
    moved_out = [
        pltpu.make_async_copy(rows_held.at[n], dst, copy_sem.at[2 + n])
        for n, dst in enumerate((layer_out, grad_out))
    ]
    for copy in moved_in:
        copy.start()
    factor = jnp.minimum(1.0, clip_limit / (norm_ref[0:1, 0:1] + 1e-06))

    for i in range(count):
        for load in loads[i]:
            load.wait()
        height, breadth = held[0][i].shape
        span = max(8, min(height, 16384 // breadth))

        def step(j, carry):
            rows = tile(j, span)
            clipped = held[0][i][rows, :] * factor
            updated, momentum, variance = adam_update(
                held[1][i][rows, :].astype(f32), clipped, held[2][i][rows, :], held[3][i][rows, :],
                learn_rate, decay_rate,
            )
            held[0][i][rows, :] = clipped
            held[2][i][rows, :] = momentum
            held[3][i][rows, :] = variance
            held[4][i][rows, :] = updated
            return carry

        lax.fori_loop(0, height // span, step, 0)
        for store in stores[i]:
            store.start()
    for before, after in zip(moved_in, moved_out):
        before.wait()
        after.start()
    clipped = gains_sum_ref[0:2, :] * factor
    updated, momentum, variance = adam_update(
        gains_ref[:, at].astype(f32), clipped, gains_first_ref[...], gains_second_ref[...], gain_rate, 0.0
    )
    for ref, value in zip(gain_outs, (clipped, momentum, variance, updated)):
        ref[...] = value
    for group in stores:
        for store in group:
            store.wait()
    for copy in moved_out:
        copy.wait()


def update(norm, gains_sum, gains, gains_first, gains_second, grads, weights, firsts, seconds, layer, grad):
    here = pl.BlockSpec(memory_space=pltpu.VMEM)
    anywhere = pl.BlockSpec(memory_space=pl.ANY)
    shape = jax.ShapeDtypeStruct
    like = [shape(first.shape, f32) for first in firsts]
    kept = [like[0], like[1], like[3], like[4], like[5]]
    blocks = [grad_part.shape for grad_part in grads]
    small = shape(gains_first.shape, f32)
    dma = pltpu.SemaphoreType.DMA

    def body(*refs):
        head, rest = refs[:5], refs[5:]
        ins, rest = rest[:6], rest[6:]
        groups = []
        for _ in range(3):
            down, gateup, out, query, keyval = rest[:5]
            groups += [down, gateup, gateup, out, query, keyval]
            rest = rest[5:]
        moved, rest = rest[:2], rest[2:]
        outs = []
        for _ in range(4):
            down, gateup, out, query, keyval = rest[:5]
            outs += [down, gateup, gateup, out, query, keyval]
            rest = rest[5:]
        update_kernel(*head, *ins, *groups, *moved, *outs, *rest)

    def five(arrays):
        return [arrays[0], arrays[1], arrays[3], arrays[4], arrays[5]]

    return pl.pallas_call(
        body,
        out_shape=tuple(kept * 4 + [shape(layer.shape, bf16), shape(grad.shape, bf16)] + [small] * 4 + [shape((1, 1), f32)]),
        in_specs=[here] * 5 + [anywhere] * 23,
        out_specs=tuple([anywhere] * 22 + [here] * 4 + [pl.BlockSpec(memory_space=pltpu.SMEM)]),
        scratch_shapes=[
            *[pltpu.VMEM(block, f32) for block in blocks],
            *[pltpu.VMEM(block, bf16) for block in blocks],
            *[pltpu.VMEM(block, f32) for block in blocks * 3],
            pltpu.VMEM((2, *layer.shape), bf16),
            dma((4, 6)),
            dma((4, 6)),
            dma((4,)),
        ],
        compiler_params=pltpu.CompilerParams(vmem_limit_bytes=63 * MB),
        name="update",
    )(
        norm, gains_sum, gains, gains_first, gains_second, *grads, *five(weights), *five(firsts),
        *five(seconds), layer, grad,
    )


def shards(
    tokens,
    cotangent,
    lengths,
    query_weight,
    keyval_weight,
    output_weight,
    gateup_weight,
    down_weight,
    norm_gains,
    query_first,
    keyval_first,
    output_first,
    gateup_first,
    down_first,
    gains_first,
    query_second,
    keyval_second,
    output_second,
    gateup_second,
    down_second,
    gains_second,
):
    bucket_count, row_count, model_width = tokens.shape
    wide_count = lax.axis_size("wide")
    token_count = bucket_count * row_count
    tables = rotation_tables(wide_count, row_count)
    inputs = tokens.reshape(token_count, model_width)
    units = down_weight.shape[0]

    def turned(values):
        return values.transpose(0, 2, 1).reshape(2 * HD, -1)

    def turned_back(values):
        return values.reshape(2, HD, -1).transpose(0, 2, 1)

    pair_weight = turned(keyval_weight)
    (
        logs, grad_hidden, gain_two, grad_heads, output_grad, down_sum, squares, normed_one, pairs,
        query_stack, out_stack, hidden, layer_part, layer_in, gate_part, up_part,
    ) = forward(
        lengths, inputs, norm_gains, pair_weight, tables, query_weight, output_weight, gateup_weight,
        down_weight, cotangent.reshape(token_count, model_width),
    )
    query_sum, pair_sum, output_sum, gate_sum, up_sum, gains_sum, norm, layer_rows, grad_rows = backward(
        lengths, norm_gains, tables, logs, gain_two, grad_heads, squares, query_stack, out_stack,
        inputs, query_weight, pair_weight, hidden, grad_hidden, output_grad, pairs, normed_one, layer_part, layer_in,
        gate_part, up_part,
    )
    results = update(
        norm, gains_sum, norm_gains, gains_first, gains_second,
        (down_sum, gate_sum, up_sum, output_sum, query_sum, pair_sum),
        (down_weight, gateup_weight, gateup_weight, output_weight, query_weight, pair_weight),
        (down_first, gateup_first, gateup_first, output_first, query_first, turned(keyval_first)),
        (down_second, gateup_second, gateup_second, output_second, query_second, turned(keyval_second)),
        layer_rows, grad_rows,
    )
    layer_out = results[20].reshape(bucket_count, row_count, model_width)
    input_grad = results[21].reshape(bucket_count, row_count, model_width)
    kinds = []
    for kind in range(4):
        down, gateup, output, query, pair = results[5 * kind : 5 * kind + 5]
        kinds.append((query, turned_back(pair), output, gateup, down, results[22 + kind]))
    clipped, momentum, variance, updated = kinds
    return (
        layer_out, input_grad, *clipped, results[26].reshape(()), *momentum, *variance, *updated,
    )


def solution(mesh):
    return jax.shard_map(
        shards,
        mesh=mesh,
        in_specs=(
            P(None, "wide", None),
            P(None, "wide", None),
            P(),
            P(None, "narrow"),
            P(None, None, "narrow"),
            P("narrow", None),
            P(None, None, "narrow"),
            P("narrow", None),
            P(),
            P("wide", "narrow"),
            P(None, "wide", "narrow"),
            P("narrow", "wide"),
            P(None, "wide", "narrow"),
            P("narrow", "wide"),
            P(None, "wide"),
            P("wide", "narrow"),
            P(None, "wide", "narrow"),
            P("narrow", "wide"),
            P(None, "wide", "narrow"),
            P("narrow", "wide"),
            P(None, "wide"),
        ),
        out_specs=(
            P(None, "wide", None),
            P(None, "wide", None),
            P("wide", "narrow"),
            P(None, "wide", "narrow"),
            P("narrow", "wide"),
            P(None, "wide", "narrow"),
            P("narrow", "wide"),
            P(None, "wide"),
            P(),
            P("wide", "narrow"),
            P(None, "wide", "narrow"),
            P("narrow", "wide"),
            P(None, "wide", "narrow"),
            P("narrow", "wide"),
            P(None, "wide"),
            P("wide", "narrow"),
            P(None, "wide", "narrow"),
            P("narrow", "wide"),
            P(None, "wide", "narrow"),
            P("narrow", "wide"),
            P(None, "wide"),
            P("wide", "narrow"),
            P(None, "wide", "narrow"),
            P("narrow", "wide"),
            P(None, "wide", "narrow"),
            P("narrow", "wide"),
            P(None, "wide"),
        ),
        check_vma=False,
    )
```

```python
import functools
import math

import jax
import jax.numpy as jnp
import numpy as np
from jax import lax
from jax.experimental import pallas as pl
from jax.experimental.pallas import tpu as pltpu
from jax.sharding import PartitionSpec as P

HD = 64
STEP = 10


norm_eps = 1e-05
rope_theta = 500000.0
rope_factor = 32.0
rope_low = 1.0
rope_high = 4.0
rope_context = 8192.0
clip_limit = 1.0
beta_first = 0.9
beta_second = 0.95
adam_eps = 1e-08
learn_rate = 0.09
gain_rate = 1.2
decay_rate = 0.1
masked_score = -1e30

bf16 = jnp.bfloat16
f32 = jnp.float32
MESH = pl.DeviceIdType.MESH
MB = 1024 * 1024
SLOTS = 7
EARLY = (0,)


def rotation_tables(wide_count, row_count):
    half_width = HD // 2
    base_freq = rope_theta ** (-np.arange(half_width) * (2.0 / HD))
    wavelen = 2.0 * math.pi / base_freq
    smooth = (rope_context / wavelen - rope_low) / (rope_high - rope_low)
    blended = (1.0 - smooth) * base_freq / rope_factor + smooth * base_freq
    scaled = np.where(
        wavelen < rope_context / rope_high,
        base_freq,
        np.where(wavelen > rope_context / rope_low, base_freq / rope_factor, blended),
    )
    lanes = np.tile(scaled, 4)[None, :]
    inside = np.arange(row_count)[:, None] * lanes
    starts = np.arange(wide_count)[:, None] * row_count * lanes
    sign = np.tile(np.repeat([-1.0, 1.0], half_width), 2)[None, :]
    tables = (np.cos(inside), np.sin(inside), np.cos(starts), np.sin(starts), sign)
    return tuple(jnp.asarray(table, f32) for table in tables)


def adam_update(weight, gradient, old_first, old_second, step_rate, decay_factor):
    momentum = beta_first * old_first + (1.0 - beta_first) * gradient
    variance = beta_second * old_second + (1.0 - beta_second) * gradient * gradient
    corrected = momentum / (1.0 - beta_first**STEP)
    second_hat = variance / (1.0 - beta_second**STEP)
    updated = weight * (1.0 - step_rate * decay_factor) - step_rate * corrected / (
        jnp.sqrt(second_hat) + adam_eps
    )
    return (updated, momentum, variance)


def dot_nn(a, b):
    return jnp.dot(a, b, preferred_element_type=f32)


def dot_nt(a, b):
    return lax.dot_general(a, b, (((1,), (1,)), ((), ())), preferred_element_type=f32)


def dot_tn(a, b):
    return lax.dot_general(a, b, (((0,), (0,)), ((), ())), preferred_element_type=f32)


def tile(j, size):
    return pl.ds(pl.multiple_of(j * size, size), size)


def greet(targets):
    barrier = pltpu.get_barrier_semaphore()
    for target in targets:
        pl.semaphore_signal(barrier, inc=1, device_id=target, device_id_type=MESH)


def met(targets):
    pl.semaphore_wait(pltpu.get_barrier_semaphore(), len(targets))


def rotation(tables, rank, first, count):
    cos_in, sin_in, cos_rank, sin_rank, sign = tables
    rows = pl.ds(first, count)
    c_in, s_in = cos_in[rows, :], sin_in[rows, :]
    c_rank, s_rank = cos_rank[pl.ds(rank, 1), :], sin_rank[pl.ds(rank, 1), :]
    return c_in * c_rank - s_in * s_rank, (s_in * c_rank + c_in * s_rank) * sign[...]


def remote(src, dst, ssem, rsem, there):
    return pltpu.make_async_remote_copy(
        src_ref=src, dst_ref=dst, send_sem=ssem, recv_sem=rsem,
        device_id=there, device_id_type=MESH,
    )


class Grid:
    def __init__(self, axis):
        wide_me, narrow_me = lax.axis_index("wide"), lax.axis_index("narrow")
        self.axis, self.wide_me, self.narrow_me = axis, wide_me, narrow_me
        place = narrow_me if axis == "narrow" else lax.div(wide_me, 2)
        self.core = lax.rem(wide_me, 2)
        self.pair, self.ring = lax.div(place, 4), lax.rem(place, 4)

    def block(self, other, step):
        pair = 1 - self.pair if other else self.pair
        return 4 * pair + lax.rem(self.ring + step + 4, 4)

    def device(self, other, step):
        index = self.block(other, step)
        if self.axis == "narrow":
            return (self.wide_me, index)
        return (2 * index + self.core, self.narrow_me)

    def neighbours(self):
        return [self.device(0, 1), self.device(0, -1), self.device(0, 2), self.device(1, 0)]


def others_of(axis):
    wide_me, narrow_me = lax.axis_index("wide"), lax.axis_index("narrow")
    size = lax.axis_size(axis)
    if axis == "wide":
        return [(lax.rem(wide_me + i, size), narrow_me) for i in range(1, size)]
    return [(wide_me, lax.rem(narrow_me + i, size)) for i in range(1, size)]


def exchange(source, into, axis, ssem, rsem):
    copies = [
        remote(source(there[0]), into.at[i], ssem.at[i], rsem.at[i], there)
        for i, there in enumerate(others_of(axis))
    ]
    for copy in copies:
        copy.start()
    for copy in copies:
        copy.wait()


def mate_of():
    wide_me = lax.axis_index("wide")
    return (wide_me + 1 - 2 * lax.rem(wide_me, 2), lax.axis_index("narrow"))


def mirror_of():
    return (lax.axis_size("wide") - 1 - lax.axis_index("wide"), lax.axis_index("narrow"))


class Relay:
    def __init__(self, grid, ssem, rsem):
        self.grid, self.ssem, self.rsem = grid, ssem, rsem

    def copy(self, i):
        block, there = self.routes[i]
        src, dst = self.source(self.grid.block(*block)), self.target(i, self.grid.block(*block))
        return remote(src, dst, self.ssem.at[i], self.rsem.at[i], self.grid.device(*there))

    def send(self, *numbers):
        for i in numbers:
            self.copy(i).start()

    def take(self, *numbers):
        for i in numbers:
            self.copy(i).wait_recv()

    def drain(self, numbers=range(7)):
        for i in numbers:
            self.copy(i).wait_send()


class SumRelay(Relay):
    def __init__(self, grid, part, into, ssem, rsem):
        super().__init__(grid, ssem, rsem)
        self.source, self.into = part, into

    def target(self, i, block):
        return self.into(self.slots[i])

    def add(self, block, slots):
        ref = self.source(self.grid.block(*block))
        total = ref[...].astype(f32)
        for slot in slots:
            total = total + self.into(slot)[...].astype(f32)
        ref[...] = total.astype(ref.dtype)

    def total(self, rows):
        total = self.source(self.grid.block(0, 0))[rows, :].astype(f32)
        for slot in self.final:
            total = total + self.into(slot)[rows, :].astype(f32)
        return total


class FarSum(SumRelay):
    routes = (
        ((1, 1), (0, 1)), ((1, -1), (0, -1)), ((1, 2), (1, 0)),
        ((0, 1), (0, 1)), ((0, -1), (0, -1)), ((1, 0), (1, 0)), ((0, 2), (0, 2)),
    )
    slots = (0, 1, 2, 3, 4, 5, 6)
    final = (3, 4, 5, 6)

    def start(self):
        self.send(0, 1, 2, 3, 4)

    def relay(self, taken=False):
        if not taken:
            self.take(0, 1)
        self.add((1, 0), (0, 1))
        self.send(5)
        if not taken:
            self.take(2)
        self.add((0, 2), (2,))
        self.send(6)

    def arrive(self, taken=False):
        self.take(*((5, 6) if taken else (3, 4, 5, 6)))


class CrossSum(SumRelay):
    routes = (
        ((1, 1), (0, 1)), ((1, -1), (0, -1)), ((1, 2), (0, 2)),
        ((0, 1), (0, 1)), ((0, -1), (0, -1)), ((0, 2), (0, 2)), ((1, 0), (1, 0)),
    )
    slots = (0, 1, 2, 3, 4, 5, 6)
    final = (3, 4, 5, 6)

    def start(self):
        self.send(0, 1, 2, 3, 4, 5)

    def relay(self):
        self.take(0, 1, 2)
        self.add((1, 0), (0, 1, 2))
        self.send(6)

    def arrive(self):
        self.take(3, 4, 5, 6)


class FarGather(Relay):
    routes = (
        ((0, 0), (1, 0)), ((0, 0), (0, 1)), ((0, 0), (0, -1)), ((0, 0), (0, 2)),
        ((1, 0), (0, 1)), ((1, 0), (0, -1)), ((0, 2), (1, 0)),
    )

    def __init__(self, grid, place, ssem, rsem):
        super().__init__(grid, ssem, rsem)
        self.source = place

    def target(self, i, block):
        return self.source(block)

    def start(self):
        self.send(0, 1, 2, 3)

    def relay(self):
        self.take(0)
        self.send(4, 5)
        self.take(3)
        self.send(6)

    def arrive(self):
        self.take(1, 2, 4, 5, 6)


class MateSum:
    def __init__(self, source, own, into, ssem, rsem, lsem=None):
        self.source, self.own, self.into = source, own, into
        self.ssem, self.rsem, self.lsem = ssem, rsem, lsem

    def out(self, k):
        core = lax.rem(lax.axis_index("wide"), 2)
        return remote(
            self.source(2 * k + 1 - core), self.into(k), self.ssem.at[k], self.rsem.at[k], mate_of()
        )

    def start(self):
        def per_block(k, carry):
            self.out(k).start()
            return carry

        lax.fori_loop(0, 8, per_block, 0)

    def add(self):
        core = lax.rem(lax.axis_index("wide"), 2)

        def per_block(k, carry):
            self.out(k).wait_recv()
            self.own(k)[...] = (
                self.source(2 * k + core)[...].astype(f32) + self.into(k)[...].astype(f32)
            ).astype(bf16)
            return carry

        lax.fori_loop(0, 8, per_block, 0)

    def drain(self):
        def per_block(k, carry):
            self.out(k).wait_send()
            return carry

        lax.fori_loop(0, 8, per_block, 0)


def swap_halves(u):
    half = HD // 2
    width = u.shape[-1]
    lane = lax.broadcasted_iota(jnp.int32, u.shape, u.ndim - 1)
    ahead = pltpu.roll(u, width - half, u.ndim - 1)
    behind = pltpu.roll(u, half, u.ndim - 1)
    return jnp.where(lax.rem(lane, HD) < half, ahead, behind)


def inverse_rms(values):
    return lax.rsqrt(jnp.mean(values * values, axis=-1, keepdims=True) + norm_eps)


def head_lanes(pair, odd, high):
    lane = lax.broadcasted_iota(jnp.int32, pair.shape, 1)
    if odd != high:
        pair = pltpu.roll(pair, HD, 1)
    return jnp.where((lane >= HD) == high, pair, 0.0)


def pair_lanes(even, odd):
    lane = lax.broadcasted_iota(jnp.int32, even.shape, 1)
    return jnp.where(lane < HD, even, pltpu.roll(odd, HD, 1))


class Item:
    def __init__(self, tree, grid, part, into, ssem, rsem, mates=None):
        self.tree = tree(grid, part, lambda slot: into.at[slot], ssem, rsem)
        self.mates = mates

    def finish(self, out_ref):
        self.tree.arrive()
        height, breadth = out_ref.shape
        span = max(8, min(height, 32768 // breadth))

        def per_tile(j, squares):
            rows = tile(j, span)
            total = self.tree.total(rows)
            out_ref[rows, :] = total
            return squares + jnp.sum(total * total, axis=0, keepdims=True)

        squares = lax.fori_loop(0, height // span, per_tile, jnp.zeros((1, breadth), f32))
        return jnp.sum(squares, axis=1, keepdims=True)

    def drain(self):
        self.tree.drain()
        if self.mates is not None:
            self.mates.drain()


def key_block(kv, j, bucket, length):
    rows = kv.shape[1] // 2
    block = kv[pl.ds(2 * j, 2), pl.ds(bucket * rows, rows), :].reshape(2 * rows, 2 * HD)
    lane = lax.broadcasted_iota(jnp.int32, block.shape, 1)
    key = 2 * rows * j + lax.broadcasted_iota(jnp.int32, block.shape, 0)
    bias = jnp.where(key < length, 0.0, masked_score)
    masked = jnp.where(lane < HD, block.astype(f32), jnp.where(lane == HD, bias, 0.0)).astype(bf16)
    return block, masked


def head_stack(values, heads, high):
    return jnp.concatenate(
        [
            head_lanes(values[:, (head // 2) * 2 * HD : (head // 2 + 1) * 2 * HD], head % 2 == 1, high)
            for head in range(heads)
        ],
        axis=0,
    )


def forward_kernel(
    len_ref, tok_ref, gains_ref, wkv_ref, tab0, tab1, tab2, tab3, tab4, wq_hbm, wo_hbm, wgu_hbm, wd_hbm,
    cot_hbm,
    log_ref, dh_ref, gain_ref, dob_ref, gout_ref, down_ref, squares_ref,
    n1_hbm, kv_hbm, qs_hbm, os_hbm, hidden_hbm, part_hbm, into_hbm, pgate_hbm, pup_hbm,
    wq_ref, qs_ref, os_ref, hidden_ref, mixed_ref,
    wo, wgu, wd, dyb, n1, kv, q, qm, ob, om, da, n2, dgu, dhb, part1, part2, into1, into2,
    mate_gu, mate_d, gdn, idown,
    in_sem, out_sem, st_sem, kv_s, kv_r, km_s, km_r, ex_s, ex_r, rs_s, rs_r, ag_s, ag_r, mt_s, mt_r, it_s, it_r,
):
    narrow, wide = Grid("narrow"), Grid("wide")
    me, wide_me = narrow.narrow_me, narrow.wide_me
    core = wide.core
    chip = lax.div(wide_me, 2)
    last_chip = lax.axis_size("wide") // 2 - 1
    mate, mirror = mate_of(), mirror_of()
    tokens, width = tok_ref.shape
    rows = tokens // 2
    half = rows // 2
    share = rows // lax.axis_size("narrow")
    units = wd.shape[0]
    heads = wo.shape[0] // HD
    span = 256
    loads = [
        pltpu.make_async_copy(src, dst, in_sem.at[i])
        for i, (src, dst) in enumerate(
            ((wo_hbm, wo), (cot_hbm, dyb), (wd_hbm, wd), (wgu_hbm, wgu), (wq_hbm, wq_ref))
        )
    ]
    partners = narrow.neighbours() + wide.neighbours() + [mate, mirror]
    greet(partners)
    for i in (4, 1, 0, 2, 3):
        loads[i].start()

    def normed(j, carry):
        at = tile(j, 64)
        values = tok_ref[at, :].astype(f32)
        n1[at, :] = (values * inverse_rms(values) * gains_ref[0:1, :].astype(f32)).astype(bf16)
        return carry

    cosine, sine = rotation((tab0, tab1, tab2, tab3, tab4), wide_me, 0, rows)

    def own_keys(b):
        lax.fori_loop(b * rows // 64, (b + 1) * rows // 64, normed, 0)
        mine = pl.ds(b * rows, rows)
        value = dot_nt(n1[mine, :], wkv_ref[...])
        lane = lax.broadcasted_iota(jnp.int32, value.shape, 1)
        turned = value * cosine + swap_halves(value) * sine
        kv[wide_me, mine, :] = jnp.where(lane < HD, turned, value).astype(bf16)

    own_keys(0)
    met(partners)

    def keys_at(b):
        bucket = pl.ds(b * rows, rows)
        return lambda block: kv.at[2 * block + core, bucket, :]

    keys = [FarGather(wide, keys_at(b), kv_s.at[b], kv_r.at[b]) for b in range(2)]

    def to_mate(b, block, i):
        ref = keys_at(b)(block)
        return remote(ref, ref, km_s.at[b, i], km_r.at[b, i], mate)

    keys[0].start()
    to_mate(0, chip, 7).start()
    own_keys(1)
    cosine, sine = jnp.concatenate([cosine] * 2, axis=0), jnp.concatenate([sine] * 2, axis=0)
    loads[4].wait()
    for pair in range(heads // 2):
        columns = pl.ds(pair * 2 * HD, 2 * HD)
        value = dot_nn(n1[...], wq_ref[:, columns])
        q[:, columns] = ((value * cosine + swap_halves(value) * sine) * HD**-0.5).astype(bf16)

    def later(bucket):
        return pl.ds(bucket * rows + half, half)

    queries = [
        remote(q.at[later(b), :], qm.at[b], ex_s.at[0, b], ex_r.at[0, b], mirror) for b in range(2)
    ]
    for copy in queries:
        copy.start()

    def store(src, dst, i):
        return pltpu.make_async_copy(src, dst, out_sem.at[i])

    store(n1, n1_hbm, 0).start()
    relayed = [
        wide.block(*where) for where in ((1, 0), (0, 2), (0, -1), (0, 1), (1, -1), (1, 1), (1, 2))
    ]

    def keys_relay(b):
        keys[b].relay()
        for i in range(2):
            to_mate(b, relayed[i], i).start()

    def keys_arrive(b):
        keys[b].arrive()
        for i in range(2, 7):
            to_mate(b, relayed[i], i).start()

    def keys_complete(b):
        for i in range(7):
            to_mate(b, relayed[i], i).wait_recv()
        to_mate(b, chip, 7).wait_recv()

    def stack_queries(b, g):
        held = (q[pl.ds(b * rows, half), :] if g == 0 else qm[b]).astype(f32)
        stack = head_stack(held, heads, False)
        lane = lax.broadcasted_iota(jnp.int32, stack.shape, 1)
        qs_ref[b, g] = jnp.where(lane == HD, 1.0, stack).astype(bf16)

    for b in range(2):
        stack_queries(b, 0)
    keys_relay(0)
    keys[1].start()
    to_mate(1, chip, 7).start()
    loads[1].wait()
    for b in range(2):
        place = wide_me * rows + lax.broadcasted_iota(jnp.int32, (rows, 1), 0)
        mine = pl.ds(b * rows, rows)
        live = (place < len_ref[b]).astype(f32)
        dyb[mine, :] = (dyb[mine, :].astype(f32) * live).astype(bf16)
    loads[2].wait()

    def grad_middle(j, carry):
        da[:, tile(j, span)] = dot_nt(dyb[...], wd[tile(j, span), :])
        return carry

    lax.fori_loop(0, units // span, grad_middle, 0)
    for b in range(2):
        queries[b].wait_recv()
        stack_queries(b, 1)
    keys_arrive(0)
    keys_relay(1)

    stack_rows = heads * half

    def attention(b, g):
        length = len_ref[b]
        final = chip if g == 0 else last_chip - chip
        first = wide_me * rows if g == 0 else (2 * last_chip + 1 - wide_me) * rows + half

        def step(masked, j, carry):
            block, scored = key_block(kv, j, b, length)
            lane = lax.broadcasted_iota(jnp.int32, block.shape, 1)
            summed = jnp.where(lane < HD, jnp.ones_like(block), block)
            scores = dot_nt(qs_ref[b, g], scored)
            if masked:
                key = 2 * rows * j + lax.broadcasted_iota(jnp.int32, scores.shape, 1)
                place = first + lax.rem(lax.broadcasted_iota(jnp.int32, scores.shape, 0), half)
                scores = jnp.where(key <= place, scores, masked_score)
            best, total = carry
            new_best = jnp.maximum(best, jnp.max(scores, axis=-1, keepdims=True))
            weights = jnp.exp(scores - new_best).astype(bf16)
            return new_best, total * jnp.exp(best - new_best) + dot_nn(weights, summed)

        carry = (jnp.full((stack_rows, 1), masked_score, f32), jnp.zeros((stack_rows, 2 * HD), f32))
        carry = lax.fori_loop(0, final, functools.partial(step, False), carry)
        best, total = step(True, final, carry)
        lane = lax.broadcasted_iota(jnp.int32, total.shape, 1)
        sums = jnp.where(lane < HD, total, pltpu.roll(total, HD, 1))
        os_ref[b, g] = total / sums
        logs = jnp.transpose(best + jnp.log(sums))
        log_ref[pl.ds(2 * b + g, 1), :] = logs[0:1, :]
        for pair in range(heads // 2):
            even = os_ref[b, g, pl.ds(2 * pair * half, half), :]
            odd = os_ref[b, g, pl.ds((2 * pair + 1) * half, half), :]
            value = pair_lanes(pltpu.roll(even, HD, 1), pltpu.roll(odd, HD, 1)).astype(bf16)
            columns = pl.ds(pair * 2 * HD, 2 * HD)
            if g == 0:
                ob[pl.ds(b * rows, half), columns] = value
            else:
                om[b, :, columns] = value

    def back_to_mirror(b):
        return remote(om.at[b], ob.at[later(b), :], ex_s.at[1, b], ex_r.at[1, b], mirror)

    def mine_in(b):
        return pl.ds(pl.multiple_of(b * rows + me * share, share), share)

    def their_rows(b):
        return lambda block: pl.ds(pl.multiple_of(b * rows + block * share, share), share)

    def sum_of(b, part, into, number):
        where = their_rows(b)
        return FarSum(
            narrow, lambda block: part.at[where(block), :], lambda slot: into.at[b, slot],
            rs_s.at[number, b], rs_r.at[number, b],
        )

    def gather_of(b, buffer, number):
        where = their_rows(b)
        return FarGather(
            narrow, lambda block: buffer.at[where(block), :], ag_s.at[number, b], ag_r.at[number, b]
        )

    whole = pl.ds(0, share)
    sums1 = [sum_of(b, part1, into1, 0) for b in range(2)]
    sums2 = [sum_of(b, part2, into2, 1) for b in range(2)]
    sums3 = [sum_of(b, part1, into1, 2) for b in range(2)]
    gather1 = [gather_of(b, n2, 0) for b in range(2)]
    gather2 = [gather_of(b, dhb, 1) for b in range(2)]

    def project(b):
        back_to_mirror(b).wait_recv()
        mine = pl.ds(b * rows, rows)
        part1[mine, :] = dot_nn(ob[mine, :], wo[...]).astype(bf16)
        sums1[b].start()

    keys_complete(0)
    attention(0, 1)
    back_to_mirror(0).start()
    keys_arrive(1)
    attention(0, 0)
    loads[0].wait()
    project(0)
    keys_complete(1)
    store(kv, kv_hbm, 1).start()
    attention(1, 1)
    back_to_mirror(1).start()
    attention(1, 0)
    store(os_ref, os_hbm, 2).start()
    store(qs_ref, qs_hbm, 3).start()
    project(1)
    sums1[0].relay()
    sums1[1].relay()
    gain2 = gains_ref[1:2, :].astype(f32)
    gain_ref[...] = jnp.zeros(gain_ref.shape, f32)

    def second_norm(b):
        sums1[b].arrive()
        hidden = tok_ref[mine_in(b), :].astype(f32) + sums1[b].total(whole)
        hidden_ref[b] = hidden
        n2[mine_in(b), :] = (hidden * inverse_rms(hidden) * gain2).astype(bf16)
        gather1[b].start()

    second_norm(0)
    second_norm(1)
    loads[3].wait()
    gather1[0].relay()
    gather1[1].relay()

    def feed(b):
        gather1[b].arrive()
        mine = pl.ds(b * rows, rows)

        def gate_up(j, carry):
            columns = tile(j, span)
            gate = dot_nn(n2[mine, :], wgu[0, :, columns])
            up = dot_nn(n2[mine, :], wgu[1, :, columns])
            sigmoid = jax.nn.sigmoid(gate)
            activated = gate * sigmoid
            mixed_ref[mine, columns] = (activated * up).astype(bf16)
            grad = da[mine, columns]
            dgu[0, mine, columns] = (
                grad * up * sigmoid * (1.0 + gate * (1.0 - sigmoid))
            ).astype(bf16)
            dgu[1, mine, columns] = (grad * activated).astype(bf16)
            return carry

        lax.fori_loop(0, units // span, gate_up, 0)

        def grad_norm_two(c, carry):
            columns = tile(c, 512)
            part2[mine, columns] = (
                dot_nt(dgu[0, mine, :], wgu[0, columns, :]) + dot_nt(dgu[1, mine, :], wgu[1, columns, :])
            ).astype(bf16)
            return carry

        lax.fori_loop(0, width // 512, grad_norm_two, 0)
        sums2[b].start()

    feed(0)
    feed(1)
    store(hidden_ref, hidden_hbm, 4).start()
    wide_share = width // 16
    mates = [
        MateSum(
            lambda w, i=i: wgu.at[i, tile(w, wide_share), :],
            lambda k, i=i: wgu.at[i, tile(2 * k + core, wide_share), :],
            lambda k, i=i: mate_gu.at[i, k], mt_s.at[i], mt_r.at[i],
        )
        for i in range(2)
    ]
    mates.append(
        MateSum(
            lambda w: gdn.at[w], lambda k: gdn.at[2 * k + core], lambda k: mate_d.at[k],
            mt_s.at[2], mt_r.at[2],
        )
    )
    down = Item(
        CrossSum, wide, mates[2].own, idown, it_s, it_r, mates[2]
    )

    def grad_down(j, carry):
        found = dot_tn(mixed_ref[:, tile(j, span)], dyb[...]).astype(bf16)
        for w in range(16):
            gdn[w, tile(j, span), :] = found[:, w * wide_share : (w + 1) * wide_share]
        return carry

    def grad_gateup(which):
        def per_tile(j, carry):
            wgu[which, tile(j, span), :] = dot_tn(n2[:, tile(j, span)], dgu[which]).astype(bf16)
            return carry

        lax.fori_loop(0, width // span, per_tile, 0)

    def second_norm_back(b):
        sums2[b].arrive()
        total = sums2[b].total(whole)
        hidden = hidden_ref[b]
        inverse = inverse_rms(hidden)
        z2 = hidden * inverse
        gain_ref[pl.ds(b, 1), :] = jnp.sum(total * z2, axis=0, keepdims=True)
        weighted = total * gain2
        dh = dyb[mine_in(b), :].astype(f32) + inverse * (
            weighted - z2 * jnp.mean(weighted * z2, axis=-1, keepdims=True)
        )
        dh_ref[b] = dh
        dhb[mine_in(b), :] = dh.astype(bf16)
        gather2[b].start()

    def kept(which, out_hbm, k):
        return pltpu.make_async_copy(mates[which].own(k), out_hbm.at[k], st_sem.at[which, k])

    def keep(which, out_hbm):
        mates[which].add()

        def per_block(k, carry):
            kept(which, out_hbm, k).start()
            return carry

        lax.fori_loop(0, 8, per_block, 0)

    def feed_down(c, carry):
        part1[:, tile(c, 512)] = dot_nn(mixed_ref[...], wd[:, tile(c, 512)]).astype(bf16)
        return carry

    def grad_heads(b):
        gather2[b].arrive()
        mine = pl.ds(b * rows, rows)
        dob_ref[mine, :] = dot_nt(dhb[mine, :], wo[...]).astype(bf16)

    def grad_out(j, carry):
        gout_ref[:, tile(j, span)] = dot_tn(ob[...], dhb[:, tile(j, span)]).astype(bf16)
        return carry

    sums2[0].relay()
    lax.fori_loop(0, units // span, grad_down, 0)
    mates[2].start()
    grad_gateup(0)
    mates[0].start()
    sums2[1].relay()
    second_norm_back(0)
    mates[2].add()
    down.tree.start()
    sums1[0].drain()
    sums1[1].drain()
    lax.fori_loop(0, width // 512, feed_down, 0)
    second_norm_back(1)
    gather2[0].relay()
    store(part1, part_hbm, 5).start()
    grad_gateup(1)
    mates[1].start()
    gather2[1].relay()
    for b in EARLY:
        sums3[b].start()
    keep(0, pgate_hbm)
    down.tree.relay()
    grad_heads(0)
    grad_heads(1)
    lax.fori_loop(0, width // span, grad_out, 0)
    keep(1, pup_hbm)
    squares_ref[...] = jnp.broadcast_to(down.finish(down_ref), squares_ref.shape)
    for b in EARLY:
        sums3[b].take(0, 1, 2, 3, 4)
        sums3[b].drain(range(5))
        store(into1.at[b, pl.ds(0, 5)], into_hbm.at[b], 6 + b).start()
    for b in range(2):
        sums2[b].drain()
        gather1[b].drain()
        gather2[b].drain()
        queries[b].wait_send()
        back_to_mirror(b).wait_send()
        keys[b].drain()
        for i in range(7):
            to_mate(b, relayed[i], i).wait_send()
        to_mate(b, chip, 7).wait_send()
    down.drain()
    mates[0].drain()
    mates[1].drain()
    for i, (src, dst) in enumerate(
        ((n1, n1_hbm), (kv, kv_hbm), (os_ref, os_hbm), (qs_ref, qs_hbm), (hidden_ref, hidden_hbm),
         (part1, part_hbm))
    ):
        store(src, dst, i).wait()
    for b in EARLY:
        store(into1.at[b, pl.ds(0, 5)], into_hbm.at[b], 6 + b).wait()
    for which, out_hbm in ((0, pgate_hbm), (1, pup_hbm)):
        def per_store(k, carry):
            kept(which, out_hbm, k).wait()
            return carry

        lax.fori_loop(0, 8, per_store, 0)


def forward(lengths, tokens, gains, wkv, tables, wq, wo, wgu, wd, cotangent):
    count, width = tokens.shape
    rows = count // 2
    share = rows // 8
    units = wd.shape[0]
    lanes = wq.shape[1]
    heads = lanes // HD
    stack = heads * rows // 2
    wide_count = 16
    wide_share = width // wide_count
    here = pl.BlockSpec(memory_space=pltpu.VMEM)
    anywhere = pl.BlockSpec(memory_space=pl.ANY)
    shape = jax.ShapeDtypeStruct
    dma = pltpu.SemaphoreType.DMA
    vmem = pltpu.VMEM
    return pl.pallas_call(
        forward_kernel,
        out_shape=(
            shape((8, stack), f32),
            shape((2, share, width), f32),
            shape((8, width), f32),
            shape((count, lanes), bf16),
            shape((lanes, width), bf16),
            shape((units, wide_share), f32),
            shape((8, wide_share), f32),
            shape((count, width), bf16),
            shape((wide_count, count, 2 * HD), bf16),
            shape((2, 2, stack, 2 * HD), bf16),
            shape((2, 2, stack, 2 * HD), f32),
            shape((2, share, width), f32),
            shape((count, width), bf16),
            shape((2, 5, share, width), bf16),
            shape((8, wide_share, units), bf16),
            shape((8, wide_share, units), bf16),
        ),
        in_specs=[pl.BlockSpec(memory_space=pltpu.SMEM)] + [here] * 8 + [anywhere] * 5,
        out_specs=(here,) * 7 + (anywhere,) * 9,
        scratch_shapes=[
            vmem(wq.shape, bf16),
            vmem((2, 2, stack, 2 * HD), bf16),
            vmem((2, 2, stack, 2 * HD), f32),
            vmem((2, share, width), f32),
            vmem((count, units), bf16),
            vmem(wo.shape, bf16),
            vmem(wgu.shape, bf16),
            vmem(wd.shape, bf16),
            vmem((count, width), bf16),
            vmem((count, width), bf16),
            vmem((wide_count, count, 2 * HD), bf16),
            vmem((count, lanes), bf16),
            vmem((2, rows // 2, lanes), bf16),
            vmem((count, lanes), bf16),
            vmem((2, rows // 2, lanes), bf16),
            vmem((count, units), f32),
            vmem((count, width), bf16),
            vmem((2, count, units), bf16),
            vmem((count, width), bf16),
            vmem((count, width), bf16),
            vmem((count, width), bf16),
            vmem((2, SLOTS, share, width), bf16),
            vmem((2, SLOTS, share, width), bf16),
            vmem((2, 8, wide_share, units), bf16),
            vmem((8, units, wide_share), bf16),
            vmem((wide_count, units, wide_share), bf16),
            vmem((SLOTS, units, wide_share), bf16),
            dma((5,)),
            dma((8,)),
            dma((2, 8)),
            dma((2, SLOTS)),
            dma((2, SLOTS)),
            dma((2, 8)),
            dma((2, 8)),
            dma((2, 2)),
            dma((2, 2)),
            dma((3, 2, SLOTS)),
            dma((3, 2, SLOTS)),
            dma((2, 2, SLOTS)),
            dma((2, 2, SLOTS)),
            dma((3, 8)),
            dma((3, 8)),
            dma((SLOTS,)),
            dma((SLOTS,)),
        ],
        compiler_params=pltpu.CompilerParams(
            collective_id=1, has_side_effects=True, vmem_limit_bytes=63 * MB
        ),
        name="forward",
    )(lengths, tokens, gains, wkv, *tables, wq, wo, wgu, wd, cotangent)


def backward_kernel(
    len_ref, gains_ref, tab0, tab1, tab2, tab3, tab4, log_ref, gain2_ref, dob_ref, squares_ref,
    qs_ref, os_ref, tok_hbm, wq_hbm, wkv_hbm, hidden_hbm, dh_hbm, gout_hbm, kv_hbm, n1_hbm, part_hbm, into_hbm,
    pgate_hbm, pup_hbm,
    q_ref, pair_ref, out_ref, gate_ref, up_ref, gains_out_ref, norm_ref, layer_hbm, grad_hbm,
    layer_ref, grad_ref, wq_ref, wkv_ref, hidden_ref, dh_ref, gout_ref, cos_ref, sin_ref, pgate, igate,
    kv, n1, tok, pup, pout, pq, pkv, iup, iout, iq, ikv,
    mout, mq, mkv, gq, gkv, part3, part4, into3, into4, acc, dkv, dkm, dkin, dkv_low, dq, dqm, dm,
    dos, qclean, delta, dqacc, grow, gpart, gnear, gwide, pair,
    ld_sem, out_sem, rs_s, rs_r, ag_s, ag_r, dm_s, dm_r, dt_s, dt_r, im_s, im_r, it_s, it_r, ex_s, ex_r,
    g_s, g_r, h_s, h_r,
):
    narrow, wide = Grid("narrow"), Grid("wide")
    me, wide_me = narrow.narrow_me, narrow.wide_me
    core = wide.core
    chip = lax.div(wide_me, 2)
    last_chip = lax.axis_size("wide") // 2 - 1
    peers = lax.axis_size("narrow")
    mate, mirror = mate_of(), mirror_of()
    tokens, width = layer_ref.shape
    rows = tokens // 2
    half = rows // 2
    share = rows // peers
    heads = wq_ref.shape[1] // HD
    span = 256
    wide_share = width // 16

    def mine_in(b):
        return pl.ds(pl.multiple_of(b * rows + me * share, share), share)

    def later(b):
        return pl.ds(b * rows + half, half)

    moves = (
        (kv_hbm, kv), (part_hbm, part3), (pup_hbm, pup), (n1_hbm, n1),
        (tok_hbm.at[mine_in(0), :], tok.at[0]), (tok_hbm.at[mine_in(1), :], tok.at[1]),
        (pgate_hbm, pgate), (gout_hbm, gout_ref), (hidden_hbm, hidden_ref), (wq_hbm, wq_ref),
        (wkv_hbm, wkv_ref), (dh_hbm, dh_ref), (into_hbm.at[0], into3.at[0, pl.ds(0, 5)]),
        (into_hbm.at[1], into3.at[1, pl.ds(0, 5)]),
    )
    loads = [pltpu.make_async_copy(src, dst, ld_sem.at[i]) for i, (src, dst) in enumerate(moves)]
    partners = others_of("narrow") + others_of("wide")
    greet(partners)
    waits_early = [12 + b for b in EARLY]
    for i in [1] + waits_early + [0, 2, 6, 7, 8, 9, 10, 3, 4, 5, 11]:
        loads[i].start()
    tables = (tab0, tab1, tab2, tab3, tab4)
    cos_ref[pl.ds(0, rows), :], sin_ref[pl.ds(0, rows), :] = rotation(tables, wide_me, 0, rows)
    cos_ref[pl.ds(rows, half), :], sin_ref[pl.ds(rows, half), :] = rotation(
        tables, 2 * last_chip + 1 - wide_me, half, half
    )
    met(partners)

    grads_there = [
        remote(dob_ref.at[later(b), :], dm.at[b], ex_s.at[0, b], ex_r.at[0, b], mirror) for b in range(2)
    ]
    for copy in grads_there:
        copy.start()

    def mates_of(source, own, into, number):
        return MateSum(
            source, lambda k: own.at[k], lambda k: into.at[k], im_s.at[number], im_r.at[number]
        )

    up = Item(FarSum, wide, lambda b: pup.at[b], iup, it_s.at[0], it_r.at[0])
    gate = Item(FarSum, wide, lambda b: pgate.at[b], igate, it_s.at[4], it_r.at[4])
    out = Item(
        FarSum, wide, lambda b: pout.at[b], iout, it_s.at[1], it_r.at[1],
        mates_of(lambda w: gout_ref.at[:, tile(w, wide_share)], pout, mout, 0),
    )
    query = Item(
        FarSum, wide, lambda b: pq.at[b], iq, it_s.at[2], it_r.at[2],
        mates_of(lambda w: gq.at[tile(w, wide_share), :], pq, mq, 1),
    )
    keyval = Item(
        FarSum, wide, lambda b: pkv.at[b], ikv, it_s.at[3], it_r.at[3],
        mates_of(lambda w: gkv.at[tile(w, wide_share), :], pkv, mkv, 2),
    )
    def their_rows(b):
        return lambda block: pl.ds(pl.multiple_of(b * rows + block * share, share), share)

    def sum_of(kind, b, part, into, number):
        where = their_rows(b)
        return kind(
            narrow, lambda block: part.at[where(block), :], lambda slot: into.at[b, slot],
            rs_s.at[number, b], rs_r.at[number, b],
        )

    def gather_of(kind, b, buffer, number):
        where = their_rows(b)
        return kind(
            narrow, lambda block: buffer.at[where(block), :], ag_s.at[number, b], ag_r.at[number, b]
        )

    whole = pl.ds(0, share)
    sums3 = [sum_of(FarSum, b, part3, into3, 0) for b in range(2)]
    sums4 = [sum_of(FarSum, b, part4, into4, 1) for b in range(2)]
    gather3 = [gather_of(FarGather, b, layer_ref, 0) for b in range(2)]
    gather4 = [gather_of(FarGather, b, grad_ref, 1) for b in range(2)]

    loads[1].wait()
    for b in range(2):
        if b in EARLY:
            loads[12 + b].wait()
            sums3[b].relay(taken=True)
        else:
            sums3[b].start()
    for i, item in ((2, up), (6, gate)):
        loads[i].wait()
        item.tree.start()
    loads[7].wait()
    out.mates.start()
    loads[0].wait()
    stack_rows = heads * half

    def attention(b, g):
        length = len_ref[b]
        final = chip if g == 0 else last_chip - chip
        first = wide_me * rows if g == 0 else (2 * last_chip + 1 - wide_me) * rows + half
        held = (dob_ref[pl.ds(b * rows, half), :] if g == 0 else dm[b]).astype(f32)
        stack = head_stack(held, heads, True)
        dos[...] = stack.astype(bf16)
        delta[...] = jnp.sum(jnp.transpose(stack * os_ref[b, g]), axis=0, keepdims=True)
        lane = lax.broadcasted_iota(jnp.int32, qclean.shape, 1)
        qclean[...] = jnp.where(lane < HD, qs_ref[b, g].astype(f32), 0.0).astype(bf16)
        both = jnp.concatenate([qclean[...], dos[...]], axis=0)
        dqacc[...] = jnp.zeros(dqacc.shape, f32)

        def step(masked, j, carry):
            block, scored = key_block(kv, j, b, length)
            scores = dot_nt(scored, qs_ref[b, g])
            if masked:
                key = 2 * rows * j + lax.broadcasted_iota(jnp.int32, scores.shape, 0)
                place = first + lax.rem(lax.broadcasted_iota(jnp.int32, scores.shape, 1), half)
                scores = jnp.where(key <= place, scores, masked_score)
            chances = jnp.exp(scores - log_ref[pl.ds(2 * b + g, 1), :])
            slope = (chances * (dot_nt(block, dos[...]) - delta[...])).astype(bf16)
            acc[j] = acc[j] + dot_nn(jnp.concatenate([slope, chances.astype(bf16)], axis=1), both)
            dqacc[...] = dqacc[...] + dot_tn(slope, block)
            return carry

        lax.fori_loop(0, final, functools.partial(step, False), 0)
        step(True, final, 0)
        for pair in range(heads // 2):
            even = dqacc[pl.ds(2 * pair * half, half), :]
            odd = dqacc[pl.ds((2 * pair + 1) * half, half), :]
            value = pair_lanes(even, odd) * HD**-0.5
            table = pl.ds(0, half) if g == 0 else pl.ds(rows, half)
            value = (value * cos_ref[table, :] - swap_halves(value) * sin_ref[table, :]).astype(bf16)
            columns = pl.ds(pair * 2 * HD, 2 * HD)
            if g == 0:
                dq[pl.ds(b * rows, half), columns] = value
            else:
                dqm[b, :, columns] = value

    def query_back(b):
        return remote(dqm.at[b], dq.at[later(b), :], ex_s.at[1, b], ex_r.at[1, b], mirror)

    def clear():
        def per_block(j, carry):
            acc[j] = jnp.zeros(acc.shape[1:], f32)
            return carry

        lax.fori_loop(0, acc.shape[0], per_block, 0)

    pair_mates = [
        MateSum(
            lambda w, b=b: dkv.at[b, w], lambda k, b=b: dkv.at[b, 2 * k + core],
            lambda k, b=b: dkm.at[b, k], dm_s.at[b], dm_r.at[b],
        )
        for b in range(2)
    ]
    pair_trees = [
        FarSum(
            wide, lambda block, b=b: dkv.at[b, 2 * block + core], lambda slot, b=b: dkin.at[b, slot],
            dt_s.at[b], dt_r.at[b],
        )
        for b in range(2)
    ]

    def pair_relay(b):
        pair_trees[b].relay()

    def pair_send(b):
        def per_block(j, carry):
            dkv[b, pl.ds(2 * j, 2)] = acc[j].astype(bf16).reshape(2, rows, 2 * HD)
            return carry

        lax.fori_loop(0, acc.shape[0], per_block, 0)
        pair_mates[b].start()

    def pair_mid(b):
        pair_mates[b].add()
        pair_trees[b].start()

    def pair_total(b):
        pair_trees[b].arrive()
        total = pair_trees[b].total(pl.ds(0, rows))
        mine = pl.ds(b * rows, rows)
        lane = lax.broadcasted_iota(jnp.int32, total.shape, 1)
        table = pl.ds(0, rows)
        turned = total * cos_ref[table, :] - swap_halves(total) * sin_ref[table, :]
        dkv_low[mine, :] = jnp.where(lane < HD, turned, total).astype(bf16)

    def norm_one_back(b):
        mine = pl.ds(b * rows, rows)

        def per_chunk(c, carry):
            columns = tile(c, 512)
            part4[mine, columns] = (
                dot_nt(dq[mine, :], wq_ref[columns, :]) + dot_nn(dkv_low[mine, :], wkv_ref[:, columns])
            ).astype(bf16)
            return carry

        lax.fori_loop(0, width // 512, per_chunk, 0)
        sums4[b].start()

    def result_rows(b):
        sums3[b].arrive(taken=b in EARLY)
        layer_ref[mine_in(b), :] = (hidden_ref[b] + sums3[b].total(whole)).astype(bf16)
        gather3[b].start()

    gains1 = gains_ref[0:1, :].astype(f32)

    def input_rows(b):
        sums4[b].arrive()
        total = sums4[b].total(whole)
        values = tok[b].astype(f32)
        inverse = inverse_rms(values)
        z1 = values * inverse
        weighted = total * gains1
        grad_ref[mine_in(b), :] = (
            dh_ref[b] + inverse * (weighted - z1 * jnp.mean(weighted * z1, axis=-1, keepdims=True))
        ).astype(bf16)
        grow[pl.ds(b, 1), :] = jnp.sum(total * z1, axis=0, keepdims=True)

    clear()
    attention(0, 0)
    for copy in grads_there:
        copy.wait_recv()
    attention(0, 1)
    query_back(0).start()
    pair_send(0)
    if 0 not in EARLY:
        sums3[0].relay()
    if 1 not in EARLY:
        sums3[1].relay()
    clear()
    attention(1, 1)
    query_back(1).start()
    pair_mid(0)
    loads[8].wait()
    result_rows(0)
    result_rows(1)
    up.tree.relay()
    attention(1, 0)
    pair_send(1)
    pair_relay(0)
    loads[9].wait()
    loads[10].wait()
    pair_mid(1)
    pair_total(0)
    query_back(0).wait_recv()
    norm_one_back(0)
    gather3[0].relay()
    gather3[1].relay()
    query_back(1).wait_recv()
    loads[3].wait()

    def grad_query(j, carry):
        gq[tile(j, span), :] = dot_tn(n1[:, tile(j, span)], dq[...]).astype(bf16)
        return carry

    pair_relay(1)
    lax.fori_loop(0, width // span, grad_query, 0)
    query.mates.start()
    sums4[0].relay()
    pair_total(1)
    norm_one_back(1)

    def grad_keyval(j, carry):
        gkv[tile(j, span), :] = dot_tn(n1[:, tile(j, span)], dkv_low[...]).astype(bf16)
        return carry

    query.mates.add()
    query.tree.start()
    gate.tree.relay()
    out.mates.add()
    out.tree.start()
    lax.fori_loop(0, width // span, grad_keyval, 0)
    keyval.mates.start()
    loads[4].wait()
    loads[5].wait()
    loads[11].wait()
    input_rows(0)
    gather4[0].start()
    keyval.mates.add()
    keyval.tree.start()
    sums4[1].relay()
    query.tree.relay()
    out.tree.relay()
    squares = squares_ref[0:1, 0:1] + up.finish(up_ref) + gate.finish(gate_ref)
    gather4[0].relay()
    keyval.tree.relay()
    input_rows(1)
    squares = squares + query.finish(q_ref) + out.finish(out_ref) + keyval.finish(pair)

    for w in range(16):
        lanes = pl.ds(w * wide_share, wide_share)
        gpart[pl.ds(w, 1), :] = grow[0:1, lanes] + grow[1:2, lanes]
        gpart[pl.ds(16 + w, 1), :] = gain2_ref[0:1, lanes] + gain2_ref[1:2, lanes]
    gpart[pl.ds(32, 8), :] = jnp.broadcast_to(squares, (8, wide_share))
    near_gains = [
        remote(gpart, gnear.at[i], h_s.at[i], h_r.at[i], there)
        for i, there in enumerate(others_of("narrow"))
    ]
    for copy in near_gains:
        copy.start()
    gather4[1].start()
    pair_ref[...] = jnp.transpose(pair[...])
    for copy in near_gains:
        copy.wait()
    total = gpart[...]
    for i in range(peers - 1):
        total = total + gnear[i]
    gpart[...] = total
    gain_copies = [
        remote(gpart, gwide.at[i], g_s.at[i], g_r.at[i], there)
        for i, there in enumerate(others_of("wide"))
    ]
    for copy in gain_copies:
        copy.start()
    gather4[1].relay()
    for b in range(2):
        gather3[b].arrive()
    layer_store = pltpu.make_async_copy(layer_ref, layer_hbm, out_sem.at[0])
    layer_store.start()
    for copy in gain_copies:
        copy.wait()
    total = gpart[...]
    for i in range(len(gain_copies)):
        total = total + gwide[i]
    gpart[...] = total
    row = lax.broadcasted_iota(jnp.int32, total.shape, 0)
    kept = jnp.where(row < 32, total, 0.0)
    gain_squares = jnp.sum(jnp.sum(kept * kept, axis=1, keepdims=True), axis=0, keepdims=True)
    norm_ref[...] = jnp.sqrt(total[32:40, :] + gain_squares)
    row = lax.broadcasted_iota(jnp.int32, gains_out_ref.shape, 0)
    gains_out_ref[...] = jnp.where(
        row == 0, gpart[pl.ds(wide_me, 1), :], gpart[pl.ds(16 + wide_me, 1), :]
    )
    for b in range(2):
        gather4[b].arrive()
    grad_store = pltpu.make_async_copy(grad_ref, grad_hbm, out_sem.at[1])
    grad_store.start()
    for b in range(2):
        sums3[b].drain((5, 6) if b in EARLY else range(7))
        for each in (sums4[b], gather3[b], gather4[b], pair_mates[b], pair_trees[b]):
            each.drain()
        grads_there[b].wait_send()
        query_back(b).wait_send()
    for item in (gate, up, out, query, keyval):
        item.drain()
    layer_store.wait()
    grad_store.wait()


def backward(
    lengths, gains, tables, logs, gain2, dob, squares, qs, outs, tokens, wq, wkv, hidden, dh, gout,
    kv, n1, part, into, pgate, pup,
):
    count, width = n1.shape
    rows = count // 2
    share = rows // 8
    units = pgate.shape[2]
    lanes = wq.shape[1]
    stack = qs.shape[2]
    wide_count = 16
    wide_share = width // wide_count
    here = pl.BlockSpec(memory_space=pltpu.VMEM)
    anywhere = pl.BlockSpec(memory_space=pl.ANY)
    shape = jax.ShapeDtypeStruct
    dma = pltpu.SemaphoreType.DMA
    vmem = pltpu.VMEM
    blocks = (
        (wide_share, units), (lanes, wide_share), (wide_share, lanes), (wide_share, 2 * HD),
    )
    return pl.pallas_call(
        backward_kernel,
        out_shape=(
            shape((wide_share, lanes), f32),
            shape((2 * HD, wide_share), f32),
            shape((lanes, wide_share), f32),
            shape((wide_share, units), f32),
            shape((wide_share, units), f32),
            shape((8, wide_share), f32),
            shape((8, wide_share), f32),
            shape((count, width), bf16),
            shape((count, width), bf16),
        ),
        in_specs=[pl.BlockSpec(memory_space=pltpu.SMEM)] + [here] * 12 + [anywhere] * 12,
        out_specs=(here,) * 7 + (anywhere,) * 2,
        scratch_shapes=[
            vmem((count, width), bf16),
            vmem((count, width), bf16),
            vmem(wq.shape, bf16),
            vmem(wkv.shape, bf16),
            vmem(hidden.shape, f32),
            vmem(dh.shape, f32),
            vmem(gout.shape, bf16),
            vmem((rows + rows // 2, 2 * HD), f32),
            vmem((rows + rows // 2, 2 * HD), f32),
            vmem(pgate.shape, bf16),
            vmem((SLOTS, wide_share, units), bf16),
            vmem(kv.shape, bf16),
            vmem((count, width), bf16),
            vmem((2, share, width), bf16),
            *[vmem((8, *block), bf16) for block in blocks],
            *[vmem((SLOTS, *block), bf16) for block in blocks],
            *[vmem((8, *block), bf16) for block in blocks[1:]],
            vmem((width, lanes), bf16),
            vmem((width, 2 * HD), bf16),
            vmem((count, width), bf16),
            vmem((count, width), bf16),
            vmem((2, SLOTS, share, width), bf16),
            vmem((2, SLOTS, share, width), bf16),
            vmem((8, 2 * rows, 2 * HD), f32),
            vmem((2, wide_count, rows, 2 * HD), bf16),
            vmem((2, 8, rows, 2 * HD), bf16),
            vmem((2, SLOTS, rows, 2 * HD), bf16),
            vmem((count, 2 * HD), bf16),
            vmem((count, lanes), bf16),
            vmem((2, rows // 2, lanes), bf16),
            vmem((2, rows // 2, lanes), bf16),
            vmem((stack, 2 * HD), bf16),
            vmem((stack, 2 * HD), bf16),
            vmem((1, stack), f32),
            vmem((stack, 2 * HD), f32),
            vmem((8, width), f32),
            vmem((40, wide_share), f32),
            vmem((7, 40, wide_share), f32),
            vmem((wide_count - 1, 40, wide_share), f32),
            vmem((wide_share, 2 * HD), f32),
            dma((14,)),
            dma((2,)),
            dma((2, 2, SLOTS)),
            dma((2, 2, SLOTS)),
            dma((2, 2, SLOTS)),
            dma((2, 2, SLOTS)),
            dma((2, 8)),
            dma((2, 8)),
            dma((2, SLOTS)),
            dma((2, SLOTS)),
            dma((3, 8)),
            dma((3, 8)),
            dma((5, SLOTS)),
            dma((5, SLOTS)),
            dma((2, 2)),
            dma((2, 2)),
            dma((wide_count - 1,)),
            dma((wide_count - 1,)),
            dma((7,)),
            dma((7,)),
        ],
        compiler_params=pltpu.CompilerParams(
            collective_id=2, has_side_effects=True, vmem_limit_bytes=63 * MB
        ),
        name="backward",
    )(
        lengths, gains, *tables, logs, gain2, dob, squares, qs, outs, tokens, wq, wkv, hidden, dh,
        gout, kv, n1, part, into, pgate, pup,
    )


def update_kernel(
    norm_ref, gains_sum_ref, gains_ref, gains_first_ref, gains_second_ref, *refs
):
    count = 6
    grads, weights, firsts, seconds = (refs[i * count : (i + 1) * count] for i in range(4))
    refs = refs[4 * count :]
    (layer, grad), refs = refs[:2], refs[2:]
    outs, refs = [refs[i * count : (i + 1) * count] for i in range(4)], refs[4 * count :]
    (layer_out, grad_out), refs = refs[:2], refs[2:]
    gain_outs, norm_out, refs = refs[:4], refs[4], refs[5:]
    norm_out[0, 0] = norm_ref[0, 0]
    held, refs = [refs[i * count : (i + 1) * count] for i in range(5)], refs[5 * count :]
    rows_held, in_sem, out_sem, copy_sem = refs
    wide_me = lax.axis_index("wide")
    at = tile(wide_me, 128)
    slices = (
        lambda ref: ref.at[:, at], lambda ref: ref.at[0, at, :], lambda ref: ref.at[1, at, :],
        lambda ref: ref.at[:, at], lambda ref: ref.at[at, :], lambda ref: ref.at[:, at],
    )
    halves = (None, 0, 1, None, None, None)
    loads, stores = [], []
    for i in range(count):
        def whole(ref):
            return ref if halves[i] is None else ref.at[halves[i]]

        sources = (grads[i], slices[i](weights[i]), whole(firsts[i]), whole(seconds[i]))
        loads.append(
            [pltpu.make_async_copy(src, held[n][i], in_sem.at[n, i]) for n, src in enumerate(sources)]
        )
        targets = (
            (held[0][i], outs[0][i]), (held[2][i], outs[1][i]), (held[3][i], outs[2][i]),
            (held[4][i], outs[3][i]),
        )
        stores.append(
            [
                pltpu.make_async_copy(src, whole(dst), out_sem.at[n, i])
                for n, (src, dst) in enumerate(targets)
            ]
        )
    for group in loads:
        for load in group:
            load.start()
    moved_in = [
        pltpu.make_async_copy(src, rows_held.at[n], copy_sem.at[n]) for n, src in enumerate((layer, grad))
    ]
    moved_out = [
        pltpu.make_async_copy(rows_held.at[n], dst, copy_sem.at[2 + n])
        for n, dst in enumerate((layer_out, grad_out))
    ]
    for copy in moved_in:
        copy.start()
    factor = jnp.minimum(1.0, clip_limit / (norm_ref[0:1, 0:1] + 1e-06))

    for i in range(count):
        for load in loads[i]:
            load.wait()
        height, breadth = held[0][i].shape
        span = max(8, min(height, 16384 // breadth))

        def step(j, carry):
            rows = tile(j, span)
            clipped = held[0][i][rows, :] * factor
            updated, momentum, variance = adam_update(
                held[1][i][rows, :].astype(f32), clipped, held[2][i][rows, :], held[3][i][rows, :],
                learn_rate, decay_rate,
            )
            held[0][i][rows, :] = clipped
            held[2][i][rows, :] = momentum
            held[3][i][rows, :] = variance
            held[4][i][rows, :] = updated
            return carry

        lax.fori_loop(0, height // span, step, 0)
        for store in stores[i]:
            store.start()
    for before, after in zip(moved_in, moved_out):
        before.wait()
        after.start()
    clipped = gains_sum_ref[0:2, :] * factor
    updated, momentum, variance = adam_update(
        gains_ref[:, at].astype(f32), clipped, gains_first_ref[...], gains_second_ref[...], gain_rate, 0.0
    )
    for ref, value in zip(gain_outs, (clipped, momentum, variance, updated)):
        ref[...] = value
    for group in stores:
        for store in group:
            store.wait()
    for copy in moved_out:
        copy.wait()


def update(norm, gains_sum, gains, gains_first, gains_second, grads, weights, firsts, seconds, layer, grad):
    here = pl.BlockSpec(memory_space=pltpu.VMEM)
    anywhere = pl.BlockSpec(memory_space=pl.ANY)
    shape = jax.ShapeDtypeStruct
    like = [shape(first.shape, f32) for first in firsts]
    kept = [like[0], like[1], like[3], like[4], like[5]]
    blocks = [grad_part.shape for grad_part in grads]
    small = shape(gains_first.shape, f32)
    dma = pltpu.SemaphoreType.DMA

    def body(*refs):
        head, rest = refs[:5], refs[5:]
        ins, rest = rest[:6], rest[6:]
        groups = []
        for _ in range(3):
            down, gateup, out, query, keyval = rest[:5]
            groups += [down, gateup, gateup, out, query, keyval]
            rest = rest[5:]
        moved, rest = rest[:2], rest[2:]
        outs = []
        for _ in range(4):
            down, gateup, out, query, keyval = rest[:5]
            outs += [down, gateup, gateup, out, query, keyval]
            rest = rest[5:]
        update_kernel(*head, *ins, *groups, *moved, *outs, *rest)

    def five(arrays):
        return [arrays[0], arrays[1], arrays[3], arrays[4], arrays[5]]

    return pl.pallas_call(
        body,
        out_shape=tuple(kept * 4 + [shape(layer.shape, bf16), shape(grad.shape, bf16)] + [small] * 4 + [shape((1, 1), f32)]),
        in_specs=[here] * 5 + [anywhere] * 23,
        out_specs=tuple([anywhere] * 22 + [here] * 4 + [pl.BlockSpec(memory_space=pltpu.SMEM)]),
        scratch_shapes=[
            *[pltpu.VMEM(block, f32) for block in blocks],
            *[pltpu.VMEM(block, bf16) for block in blocks],
            *[pltpu.VMEM(block, f32) for block in blocks * 3],
            pltpu.VMEM((2, *layer.shape), bf16),
            dma((4, 6)),
            dma((4, 6)),
            dma((4,)),
        ],
        compiler_params=pltpu.CompilerParams(vmem_limit_bytes=63 * MB),
        name="update",
    )(
        norm, gains_sum, gains, gains_first, gains_second, *grads, *five(weights), *five(firsts),
        *five(seconds), layer, grad,
    )


def shards(
    tokens,
    cotangent,
    lengths,
    query_weight,
    keyval_weight,
    output_weight,
    gateup_weight,
    down_weight,
    norm_gains,
    query_first,
    keyval_first,
    output_first,
    gateup_first,
    down_first,
    gains_first,
    query_second,
    keyval_second,
    output_second,
    gateup_second,
    down_second,
    gains_second,
):
    bucket_count, row_count, model_width = tokens.shape
    wide_count = lax.axis_size("wide")
    token_count = bucket_count * row_count
    tables = rotation_tables(wide_count, row_count)
    inputs = tokens.reshape(token_count, model_width)
    units = down_weight.shape[0]

    def turned(values):
        return values.transpose(0, 2, 1).reshape(2 * HD, -1)

    def turned_back(values):
        return values.reshape(2, HD, -1).transpose(0, 2, 1)

    pair_weight = turned(keyval_weight)
    (
        logs, grad_hidden, gain_two, grad_heads, output_grad, down_sum, squares, normed_one, pairs,
        query_stack, out_stack, hidden, layer_part, layer_in, gate_part, up_part,
    ) = forward(
        lengths, inputs, norm_gains, pair_weight, tables, query_weight, output_weight, gateup_weight,
        down_weight, cotangent.reshape(token_count, model_width),
    )
    query_sum, pair_sum, output_sum, gate_sum, up_sum, gains_sum, norm, layer_rows, grad_rows = backward(
        lengths, norm_gains, tables, logs, gain_two, grad_heads, squares, query_stack, out_stack,
        inputs, query_weight, pair_weight, hidden, grad_hidden, output_grad, pairs, normed_one, layer_part, layer_in,
        gate_part, up_part,
    )
    results = update(
        norm, gains_sum, norm_gains, gains_first, gains_second,
        (down_sum, gate_sum, up_sum, output_sum, query_sum, pair_sum),
        (down_weight, gateup_weight, gateup_weight, output_weight, query_weight, pair_weight),
        (down_first, gateup_first, gateup_first, output_first, query_first, turned(keyval_first)),
        (down_second, gateup_second, gateup_second, output_second, query_second, turned(keyval_second)),
        layer_rows, grad_rows,
    )
    layer_out = results[20].reshape(bucket_count, row_count, model_width)
    input_grad = results[21].reshape(bucket_count, row_count, model_width)
    kinds = []
    for kind in range(4):
        down, gateup, output, query, pair = results[5 * kind : 5 * kind + 5]
        kinds.append((query, turned_back(pair), output, gateup, down, results[22 + kind]))
    clipped, momentum, variance, updated = kinds
    return (
        layer_out, input_grad, *clipped, results[26].reshape(()), *momentum, *variance, *updated,
    )


def solution(mesh):
    return jax.shard_map(
        shards,
        mesh=mesh,
        in_specs=(
            P(None, "wide", None),
            P(None, "wide", None),
            P(),
            P(None, "narrow"),
            P(None, None, "narrow"),
            P("narrow", None),
            P(None, None, "narrow"),
            P("narrow", None),
            P(),
            P("wide", "narrow"),
            P(None, "wide", "narrow"),
            P("narrow", "wide"),
            P(None, "wide", "narrow"),
            P("narrow", "wide"),
            P(None, "wide"),
            P("wide", "narrow"),
            P(None, "wide", "narrow"),
            P("narrow", "wide"),
            P(None, "wide", "narrow"),
            P("narrow", "wide"),
            P(None, "wide"),
        ),
        out_specs=(
            P(None, "wide", None),
            P(None, "wide", None),
            P("wide", "narrow"),
            P(None, "wide", "narrow"),
            P("narrow", "wide"),
            P(None, "wide", "narrow"),
            P("narrow", "wide"),
            P(None, "wide"),
            P(),
            P("wide", "narrow"),
            P(None, "wide", "narrow"),
            P("narrow", "wide"),
            P(None, "wide", "narrow"),
            P("narrow", "wide"),
            P(None, "wide"),
            P("wide", "narrow"),
            P(None, "wide", "narrow"),
            P("narrow", "wide"),
            P(None, "wide", "narrow"),
            P("narrow", "wide"),
            P(None, "wide"),
            P("wide", "narrow"),
            P(None, "wide", "narrow"),
            P("narrow", "wide"),
            P(None, "wide", "narrow"),
            P("narrow", "wide"),
            P(None, "wide"),
        ),
        check_vma=False,
    )
```
